32 devices in a mesh: seq: 8 (over z, x), dp: 4 (over y, core).
Axes of the slice: x: 2, y: 2, z: 4, core: 2. Of those that a mesh axis runs over, the one named last changes fastest.
Arguments:
- queries: bfloat16 [4, 1024, 2048], P('dp', 'seq'), may hold values from -6 to 6
- keys: bfloat16 [4, 1024, 2048], P('dp', 'seq'), may hold values from -6 to 6
- values: bfloat16 [4, 1024, 2048], P('dp', 'seq'), may hold values from -6 to 6
- out_grad: bfloat16 [4, 1024, 2048], P('dp', 'seq'), may hold values from -6 to 6
- gain: float32 [2048], replicated, may hold values from 0.1 to 1.9
Outputs:
- normed_out: bfloat16 [4, 1024, 2048], P('dp', 'seq')
- query_grad: bfloat16 [4, 1024, 2048], P('dp', 'seq')
- key_grad: bfloat16 [4, 1024, 2048], P('dp', 'seq')
- value_grad: bfloat16 [4, 1024, 2048], P('dp', 'seq')
- gain_grad: float32 [2048], replicated
The draws below stay inside these ranges and needn't reach their ends.
All inputs are finite; a program needn't handle non-finite values.
Results may differ from the reference program's by a relative error of at most 0.0085.
Values sent between devices are 32-bit elements; how exact they have to be, the bound alone decides.
A program may use at most 192 MiB of HBM per device.

```python
import functools
import math
import jax
import jax.numpy as jnp
from jax import lax

HEADS = 16
HEAD = 128
GROUP = 128
WIDTH = 2048
SEQLEN = 1024
BATCH = 4


def steps_of(rng, dims, cuts, smallest, top_value):
    loudness = 1.0
    for position, shards_of in cuts:
        steps = jax.random.uniform(jax.random.fold_in(jax.random.fold_in(rng, 6), position), (shards_of,), jnp.float32, smallest / len(cuts), top_value / len(cuts))
        loudness = loudness * jnp.repeat(jnp.exp(steps), dims[position] // shards_of).reshape((-1,) + (1,) * (len(dims) - 1 - position))
    return loudness


def gaussian(own_key, shape, deviation, reach, split=(), held_as=jnp.bfloat16):
    values = deviation * jax.random.normal(own_key, shape, jnp.float32)
    if split:
        values = values * steps_of(own_key, shape, split, -0.22, 0.18)
    return jnp.clip(values, -reach, reach).astype(held_as)


def setup_inputs(seed: int = 0) -> dict:
    splits = jax.random.split(jax.random.key(seed), 6)
    return {
        "queries": gaussian(splits[0], (BATCH, SEQLEN, WIDTH), 1.0, 6.0, ((0, 4), (1, 8))),
        "keys": gaussian(splits[1], (BATCH, SEQLEN, WIDTH), 1.0, 6.0, ((0, 4), (1, 8))),
        "values": gaussian(splits[2], (BATCH, SEQLEN, WIDTH), 1.0, 6.0, ((0, 4), (1, 8))),
        "out_grad": gaussian(splits[3], (BATCH, SEQLEN, WIDTH), 1.0, 6.0, ((0, 4), (1, 8))),
        "gain": jnp.clip(1.0 + 0.18 * jax.random.normal(splits[4], (WIDTH,), jnp.float32), 0.1, 1.9),
    }


def to_blocks(array, batch_size, block_count):
    shaped = array.reshape(batch_size, block_count, GROUP, HEADS, HEAD)
    return shaped.transpose(1, 0, 2, 3, 4)

def from_blocks(array, batch_size, seq_total):
    return array.transpose(1, 0, 2, 3, 4).reshape(batch_size, seq_total, HEADS * HEAD)

def split_state(state):
    state_high = state.astype(jnp.bfloat16)
    state_low = (state - state_high.astype(jnp.float32)).astype(jnp.bfloat16)
    return (state_high.astype(jnp.float32), state_low.astype(jnp.float32))

def forward_block(causal, gain_rows, state, inputs):
    query_rows, key_rows, value_rows, grad_rows = inputs
    query_wide = query_rows.astype(jnp.float32)
    key_wide = key_rows.astype(jnp.float32)
    value_wide = value_rows.astype(jnp.float32)
    state_high, state_low = split_state(state)
    scores = jnp.einsum('bthe,bshe->bhts', query_wide, key_wide) * causal
    weights = scores.astype(jnp.bfloat16)
    attended = jnp.einsum('bhts,bshe->bthe', weights.astype(jnp.float32), value_wide)
    attended = attended + jnp.einsum('bthe,bhef->bthf', query_wide, state_high, precision=lax.Precision.HIGHEST)
    attended = attended + jnp.einsum('bthe,bhef->bthf', query_wide, state_low, precision=lax.Precision.HIGHEST)
    mean_square = lax.optimization_barrier(jnp.mean(attended * attended, axis=-1, keepdims=True))
    inv_rms = lax.rsqrt(mean_square + 1e-05)
    normed = attended * inv_rms
    output_rows = (normed * gain_rows).astype(jnp.bfloat16)
    grad_wide = grad_rows.astype(jnp.float32)
    grad_normed = grad_wide * gain_rows
    grad_out = inv_rms * (grad_normed - normed * lax.optimization_barrier(jnp.mean(grad_normed * normed, axis=-1, keepdims=True)))
    grad_half = grad_out.astype(jnp.bfloat16)
    gain_part = lax.optimization_barrier(jnp.sum(normed * grad_wide, axis=(0, 1)))
    grad_half_wide = grad_half.astype(jnp.float32)
    mixed = (jnp.einsum('bthe,bshe->bhts', grad_half_wide, value_wide) * causal).astype(jnp.bfloat16)
    grad_query = jnp.einsum('bhts,bshe->bthe', mixed.astype(jnp.float32), key_wide)
    grad_query = grad_query + jnp.einsum('bthf,bhef->bthe', grad_half_wide, state_high, precision=lax.Precision.HIGHEST)
    grad_query = grad_query + jnp.einsum('bthf,bhef->bthe', grad_half_wide, state_low, precision=lax.Precision.HIGHEST)
    key_value = jnp.einsum('bshe,bshf->bhef', key_wide, value_wide)
    return (state + key_value, (output_rows, grad_query.astype(jnp.bfloat16), grad_half, gain_part))

def backward_block(causal, later_sum, inputs):
    query_rows, key_rows, value_rows, grad_half = inputs
    query_wide = query_rows.astype(jnp.float32)
    key_wide = key_rows.astype(jnp.float32)
    value_wide = value_rows.astype(jnp.float32)
    grad_half_wide = grad_half.astype(jnp.float32)
    later_high, later_low = split_state(later_sum)
    weights = (jnp.einsum('bthe,bshe->bhts', query_wide, key_wide) * causal).astype(jnp.bfloat16)
    mixed = (jnp.einsum('bthe,bshe->bhts', grad_half_wide, value_wide) * causal).astype(jnp.bfloat16)
    grad_key = jnp.einsum('bhts,bthe->bshe', mixed.astype(jnp.float32), query_wide)
    grad_key = grad_key + jnp.einsum('bshf,bhef->bshe', value_wide, later_high, precision=lax.Precision.HIGHEST)
    grad_key = grad_key + jnp.einsum('bshf,bhef->bshe', value_wide, later_low, precision=lax.Precision.HIGHEST)
    grad_value = jnp.einsum('bhts,bthf->bshf', weights.astype(jnp.float32), grad_half_wide)
    grad_value = grad_value + jnp.einsum('bshe,bhef->bshf', key_wide, later_high, precision=lax.Precision.HIGHEST)
    grad_value = grad_value + jnp.einsum('bshe,bhef->bshf', key_wide, later_low, precision=lax.Precision.HIGHEST)
    outer = jnp.einsum('bthe,bthf->bhef', query_wide, grad_half_wide)
    return (later_sum + outer, (grad_key.astype(jnp.bfloat16), grad_value.astype(jnp.bfloat16)))

def reference(queries, keys, values, out_grad, gain):
    batch_size = queries.shape[0]
    seq_total = queries.shape[1]
    block_count = seq_total // GROUP
    blocked = [to_blocks(a, batch_size, block_count) for a in (queries, keys, values, out_grad)]
    row_index = lax.broadcasted_iota(jnp.int32, (GROUP, GROUP), 0)
    col_index = lax.broadcasted_iota(jnp.int32, (GROUP, GROUP), 1)
    causal = (row_index >= col_index).astype(jnp.float32)
    gain_rows = gain.astype(jnp.float32).reshape(HEADS, HEAD)
    empty_state = jnp.zeros((batch_size, HEADS, HEAD, HEAD), jnp.float32)
    forward_fn = functools.partial(forward_block, causal, gain_rows)
    unused_state, results = lax.scan(forward_fn, empty_state, tuple(blocked))
    output_blocks, query_blocks, grad_blocks, gain_parts = results
    backward_fn = functools.partial(backward_block, causal)
    unused_later, grads = lax.scan(backward_fn, empty_state, (blocked[0], blocked[1], blocked[2], grad_blocks), reverse=True)
    key_blocks, value_blocks = grads
    gain_grad = (lax.optimization_barrier(jnp.sum(gain_parts, axis=0)) / math.sqrt(batch_size * seq_total)).reshape(HEADS * HEAD)
    normed_out = from_blocks(output_blocks, batch_size, seq_total)
    query_grad = from_blocks(query_blocks, batch_size, seq_total)
    key_grad = from_blocks(key_blocks, batch_size, seq_total)
    value_grad = from_blocks(value_blocks, batch_size, seq_total)
    return (normed_out, query_grad, key_grad, value_grad, gain_grad)
```

```python
import functools
import math

import jax
import jax.numpy as jnp
from jax import lax
from jax.experimental import pallas as pl
from jax.experimental.pallas import tpu as pltpu
from jax.sharding import PartitionSpec as P

HEAD = 128
GROUP = 128
LAG_FIRST = 2
LAG_HOP = 2
MESH = pl.DeviceIdType.MESH
F32 = jnp.float32
BF16 = jnp.bfloat16


def prefix(part, axis, combine, identity, reverse):
    count = lax.axis_size(axis)
    place = lax.axis_index(axis)
    ahead = count - 1 - place if reverse else place
    gathered = lax.all_gather(part, axis)
    state = jnp.zeros_like(part) + jnp.asarray(identity, part.dtype)

    def one(lap, state):
        source = count - 1 - lap if reverse else lap
        return combine(state, lax.dynamic_index_in_dim(gathered, source, 0, False))

    return lax.fori_loop(0, ahead, one, state)


def add_states(first_part, second_part):
    return first_part + second_part


def split_state(state):
    state_high = state.astype(jnp.bfloat16)
    state_low = (state - state_high.astype(jnp.float32)).astype(jnp.bfloat16)
    return (state_high, state_low)


def per_device(queries, keys, values, out_grad, gain):
    feature_width = queries.shape[2]
    head_size = HEAD
    head_count = feature_width // head_size
    block_size = GROUP

    def to_blocks(array):
        return array.reshape(-1, block_size, head_count, head_size)

    query_rows = to_blocks(queries)
    key_rows = to_blocks(keys)
    value_rows = to_blocks(values)
    grad_rows = to_blocks(out_grad)
    row_index = lax.broadcasted_iota(jnp.int32, (block_size, block_size), 0)
    col_index = lax.broadcasted_iota(jnp.int32, (block_size, block_size), 1)
    causal = (row_index >= col_index).astype(jnp.float32)
    gain_rows = gain.reshape(head_count, head_size)
    key_value = jnp.einsum(
        "nshe,nshf->nhef", key_rows, value_rows, preferred_element_type=jnp.float32
    )
    device_sum = jnp.sum(key_value, axis=0)
    empty_state = jnp.zeros_like(device_sum)
    incoming = prefix(device_sum, "seq", add_states, empty_state, False)
    states = incoming[None] + (jnp.cumsum(key_value, axis=0) - key_value)
    states_high, states_low = split_state(states)
    scores = (
        jnp.einsum("nthe,nshe->nhts", query_rows, key_rows, preferred_element_type=jnp.float32)
        * causal
    )
    weights = scores.astype(jnp.bfloat16)
    attended = jnp.einsum(
        "nhts,nshe->nthe", weights, value_rows, preferred_element_type=jnp.float32
    )
    attended = attended + jnp.einsum(
        "nthe,nhef->nthf", query_rows, states_high, preferred_element_type=jnp.float32
    )
    attended = attended + jnp.einsum(
        "nthe,nhef->nthf", query_rows, states_low, preferred_element_type=jnp.float32
    )
    mean_square = jnp.mean(attended * attended, axis=-1, keepdims=True)
    inv_rms = lax.rsqrt(mean_square + 1e-05)
    normed = attended * inv_rms
    normed_out = (normed * gain_rows).astype(jnp.bfloat16)
    grad_wide = grad_rows.astype(jnp.float32)
    grad_normed = grad_wide * gain_rows
    grad_out = inv_rms * (
        grad_normed - normed * jnp.mean(grad_normed * normed, axis=-1, keepdims=True)
    )
    grad_half = grad_out.astype(jnp.bfloat16)
    gain_part = jnp.sum(normed * grad_wide, axis=(0, 1)).reshape(feature_width)
    total_tokens = queries.shape[0] * queries.shape[1] * lax.axis_size("seq") * lax.axis_size("dp")
    gain_grad = lax.psum(gain_part, ("seq", "dp")) / math.sqrt(total_tokens)
    mixed = (
        jnp.einsum("nthe,nshe->nhts", grad_half, value_rows, preferred_element_type=jnp.float32)
        * causal
    )
    mixed_half = mixed.astype(jnp.bfloat16)
    grad_query = jnp.einsum(
        "nhts,nshe->nthe", mixed_half, key_rows, preferred_element_type=jnp.float32
    )
    grad_query = grad_query + jnp.einsum(
        "nthf,nhef->nthe", grad_half, states_high, preferred_element_type=jnp.float32
    )
    grad_query = grad_query + jnp.einsum(
        "nthf,nhef->nthe", grad_half, states_low, preferred_element_type=jnp.float32
    )
    outer = jnp.einsum("nthe,nthf->nhef", query_rows, grad_half, preferred_element_type=jnp.float32)
    outer_sum = jnp.sum(outer, axis=0)
    arriving = prefix(outer_sum, "seq", add_states, empty_state, True)
    later_sum = arriving[None] + (outer_sum[None] - jnp.cumsum(outer, axis=0))
    later_high, later_low = split_state(later_sum)
    grad_key = jnp.einsum(
        "nhts,nthe->nshe", mixed_half, query_rows, preferred_element_type=jnp.float32
    )
    grad_key = grad_key + jnp.einsum(
        "nshf,nhef->nshe", value_rows, later_high, preferred_element_type=jnp.float32
    )
    grad_key = grad_key + jnp.einsum(
        "nshf,nhef->nshe", value_rows, later_low, preferred_element_type=jnp.float32
    )
    grad_value = jnp.einsum(
        "nhts,nthf->nshf", weights, grad_half, preferred_element_type=jnp.float32
    )
    grad_value = grad_value + jnp.einsum(
        "nshe,nhef->nshf", key_rows, later_high, preferred_element_type=jnp.float32
    )
    grad_value = grad_value + jnp.einsum(
        "nshe,nhef->nshf", key_rows, later_low, preferred_element_type=jnp.float32
    )
    shape_out = queries.shape
    return (
        normed_out.reshape(shape_out),
        grad_query.astype(jnp.bfloat16).reshape(shape_out),
        grad_key.astype(jnp.bfloat16).reshape(shape_out),
        grad_value.astype(jnp.bfloat16).reshape(shape_out),
        gain_grad,
    )


def dot(a, b, a_dim=1, b_dim=0):
    return lax.dot_general(a, b, (((a_dim,), (b_dim,)), ((), ())), preferred_element_type=F32)


def flip(index, bit):
    return index + bit * (1 - 2 * lax.rem(lax.div(index, bit), 2))


def kernel(
    pairs, hops, scale,
    q_ref, k_ref, v_ref, g_ref, gain_ref,
    out_ref, dq_ref, dk_ref, dv_ref, gg_ref,
    f_own, f_src, f_in, fz_in, fz_out, f_give, f_take,
    b_own, b_src, b_in, bz_in, bz_out, b_give, b_take,
    w_all, hi_all, lo_all, go_all, gain_sum, gain_in,
    send, recv, gain_send, gain_recv,
):
    half = f_own.shape[0]
    stages = len(hops)
    place = lax.axis_index("seq")
    side = lax.rem(place, 2)
    pair = lax.div(place, 2)
    has_before = pair > 0
    has_after = pair < pairs - 1
    partner = {"seq": flip(place, 1)}
    before = {"seq": place - 2}
    after = {"seq": place + 2}
    own_first = side * half
    other_first = (1 - side) * half

    def greet(device):
        pl.semaphore_signal(barrier, inc=1, device_id=device, device_id_type=MESH)

    def hop_device(axis, bit):
        return {axis: flip(lax.axis_index(axis), bit)}

    barrier = pltpu.get_barrier_semaphore()
    peers = [hop for hop in hops if hop != ("seq", 2)]
    for axis, bit in peers:
        greet(hop_device(axis, bit))

    @pl.when(has_before)
    def _():
        greet(before)

    @pl.when(has_after)
    def _():
        greet(after)

    def move(kind, src, dst, c, device):
        return pltpu.make_async_remote_copy(
            src_ref=src.at[c], dst_ref=dst.at[c],
            send_sem=send.at[kind, c], recv_sem=recv.at[kind, c],
            device_id=device, device_id_type=MESH,
        )

    def fx(c):
        return move(0, f_src, f_in, c, partner)

    def fz(c, device):
        return move(1, fz_out, fz_in, c, device)

    def fg(c):
        return move(2, f_give, f_take, c, partner)

    def bx(c):
        return move(3, b_src, b_in, c, partner)

    def bz(c, device):
        return move(4, bz_out, bz_in, c, device)

    def bg(c):
        return move(5, b_give, b_take, c, partner)

    def gain_move(s):
        axis, bit = hops[s]
        return pltpu.make_async_remote_copy(
            src_ref=gain_sum.at[s], dst_ref=gain_in.at[s],
            send_sem=gain_send.at[s], recv_sem=gain_recv.at[s],
            device_id=hop_device(axis, bit), device_id_type=MESH,
        )

    def cols(h):
        return pl.ds(pl.multiple_of(h * HEAD, HEAD), HEAD)

    row = lax.broadcasted_iota(jnp.int32, (GROUP, GROUP), 0)
    col = lax.broadcasted_iota(jnp.int32, (GROUP, GROUP), 1)
    causal = row >= col

    def key_value(h):
        return dot(k_ref[:, cols(h)], v_ref[:, cols(h)], 0, 0)

    def local_part(h):
        w = jnp.where(causal, dot(q_ref[:, cols(h)], k_ref[:, cols(h)], 1, 1), 0.0).astype(BF16)
        w_all[h] = w
        return dot(w, v_ref[:, cols(h)])

    def forward(h, inner, state):
        q = q_ref[:, cols(h)]
        hi, lo = split_state(state)
        hi_all[h] = hi
        lo_all[h] = lo
        attended = inner + dot(
            jnp.concatenate([q, q], axis=1), jnp.concatenate([hi, lo], axis=0)
        )
        inv = lax.rsqrt(jnp.mean(attended * attended, axis=1, keepdims=True) + 1e-05)
        normed = attended * inv
        gain = gain_ref[pl.ds(h, 1), :]
        wide = g_ref[:, cols(h)].astype(F32)
        grad_normed = wide * gain
        go = inv * (
            grad_normed - normed * jnp.mean(grad_normed * normed, axis=1, keepdims=True)
        )
        go = go.astype(BF16)
        go_all[h] = go
        out_ref[:, cols(h)] = (normed * gain).astype(BF16)
        gain_sum[0, pl.ds(h, 1), :] = jnp.sum(normed * wide, axis=0, keepdims=True)
        return dot(q, go, 0, 0)

    def backward_local(h):
        go = go_all[h]
        mixed = jnp.where(causal, dot(go, v_ref[:, cols(h)], 1, 1), 0.0).astype(BF16)
        dq = dot(mixed, k_ref[:, cols(h)]) + dot(
            jnp.concatenate([go, go], axis=1),
            jnp.concatenate([hi_all[h], lo_all[h]], axis=1), 1, 1,
        )
        dq_ref[:, cols(h)] = dq.astype(BF16)
        return dot(mixed, q_ref[:, cols(h)], 0, 0), dot(w_all[h], go, 0, 0)

    def backward_later(h, parts, later):
        hi, lo = split_state(later)
        v = v_ref[:, cols(h)]
        k = k_ref[:, cols(h)]
        dk = parts[0] + dot(
            jnp.concatenate([v, v], axis=1), jnp.concatenate([hi, lo], axis=1), 1, 1
        )
        dv = parts[1] + dot(
            jnp.concatenate([k, k], axis=1), jnp.concatenate([hi, lo], axis=0)
        )
        dk_ref[:, cols(h)] = dk.astype(BF16)
        dv_ref[:, cols(h)] = dv.astype(BF16)

    @pl.when(jnp.logical_not(has_before))
    def _():
        fz_in[...] = jnp.zeros_like(fz_in)

    @pl.when(jnp.logical_not(has_after))
    def _():
        bz_in[...] = jnp.zeros_like(bz_in)

    f_src[0] = key_value(other_first)
    ends = has_before.astype(jnp.int32) + has_after.astype(jnp.int32)
    pl.semaphore_wait(barrier, len(peers) + ends)

    fx(0).start()
    for c in range(1, half):
        f_src[c] = key_value(other_first + c)
        fx(c).start()
    for c in range(half):
        f_own[c] = key_value(own_first + c)

    lag = LAG_FIRST + LAG_HOP * (pairs - 1 - pair)
    steps = max(half + 1 + LAG_FIRST + LAG_HOP * (pairs - 1), half + stages + 1)

    def step(t, carry):
        @pl.when(t < half)
        def _():
            inner = local_part(own_first + t)
            fx(t).wait_recv()

            @pl.when(has_before)
            def _():
                fz(t, partner).wait_recv()

            past, mine, theirs = fz_in[t], f_own[t], f_in[t]
            fz_out[t] = past + (mine + theirs)

            @pl.when(has_after)
            def _():
                fz(t, after).start()

            f_give[t] = past + jnp.where(side == 0, mine, 0.0)
            fg(t).start()
            b_own[t] = forward(own_first + t, inner, past + jnp.where(side == 1, theirs, 0.0))

        @pl.when((t >= 1) & (t < half + 1))
        def _():
            c = t - 1
            inner = local_part(other_first + c)
            fg(c).wait_recv()
            b_src[c] = forward(other_first + c, inner, f_take[c])
            bx(c).start()

        j = t - lag

        @pl.when((j >= 0) & (j < half))
        def _():
            bx(j).wait_recv()

            @pl.when(has_after)
            def _():
                bz(j, partner).wait_recv()

            past, mine, theirs = bz_in[j], b_own[j], b_in[j]
            bz_out[j] = past + (mine + theirs)

            @pl.when(has_before)
            def _():
                bz(j, before).start()

            b_give[j] = past + jnp.where(side == 1, mine, 0.0)
            bg(j).start()
            parts = backward_local(own_first + j)
            backward_later(own_first + j, parts, past + jnp.where(side == 0, theirs, 0.0))

        @pl.when((j >= 1) & (j < half + 1))
        def _():
            c = j - 1
            parts = backward_local(other_first + c)
            bg(c).wait_recv()
            backward_later(other_first + c, parts, b_take[c])

        for s in range(stages + 1):

            @pl.when(t == half + s)
            def _(s=s):
                if s > 0:
                    gain_move(s - 1).wait_recv()
                    gain_sum[s] = gain_sum[s - 1] + gain_in[s - 1]
                if s < stages:
                    gain_move(s).start()
                else:
                    gg_ref[...] = gain_sum[s] / scale

        return carry

    lax.fori_loop(0, steps, step, 0)

    def finish(c, carry):
        fx(c).wait_send()
        fg(c).wait_send()
        bx(c).wait_send()
        bg(c).wait_send()

        @pl.when(has_after)
        def _():
            fz(c, after).wait_send()

        @pl.when(has_before)
        def _():
            bz(c, before).wait_send()

        return carry

    lax.fori_loop(0, half, finish, 0)
    for s in range(stages):
        gain_move(s).wait_send()


def fused(queries, keys, values, out_grad, gain):
    shape = queries.shape
    rows, width = shape[1], shape[2]
    heads = width // HEAD
    half = heads // 2
    count = lax.axis_size("seq")
    spread = lax.axis_size("dp")
    hops = []
    for axis, size in (("seq", count), ("dp", spread)):
        bit = 1
        while bit < size:
            hops.append((axis, bit))
            bit *= 2
    stages = len(hops)
    scale = math.sqrt(shape[0] * rows * count * spread)
    flat = [a.reshape(rows, width) for a in (queries, keys, values, out_grad)]
    state = pltpu.VMEM((half, HEAD, HEAD), F32)
    held = pltpu.VMEM((heads, HEAD, HEAD), BF16)
    vmem = pl.BlockSpec(memory_space=pltpu.VMEM)
    result = pl.pallas_call(
        functools.partial(kernel, count // 2, tuple(hops), scale),
        out_shape=[jax.ShapeDtypeStruct((rows, width), BF16)] * 4
        + [jax.ShapeDtypeStruct((heads, HEAD), F32)],
        in_specs=[vmem] * 5,
        out_specs=[vmem] * 5,
        scratch_shapes=[state] * 14
        + [held] * 4
        + [
            pltpu.VMEM((stages + 1, heads, HEAD), F32),
            pltpu.VMEM((stages, heads, HEAD), F32),
            pltpu.SemaphoreType.DMA((6, half)),
            pltpu.SemaphoreType.DMA((6, half)),
            pltpu.SemaphoreType.DMA((stages,)),
            pltpu.SemaphoreType.DMA((stages,)),
        ],
        compiler_params=pltpu.CompilerParams(
            collective_id=0, has_side_effects=True, vmem_limit_bytes=40 * 1024 * 1024
        ),
    )(*flat, gain.reshape(heads, HEAD))
    return tuple(a.reshape(shape) for a in result[:4]) + (result[4].reshape(width),)


def fits(queries):
    def power_of_two(size):
        return size & (size - 1) == 0

    heads = queries.shape[2] // HEAD
    return (
        queries.shape[:2] == (1, GROUP)
        and heads % 2 == 0
        and lax.axis_size("seq") >= 2
        and power_of_two(lax.axis_size("seq"))
        and power_of_two(lax.axis_size("dp"))
    )


def on_device(queries, keys, values, out_grad, gain):
    run = fused if fits(queries) else per_device
    return run(queries, keys, values, out_grad, gain)


def solution(mesh):
    in_specs = (
        P("dp", "seq", None),
        P("dp", "seq", None),
        P("dp", "seq", None),
        P("dp", "seq", None),
        P(),
    )
    out_specs = (
        P("dp", "seq", None),
        P("dp", "seq", None),
        P("dp", "seq", None),
        P("dp", "seq", None),
        P(),
    )
    return jax.shard_map(
        on_device, mesh=mesh, in_specs=in_specs, out_specs=out_specs, check_vma=False
    )
```

```python
import functools
import math

import jax
import jax.numpy as jnp
from jax import lax
from jax.experimental import pallas as pl
from jax.experimental.pallas import tpu as pltpu
from jax.sharding import PartitionSpec as P

HEAD = 128
GROUP = 128
LAG_FIRST = 2
LAG_HOP = 2
VMEM_LIMIT = 56 * 1024 * 1024
MESH = pl.DeviceIdType.MESH
F32 = jnp.float32
BF16 = jnp.bfloat16


def prefix(part, axis, combine, identity, reverse):
    count = lax.axis_size(axis)
    place = lax.axis_index(axis)
    ahead = count - 1 - place if reverse else place
    gathered = lax.all_gather(part, axis)
    state = jnp.zeros_like(part) + jnp.asarray(identity, part.dtype)

    def one(lap, state):
        source = count - 1 - lap if reverse else lap
        return combine(state, lax.dynamic_index_in_dim(gathered, source, 0, False))

    return lax.fori_loop(0, ahead, one, state)


def add_states(first_part, second_part):
    return first_part + second_part


def split_state(state):
    state_high = state.astype(jnp.bfloat16)
    state_low = (state - state_high.astype(jnp.float32)).astype(jnp.bfloat16)
    return (state_high, state_low)


def per_device(queries, keys, values, out_grad, gain):
    feature_width = queries.shape[2]
    head_size = HEAD
    head_count = feature_width // head_size
    block_size = GROUP

    def to_blocks(array):
        return array.reshape(-1, block_size, head_count, head_size)

    query_rows = to_blocks(queries)
    key_rows = to_blocks(keys)
    value_rows = to_blocks(values)
    grad_rows = to_blocks(out_grad)
    row_index = lax.broadcasted_iota(jnp.int32, (block_size, block_size), 0)
    col_index = lax.broadcasted_iota(jnp.int32, (block_size, block_size), 1)
    causal = (row_index >= col_index).astype(jnp.float32)
    gain_rows = gain.reshape(head_count, head_size)
    key_value = jnp.einsum(
        "nshe,nshf->nhef", key_rows, value_rows, preferred_element_type=jnp.float32
    )
    device_sum = jnp.sum(key_value, axis=0)
    empty_state = jnp.zeros_like(device_sum)
    incoming = prefix(device_sum, "seq", add_states, empty_state, False)
    states = incoming[None] + (jnp.cumsum(key_value, axis=0) - key_value)
    states_high, states_low = split_state(states)
    scores = (
        jnp.einsum("nthe,nshe->nhts", query_rows, key_rows, preferred_element_type=jnp.float32)
        * causal
    )
    weights = scores.astype(jnp.bfloat16)
    attended = jnp.einsum(
        "nhts,nshe->nthe", weights, value_rows, preferred_element_type=jnp.float32
    )
    attended = attended + jnp.einsum(
        "nthe,nhef->nthf", query_rows, states_high, preferred_element_type=jnp.float32
    )
    attended = attended + jnp.einsum(
        "nthe,nhef->nthf", query_rows, states_low, preferred_element_type=jnp.float32
    )
    mean_square = jnp.mean(attended * attended, axis=-1, keepdims=True)
    inv_rms = lax.rsqrt(mean_square + 1e-05)
    normed = attended * inv_rms
    normed_out = (normed * gain_rows).astype(jnp.bfloat16)
    grad_wide = grad_rows.astype(jnp.float32)
    grad_normed = grad_wide * gain_rows
    grad_out = inv_rms * (
        grad_normed - normed * jnp.mean(grad_normed * normed, axis=-1, keepdims=True)
    )
    grad_half = grad_out.astype(jnp.bfloat16)
    gain_part = jnp.sum(normed * grad_wide, axis=(0, 1)).reshape(feature_width)
    total_tokens = queries.shape[0] * queries.shape[1] * lax.axis_size("seq") * lax.axis_size("dp")
    gain_grad = lax.psum(gain_part, ("seq", "dp")) / math.sqrt(total_tokens)
    mixed = (
        jnp.einsum("nthe,nshe->nhts", grad_half, value_rows, preferred_element_type=jnp.float32)
        * causal
    )
    mixed_half = mixed.astype(jnp.bfloat16)
    grad_query = jnp.einsum(
        "nhts,nshe->nthe", mixed_half, key_rows, preferred_element_type=jnp.float32
    )
    grad_query = grad_query + jnp.einsum(
        "nthf,nhef->nthe", grad_half, states_high, preferred_element_type=jnp.float32
    )
    grad_query = grad_query + jnp.einsum(
        "nthf,nhef->nthe", grad_half, states_low, preferred_element_type=jnp.float32
    )
    outer = jnp.einsum("nthe,nthf->nhef", query_rows, grad_half, preferred_element_type=jnp.float32)
    outer_sum = jnp.sum(outer, axis=0)
    arriving = prefix(outer_sum, "seq", add_states, empty_state, True)
    later_sum = arriving[None] + (outer_sum[None] - jnp.cumsum(outer, axis=0))
    later_high, later_low = split_state(later_sum)
    grad_key = jnp.einsum(
        "nhts,nthe->nshe", mixed_half, query_rows, preferred_element_type=jnp.float32
    )
    grad_key = grad_key + jnp.einsum(
        "nshf,nhef->nshe", value_rows, later_high, preferred_element_type=jnp.float32
    )
    grad_key = grad_key + jnp.einsum(
        "nshf,nhef->nshe", value_rows, later_low, preferred_element_type=jnp.float32
    )
    grad_value = jnp.einsum(
        "nhts,nthf->nshf", weights, grad_half, preferred_element_type=jnp.float32
    )
    grad_value = grad_value + jnp.einsum(
        "nshe,nhef->nshf", key_rows, later_high, preferred_element_type=jnp.float32
    )
    grad_value = grad_value + jnp.einsum(
        "nshe,nhef->nshf", key_rows, later_low, preferred_element_type=jnp.float32
    )
    shape_out = queries.shape
    return (
        normed_out.reshape(shape_out),
        grad_query.astype(jnp.bfloat16).reshape(shape_out),
        grad_key.astype(jnp.bfloat16).reshape(shape_out),
        grad_value.astype(jnp.bfloat16).reshape(shape_out),
        gain_grad,
    )


def dot(a, b, a_dim=1, b_dim=0):
    return lax.dot_general(a, b, (((a_dim,), (b_dim,)), ((), ())), preferred_element_type=F32)


def flip(index, bit):
    return index + bit * (1 - 2 * lax.rem(lax.div(index, bit), 2))


def kernel(
    pairs, hops, scale,
    q_hbm, k_hbm, v_hbm, g_hbm, gain_hbm,
    out_hbm, dq_hbm, dk_hbm, dv_hbm, gg_hbm,
    f_own, f_src, f_in, fz_in, fz_out, f_give, f_take,
    b_own, b_src, b_in, bz_in, bz_out, b_give, b_take,
    w_all, hi_all, lo_all, go_all, inner_all, dk_all, dv_all, gain_sum, gain_in,
    q_ref, k_ref, v_ref, g_ref, gain_ref,
    out_ref, dq_ref, dk_ref, dv_ref, gg_ref,
    send, recv, gain_send, gain_recv, load_sem, store_sem,
):
    half = f_own.shape[0]
    stages = len(hops)
    place = lax.axis_index("seq")
    side = lax.rem(place, 2)
    pair = lax.div(place, 2)
    has_before = pair > 0
    has_after = pair < pairs - 1
    partner = {"seq": flip(place, 1)}
    before = {"seq": place - 2}
    after = {"seq": place + 2}
    own_first = side * half
    other_first = (1 - side) * half

    loads = [
        pltpu.make_async_copy(src, dst, load_sem.at[i])
        for i, (src, dst) in enumerate((
            (k_hbm, k_ref), (v_hbm, v_ref), (q_hbm, q_ref), (g_hbm, g_ref), (gain_hbm, gain_ref),
        ))
    ]
    for load in loads:
        load.start()

    stores = [
        pltpu.make_async_copy(src, dst, store_sem.at[i])
        for i, (src, dst) in enumerate((
            (out_ref, out_hbm), (dq_ref, dq_hbm), (dk_ref, dk_hbm), (dv_ref, dv_hbm),
            (gg_ref, gg_hbm),
        ))
    ]

    def greet(device):
        pl.semaphore_signal(barrier, inc=1, device_id=device, device_id_type=MESH)

    def hop_device(axis, bit):
        return {axis: flip(lax.axis_index(axis), bit)}

    barrier = pltpu.get_barrier_semaphore()
    peers = [hop for hop in hops if hop != ("seq", 2)]
    for axis, bit in peers:
        greet(hop_device(axis, bit))

    @pl.when(has_before)
    def _():
        greet(before)

    @pl.when(has_after)
    def _():
        greet(after)

    def move(kind, src, dst, c, device):
        return pltpu.make_async_remote_copy(
            src_ref=src.at[c], dst_ref=dst.at[c],
            send_sem=send.at[kind, c], recv_sem=recv.at[kind, c],
            device_id=device, device_id_type=MESH,
        )

    def fx(c):
        return move(0, f_src, f_in, c, partner)

    def fz(c, device):
        return move(1, fz_out, fz_in, c, device)

    def fg(c):
        return move(2, f_give, f_take, c, partner)

    def bx(c):
        return move(3, b_src, b_in, c, partner)

    def bz(c, device):
        return move(4, bz_out, bz_in, c, device)

    def bg(c):
        return move(5, b_give, b_take, c, partner)

    def gain_move(s):
        axis, bit = hops[s]
        return pltpu.make_async_remote_copy(
            src_ref=gain_sum.at[s], dst_ref=gain_in.at[s],
            send_sem=gain_send.at[s], recv_sem=gain_recv.at[s],
            device_id=hop_device(axis, bit), device_id_type=MESH,
        )

    def cols(h):
        return pl.ds(pl.multiple_of(h * HEAD, HEAD), HEAD)

    row = lax.broadcasted_iota(jnp.int32, (GROUP, GROUP), 0)
    col = lax.broadcasted_iota(jnp.int32, (GROUP, GROUP), 1)
    causal = row >= col

    def key_value(h):
        return dot(k_ref[:, cols(h)], v_ref[:, cols(h)], 0, 0)

    def local_forward(h):
        w = jnp.where(causal, dot(q_ref[:, cols(h)], k_ref[:, cols(h)], 1, 1), 0.0).astype(BF16)
        return w, dot(w, v_ref[:, cols(h)])

    def forward(h, state):
        q = q_ref[:, cols(h)]
        hi, lo = split_state(state)
        attended = inner_all[h] + dot(
            jnp.concatenate([q, q], axis=1), jnp.concatenate([hi, lo], axis=0)
        )
        inv = lax.rsqrt(jnp.mean(attended * attended, axis=1, keepdims=True) + 1e-05)
        normed = attended * inv
        gain = gain_ref[pl.ds(h, 1), :]
        wide = g_ref[:, cols(h)].astype(F32)
        grad_normed = wide * gain
        go = inv * (
            grad_normed - normed * jnp.mean(grad_normed * normed, axis=1, keepdims=True)
        )
        go = go.astype(BF16)
        normed_out = (normed * gain).astype(BF16)
        gain_part = jnp.sum(normed * wide, axis=0, keepdims=True)
        return dot(q, go, 0, 0), hi, lo, go, normed_out, gain_part

    def keep_forward(h, results):
        outer, hi, lo, go, normed_out, gain_part = results
        hi_all[h] = hi
        lo_all[h] = lo
        go_all[h] = go
        out_ref[:, cols(h)] = normed_out
        gain_sum[0, pl.ds(h, 1), :] = gain_part

    def local_backward(h):
        go = go_all[h]
        mixed = jnp.where(causal, dot(go, v_ref[:, cols(h)], 1, 1), 0.0).astype(BF16)
        dq = dot(mixed, k_ref[:, cols(h)]) + dot(
            jnp.concatenate([go, go], axis=1),
            jnp.concatenate([hi_all[h], lo_all[h]], axis=1), 1, 1,
        )
        return dq.astype(BF16), dot(mixed, q_ref[:, cols(h)], 0, 0), dot(w_all[h], go, 0, 0)

    def keep_local_backward(h, results):
        dq_ref[:, cols(h)], dk_all[h], dv_all[h] = results

    def backward(h, later):
        hi, lo = split_state(later)
        v = v_ref[:, cols(h)]
        k = k_ref[:, cols(h)]
        dk = dk_all[h] + dot(
            jnp.concatenate([v, v], axis=1), jnp.concatenate([hi, lo], axis=1), 1, 1
        )
        dv = dv_all[h] + dot(
            jnp.concatenate([k, k], axis=1), jnp.concatenate([hi, lo], axis=0)
        )
        return dk.astype(BF16), dv.astype(BF16)

    def keep_backward(h, results):
        dk_ref[:, cols(h)], dv_ref[:, cols(h)] = results

    @pl.when(jnp.logical_not(has_before))
    def _():
        fz_in[...] = jnp.zeros_like(fz_in)

    @pl.when(jnp.logical_not(has_after))
    def _():
        bz_in[...] = jnp.zeros_like(bz_in)

    loads[0].wait()
    loads[1].wait()
    f_src[0] = key_value(other_first)
    ends = has_before.astype(jnp.int32) + has_after.astype(jnp.int32)
    pl.semaphore_wait(barrier, len(peers) + ends)
    fx(0).start()
    for c in range(1, half):
        f_src[c] = key_value(other_first + c)
        fx(c).start()
    for c in range(half):
        f_own[c] = key_value(own_first + c)
    for load in loads[2:]:
        load.wait()

    lag = LAG_FIRST + LAG_HOP * (pairs - 1 - pair)
    steps = max(half + 1 + LAG_FIRST + LAG_HOP * (pairs - 1), half + stages + 1)

    def step(t, carry):
        @pl.when(t < half)
        def _():
            fx(t).wait_recv()

            @pl.when(has_before)
            def _():
                fz(t, partner).wait_recv()

            past, mine, theirs = fz_in[t], f_own[t], f_in[t]
            fz_out[t] = past + (mine + theirs)

            @pl.when(has_after)
            def _():
                fz(t, after).start()

            f_give[t] = past + jnp.where(side == 0, mine, 0.0)
            fg(t).start()
            f_own[t] = past + jnp.where(side == 1, theirs, 0.0)

        @pl.when((t >= 1) & (t < half + 1))
        def _():
            c = t - 1
            fg(c).wait_recv()
            theirs = forward(other_first + c, f_take[c])
            mine = forward(own_first + c, f_own[c])
            b_src[c] = theirs[0]
            bx(c).start()
            b_own[c] = mine[0]
            keep_forward(other_first + c, theirs)
            keep_forward(own_first + c, mine)

        j = t - lag

        @pl.when((j >= 0) & (j < half))
        def _():
            bx(j).wait_recv()

            @pl.when(has_after)
            def _():
                bz(j, partner).wait_recv()

            past, mine, theirs = bz_in[j], b_own[j], b_in[j]
            bz_out[j] = past + (mine + theirs)

            @pl.when(has_before)
            def _():
                bz(j, before).start()

            b_give[j] = past + jnp.where(side == 1, mine, 0.0)
            bg(j).start()
            b_own[j] = past + jnp.where(side == 0, theirs, 0.0)

        @pl.when(t < half)
        def _():
            mine = local_forward(own_first + t)
            theirs = local_forward(other_first + t)
            w_all[own_first + t], inner_all[own_first + t] = mine
            w_all[other_first + t], inner_all[other_first + t] = theirs

        @pl.when((t >= 2) & (t < half + 2))
        def _():
            c = t - 2
            mine = local_backward(own_first + c)
            theirs = local_backward(other_first + c)
            keep_local_backward(own_first + c, mine)
            keep_local_backward(other_first + c, theirs)

        @pl.when((j >= 1) & (j < half + 1))
        def _():
            c = j - 1
            bg(c).wait_recv()
            mine = backward(own_first + c, b_own[c])
            theirs = backward(other_first + c, b_take[c])
            keep_backward(own_first + c, mine)
            keep_backward(other_first + c, theirs)

        for s in range(stages + 1):

            @pl.when(t == half + s)
            def _(s=s):
                if s > 0:
                    gain_move(s - 1).wait_recv()
                    gain_sum[s] = gain_sum[s - 1] + gain_in[s - 1]
                if s < stages:
                    gain_move(s).start()
                else:
                    gg_ref[...] = gain_sum[s] / scale
                    stores[4].start()
                if s < 2:
                    stores[s].start()

        return carry

    lax.fori_loop(0, steps, step, 0)
    stores[2].start()
    stores[3].start()

    def finish(c, carry):
        fx(c).wait_send()
        fg(c).wait_send()
        bx(c).wait_send()
        bg(c).wait_send()

        @pl.when(has_after)
        def _():
            fz(c, after).wait_send()

        @pl.when(has_before)
        def _():
            bz(c, before).wait_send()

        return carry

    lax.fori_loop(0, half, finish, 0)
    for s in range(stages):
        gain_move(s).wait_send()
    for store in stores:
        store.wait()


def flush(*refs):
    done = refs[-1]
    copies = [
        pltpu.make_async_copy(refs[i], refs[5 + i], done.at[i]) for i in range(5)
    ]
    for copy in copies:
        copy.start()
    for copy in copies:
        copy.wait()


def fused(queries, keys, values, out_grad, gain):
    shape = queries.shape
    rows, width = shape[1], shape[2]
    heads = width // HEAD
    half = heads // 2
    count = lax.axis_size("seq")
    spread = lax.axis_size("dp")
    hops = []
    for axis, size in (("seq", count), ("dp", spread)):
        bit = 1
        while bit < size:
            hops.append((axis, bit))
            bit *= 2
    stages = len(hops)
    scale = math.sqrt(shape[0] * rows * count * spread)
    flat = [a.reshape(rows, width) for a in (queries, keys, values, out_grad)]
    state = pltpu.VMEM((half, HEAD, HEAD), F32)
    held = pltpu.VMEM((heads, HEAD, HEAD), BF16)
    wide = pltpu.VMEM((heads, HEAD, HEAD), F32)
    block = pltpu.VMEM((rows, width), BF16)
    anywhere = pl.BlockSpec(memory_space=pl.ANY)
    result = pl.pallas_call(
        functools.partial(kernel, count // 2, tuple(hops), scale),
        out_shape=[jax.ShapeDtypeStruct((rows, width), BF16)] * 4
        + [jax.ShapeDtypeStruct((heads, HEAD), F32)],
        in_specs=[anywhere] * 5,
        out_specs=[anywhere] * 5,
        scratch_shapes=[state] * 14
        + [held] * 4
        + [wide] * 3
        + [
            pltpu.VMEM((stages + 1, heads, HEAD), F32),
            pltpu.VMEM((stages, heads, HEAD), F32),
            block, block, block, block,
            pltpu.VMEM((heads, HEAD), F32),
            block, block, block, block,
            pltpu.VMEM((heads, HEAD), F32),
            pltpu.SemaphoreType.DMA((6, half)),
            pltpu.SemaphoreType.DMA((6, half)),
            pltpu.SemaphoreType.DMA((stages,)),
            pltpu.SemaphoreType.DMA((stages,)),
            pltpu.SemaphoreType.DMA((5,)),
            pltpu.SemaphoreType.DMA((5,)),
        ],
        compiler_params=pltpu.CompilerParams(
            collective_id=0, has_side_effects=True, vmem_limit_bytes=VMEM_LIMIT
        ),
    )(*flat, gain.reshape(heads, HEAD))
    result = pl.pallas_call(
        flush,
        out_shape=[jax.ShapeDtypeStruct(a.shape, a.dtype) for a in result],
        in_specs=[anywhere] * 5,
        out_specs=[anywhere] * 5,
        scratch_shapes=[pltpu.SemaphoreType.DMA((5,))],
        compiler_params=pltpu.CompilerParams(vmem_limit_bytes=VMEM_LIMIT),
    )(*result)
    return tuple(a.reshape(shape) for a in result[:4]) + (result[4].reshape(width),)


def fits(queries):
    def power_of_two(size):
        return size & (size - 1) == 0

    heads = queries.shape[2] // HEAD
    return (
        queries.shape[:2] == (1, GROUP)
        and heads % 2 == 0
        and lax.axis_size("seq") >= 2
        and power_of_two(lax.axis_size("seq"))
        and power_of_two(lax.axis_size("dp"))
    )


def on_device(queries, keys, values, out_grad, gain):
    run = fused if fits(queries) else per_device
    return run(queries, keys, values, out_grad, gain)


def solution(mesh):
    in_specs = (
        P("dp", "seq", None),
        P("dp", "seq", None),
        P("dp", "seq", None),
        P("dp", "seq", None),
        P(),
    )
    out_specs = (
        P("dp", "seq", None),
        P("dp", "seq", None),
        P("dp", "seq", None),
        P("dp", "seq", None),
        P(),
    )
    return jax.shard_map(
        on_device, mesh=mesh, in_specs=in_specs, out_specs=out_specs, check_vma=False
    )
```

```python
import functools
import math

import jax
import jax.numpy as jnp
from jax import lax
from jax.experimental import pallas as pl
from jax.experimental.pallas import tpu as pltpu
from jax.sharding import PartitionSpec as P

HEAD = 128
GROUP = 128
LAG_FIRST = 2
LAG_HOP = 2
AHEAD = 2
VMEM_LIMIT = 56 * 1024 * 1024
MESH = pl.DeviceIdType.MESH
F32 = jnp.float32
BF16 = jnp.bfloat16


def prefix(part, axis, combine, identity, reverse):
    count = lax.axis_size(axis)
    place = lax.axis_index(axis)
    ahead = count - 1 - place if reverse else place
    gathered = lax.all_gather(part, axis)
    state = jnp.zeros_like(part) + jnp.asarray(identity, part.dtype)

    def one(lap, state):
        source = count - 1 - lap if reverse else lap
        return combine(state, lax.dynamic_index_in_dim(gathered, source, 0, False))

    return lax.fori_loop(0, ahead, one, state)


def add_states(first_part, second_part):
    return first_part + second_part


def split_state(state):
    state_high = state.astype(jnp.bfloat16)
    state_low = (state - state_high.astype(jnp.float32)).astype(jnp.bfloat16)
    return (state_high, state_low)


def per_device(queries, keys, values, out_grad, gain):
    feature_width = queries.shape[2]
    head_size = HEAD
    head_count = feature_width // head_size
    block_size = GROUP

    def to_blocks(array):
        return array.reshape(-1, block_size, head_count, head_size)

    query_rows = to_blocks(queries)
    key_rows = to_blocks(keys)
    value_rows = to_blocks(values)
    grad_rows = to_blocks(out_grad)
    row_index = lax.broadcasted_iota(jnp.int32, (block_size, block_size), 0)
    col_index = lax.broadcasted_iota(jnp.int32, (block_size, block_size), 1)
    causal = (row_index >= col_index).astype(jnp.float32)
    gain_rows = gain.reshape(head_count, head_size)
    key_value = jnp.einsum(
        "nshe,nshf->nhef", key_rows, value_rows, preferred_element_type=jnp.float32
    )
    device_sum = jnp.sum(key_value, axis=0)
    empty_state = jnp.zeros_like(device_sum)
    incoming = prefix(device_sum, "seq", add_states, empty_state, False)
    states = incoming[None] + (jnp.cumsum(key_value, axis=0) - key_value)
    states_high, states_low = split_state(states)
    scores = (
        jnp.einsum("nthe,nshe->nhts", query_rows, key_rows, preferred_element_type=jnp.float32)
        * causal
    )
    weights = scores.astype(jnp.bfloat16)
    attended = jnp.einsum(
        "nhts,nshe->nthe", weights, value_rows, preferred_element_type=jnp.float32
    )
    attended = attended + jnp.einsum(
        "nthe,nhef->nthf", query_rows, states_high, preferred_element_type=jnp.float32
    )
    attended = attended + jnp.einsum(
        "nthe,nhef->nthf", query_rows, states_low, preferred_element_type=jnp.float32
    )
    mean_square = jnp.mean(attended * attended, axis=-1, keepdims=True)
    inv_rms = lax.rsqrt(mean_square + 1e-05)
    normed = attended * inv_rms
    normed_out = (normed * gain_rows).astype(jnp.bfloat16)
    grad_wide = grad_rows.astype(jnp.float32)
    grad_normed = grad_wide * gain_rows
    grad_out = inv_rms * (
        grad_normed - normed * jnp.mean(grad_normed * normed, axis=-1, keepdims=True)
    )
    grad_half = grad_out.astype(jnp.bfloat16)
    gain_part = jnp.sum(normed * grad_wide, axis=(0, 1)).reshape(feature_width)
    total_tokens = queries.shape[0] * queries.shape[1] * lax.axis_size("seq") * lax.axis_size("dp")
    gain_grad = lax.psum(gain_part, ("seq", "dp")) / math.sqrt(total_tokens)
    mixed = (
        jnp.einsum("nthe,nshe->nhts", grad_half, value_rows, preferred_element_type=jnp.float32)
        * causal
    )
    mixed_half = mixed.astype(jnp.bfloat16)
    grad_query = jnp.einsum(
        "nhts,nshe->nthe", mixed_half, key_rows, preferred_element_type=jnp.float32
    )
    grad_query = grad_query + jnp.einsum(
        "nthf,nhef->nthe", grad_half, states_high, preferred_element_type=jnp.float32
    )
    grad_query = grad_query + jnp.einsum(
        "nthf,nhef->nthe", grad_half, states_low, preferred_element_type=jnp.float32
    )
    outer = jnp.einsum("nthe,nthf->nhef", query_rows, grad_half, preferred_element_type=jnp.float32)
    outer_sum = jnp.sum(outer, axis=0)
    arriving = prefix(outer_sum, "seq", add_states, empty_state, True)
    later_sum = arriving[None] + (outer_sum[None] - jnp.cumsum(outer, axis=0))
    later_high, later_low = split_state(later_sum)
    grad_key = jnp.einsum(
        "nhts,nthe->nshe", mixed_half, query_rows, preferred_element_type=jnp.float32
    )
    grad_key = grad_key + jnp.einsum(
        "nshf,nhef->nshe", value_rows, later_high, preferred_element_type=jnp.float32
    )
    grad_key = grad_key + jnp.einsum(
        "nshf,nhef->nshe", value_rows, later_low, preferred_element_type=jnp.float32
    )
    grad_value = jnp.einsum(
        "nhts,nthf->nshf", weights, grad_half, preferred_element_type=jnp.float32
    )
    grad_value = grad_value + jnp.einsum(
        "nshe,nhef->nshf", key_rows, later_high, preferred_element_type=jnp.float32
    )
    grad_value = grad_value + jnp.einsum(
        "nshe,nhef->nshf", key_rows, later_low, preferred_element_type=jnp.float32
    )
    shape_out = queries.shape
    return (
        normed_out.reshape(shape_out),
        grad_query.astype(jnp.bfloat16).reshape(shape_out),
        grad_key.astype(jnp.bfloat16).reshape(shape_out),
        grad_value.astype(jnp.bfloat16).reshape(shape_out),
        gain_grad,
    )


def dot(a, b, a_dim=1, b_dim=0):
    return lax.dot_general(a, b, (((a_dim,), (b_dim,)), ((), ())), preferred_element_type=F32)


def flip(index, bit):
    return index + bit * (1 - 2 * lax.rem(lax.div(index, bit), 2))


def kernel(
    pairs, hops, scale,
    q_hbm, k_hbm, v_hbm, g_hbm, gain_hbm,
    out_hbm, dq_hbm, dk_hbm, dv_hbm, gg_hbm,
    f_own, f_src, f_in, fz_in, fz_out, f_give, f_take,
    b_own, b_src, b_in, bz_in, bz_out, b_give, b_take,
    w_all, hi_all, lo_all, go_all, inner_all, dk_all, dv_all, gain_sum, gain_in,
    q_ref, k_ref, v_ref, g_ref, gain_ref,
    out_ref, dq_ref, dk_ref, dv_ref, gg_ref,
    send, recv, gain_send, gain_recv, load_sem, store_sem,
):
    half = f_own.shape[0]
    stages = len(hops)
    place = lax.axis_index("seq")
    side = lax.rem(place, 2)
    pair = lax.div(place, 2)
    has_before = pair > 0
    has_after = pair < pairs - 1
    partner = {"seq": flip(place, 1)}
    before = {"seq": place - 2}
    after = {"seq": place + 2}
    def needed(sender, at_end):
        return jnp.logical_not((side == sender) & jnp.logical_not(at_end))

    fx_send, fx_wait = needed(1, has_after), needed(0, has_after)
    fg_send, fg_wait = needed(1, has_before), needed(0, has_before)
    bx_send, bx_wait = needed(0, has_before), needed(1, has_before)
    bg_send, bg_wait = needed(0, has_after), needed(1, has_after)
    own_first = side * half
    other_first = (1 - side) * half

    loads = [
        pltpu.make_async_copy(src, dst, load_sem.at[i])
        for i, (src, dst) in enumerate((
            (k_hbm, k_ref), (v_hbm, v_ref), (q_hbm, q_ref), (g_hbm, g_ref), (gain_hbm, gain_ref),
        ))
    ]
    for load in loads:
        load.start()

    stores = [
        pltpu.make_async_copy(src, dst, store_sem.at[i])
        for i, (src, dst) in enumerate((
            (out_ref, out_hbm), (dq_ref, dq_hbm), (dk_ref, dk_hbm), (dv_ref, dv_hbm),
            (gg_ref, gg_hbm),
        ))
    ]

    def greet(device):
        pl.semaphore_signal(barrier, inc=1, device_id=device, device_id_type=MESH)

    def hop_device(axis, bit):
        return {axis: flip(lax.axis_index(axis), bit)}

    barrier = pltpu.get_barrier_semaphore()
    peers = [hop for hop in hops if hop != ("seq", 2)]
    for axis, bit in peers:
        greet(hop_device(axis, bit))

    @pl.when(has_before)
    def _():
        greet(before)

    @pl.when(has_after)
    def _():
        greet(after)

    def move(kind, src, dst, c, device):
        return pltpu.make_async_remote_copy(
            src_ref=src.at[c], dst_ref=dst.at[c],
            send_sem=send.at[kind, c], recv_sem=recv.at[kind, c],
            device_id=device, device_id_type=MESH,
        )

    def fx(c):
        return move(0, f_src, f_in, c, partner)

    def fz(c, device):
        return move(1, fz_out, fz_in, c, device)

    def fg(c):
        return move(2, f_give, f_take, c, partner)

    def bx(c):
        return move(3, b_src, b_in, c, partner)

    def bz(c, device):
        return move(4, bz_out, bz_in, c, device)

    def bg(c):
        return move(5, b_give, b_take, c, partner)

    def gain_move(s):
        axis, bit = hops[s]
        return pltpu.make_async_remote_copy(
            src_ref=gain_sum.at[s], dst_ref=gain_in.at[s],
            send_sem=gain_send.at[s], recv_sem=gain_recv.at[s],
            device_id=hop_device(axis, bit), device_id_type=MESH,
        )

    def cols(h):
        return pl.ds(pl.multiple_of(h * HEAD, HEAD), HEAD)

    row = lax.broadcasted_iota(jnp.int32, (GROUP, GROUP), 0)
    col = lax.broadcasted_iota(jnp.int32, (GROUP, GROUP), 1)
    causal = row >= col

    def key_value(h):
        return dot(k_ref[:, cols(h)], v_ref[:, cols(h)], 0, 0)

    def local_forward(h):
        w = jnp.where(causal, dot(q_ref[:, cols(h)], k_ref[:, cols(h)], 1, 1), 0.0).astype(BF16)
        return w, dot(w, v_ref[:, cols(h)])

    def forward(h, state):
        q = q_ref[:, cols(h)]
        hi, lo = split_state(state)
        attended = inner_all[h] + dot(
            jnp.concatenate([q, q], axis=1), jnp.concatenate([hi, lo], axis=0)
        )
        inv = lax.rsqrt(jnp.mean(attended * attended, axis=1, keepdims=True) + 1e-05)
        normed = attended * inv
        gain = gain_ref[pl.ds(h, 1), :]
        wide = g_ref[:, cols(h)].astype(F32)
        grad_normed = wide * gain
        go = inv * (
            grad_normed - normed * jnp.mean(grad_normed * normed, axis=1, keepdims=True)
        )
        go = go.astype(BF16)
        normed_out = (normed * gain).astype(BF16)
        gain_part = jnp.sum(normed * wide, axis=0, keepdims=True)
        return dot(q, go, 0, 0), hi, lo, go, normed_out, gain_part

    def keep_forward(h, results):
        outer, hi, lo, go, normed_out, gain_part = results
        hi_all[h] = hi
        lo_all[h] = lo
        go_all[h] = go
        out_ref[:, cols(h)] = normed_out
        gain_sum[0, pl.ds(h, 1), :] = gain_part

    def local_backward(h):
        go = go_all[h]
        mixed = jnp.where(causal, dot(go, v_ref[:, cols(h)], 1, 1), 0.0).astype(BF16)
        dq = dot(mixed, k_ref[:, cols(h)]) + dot(
            jnp.concatenate([go, go], axis=1),
            jnp.concatenate([hi_all[h], lo_all[h]], axis=1), 1, 1,
        )
        return dq.astype(BF16), dot(mixed, q_ref[:, cols(h)], 0, 0), dot(w_all[h], go, 0, 0)

    def keep_local_backward(h, results):
        dq_ref[:, cols(h)], dk_all[h], dv_all[h] = results

    def backward(h, later):
        hi, lo = split_state(later)
        v = v_ref[:, cols(h)]
        k = k_ref[:, cols(h)]
        dk = dk_all[h] + dot(
            jnp.concatenate([v, v], axis=1), jnp.concatenate([hi, lo], axis=1), 1, 1
        )
        dv = dv_all[h] + dot(
            jnp.concatenate([k, k], axis=1), jnp.concatenate([hi, lo], axis=0)
        )
        return dk.astype(BF16), dv.astype(BF16)

    def keep_backward(h, results):
        dk_ref[:, cols(h)], dv_ref[:, cols(h)] = results

    def clear(ref, condition):
        @pl.when(condition)
        def _():
            ref[...] = jnp.zeros_like(ref)

    clear(fz_in, jnp.logical_not(has_before))
    clear(bz_in, jnp.logical_not(has_after))
    clear(f_take, jnp.logical_not(fg_wait))
    clear(b_take, jnp.logical_not(bg_wait))

    loads[0].wait()
    loads[1].wait()
    f_src[0] = key_value(other_first)
    ends = has_before.astype(jnp.int32) + has_after.astype(jnp.int32)
    pl.semaphore_wait(barrier, len(peers) + ends)

    def start_if(condition, copy):
        @pl.when(condition)
        def _():
            copy.start()

    def recv_if(condition, copy):
        @pl.when(condition)
        def _():
            copy.wait_recv()

    def sent_if(condition, copy):
        @pl.when(condition)
        def _():
            copy.wait_send()

    start_if(fx_send, fx(0))
    for c in range(1, half):
        f_src[c] = key_value(other_first + c)
        if c < AHEAD:
            start_if(fx_send, fx(c))
    for c in range(half):
        f_own[c] = key_value(own_first + c)
    for load in loads[2:]:
        load.wait()

    lag = LAG_FIRST + LAG_HOP * (pairs - 1 - pair)
    steps = max(half + 1 + LAG_FIRST + LAG_HOP * (pairs - 1), half + stages + 1)

    def step(t, carry):
        @pl.when(t < half)
        def _():
            recv_if(fx_wait, fx(t))
            recv_if(has_before, fz(t, partner))

            past, mine, theirs = fz_in[t], f_own[t], f_in[t]
            fz_out[t] = past + (mine + theirs)
            start_if(has_after, fz(t, after))
            f_give[t] = past + jnp.where(side == 0, mine, 0.0)
            start_if(fg_send, fg(t))
            start_if(fx_send & (t < half - AHEAD), fx(jnp.minimum(t + AHEAD, half - 1)))
            f_own[t] = past + jnp.where(side == 1, theirs, 0.0)

        @pl.when((t >= 1) & (t < half + 1))
        def _():
            c = t - 1
            recv_if(fg_wait, fg(c))
            theirs = forward(other_first + c, f_take[c])
            mine = forward(own_first + c, f_own[c])
            b_src[c] = theirs[0]
            start_if(bx_send, bx(c))
            b_own[c] = mine[0]
            keep_forward(other_first + c, theirs)
            keep_forward(own_first + c, mine)

        j = t - lag

        @pl.when((j >= 0) & (j < half))
        def _():
            recv_if(bx_wait, bx(j))
            recv_if(has_after, bz(j, partner))

            past, mine, theirs = bz_in[j], b_own[j], b_in[j]
            bz_out[j] = past + (mine + theirs)
            start_if(has_before, bz(j, before))
            b_give[j] = past + jnp.where(side == 1, mine, 0.0)
            start_if(bg_send, bg(j))
            b_own[j] = past + jnp.where(side == 0, theirs, 0.0)

        @pl.when(t < half)
        def _():
            mine = local_forward(own_first + t)
            theirs = local_forward(other_first + t)
            w_all[own_first + t], inner_all[own_first + t] = mine
            w_all[other_first + t], inner_all[other_first + t] = theirs

        @pl.when((t >= 2) & (t < half + 2))
        def _():
            c = t - 2
            mine = local_backward(own_first + c)
            theirs = local_backward(other_first + c)
            keep_local_backward(own_first + c, mine)
            keep_local_backward(other_first + c, theirs)

        @pl.when((j >= 1) & (j < half + 1))
        def _():
            c = j - 1
            recv_if(bg_wait, bg(c))
            mine = backward(own_first + c, b_own[c])
            theirs = backward(other_first + c, b_take[c])
            keep_backward(own_first + c, mine)
            keep_backward(other_first + c, theirs)

        for s in range(stages + 1):

            @pl.when(t == half + s)
            def _(s=s):
                if s > 0:
                    gain_move(s - 1).wait_recv()
                    gain_sum[s] = gain_sum[s - 1] + gain_in[s - 1]
                if s < stages:
                    gain_move(s).start()
                else:
                    gg_ref[...] = gain_sum[s] / scale
                    stores[4].start()
                if s < 2:
                    stores[s].start()

        return carry

    lax.fori_loop(0, steps, step, 0)
    stores[2].start()
    stores[3].start()

    def finish(c, carry):
        sent_if(fx_send, fx(c))
        sent_if(fg_send, fg(c))
        sent_if(bx_send, bx(c))
        sent_if(bg_send, bg(c))
        sent_if(has_after, fz(c, after))
        sent_if(has_before, bz(c, before))
        return carry

    lax.fori_loop(0, half, finish, 0)
    for s in range(stages):
        gain_move(s).wait_send()
    for store in stores:
        store.wait()


def flush(*refs):
    source, target, held = refs[:5], refs[5:10], refs[10:15]
    sems = refs[15]
    reads = [pltpu.make_async_copy(source[i], held[i], sems.at[0, i]) for i in range(5)]
    writes = [pltpu.make_async_copy(held[i], target[i], sems.at[1, i]) for i in range(5)]
    for read in reads:
        read.start()
    for read, write in zip(reads, writes):
        read.wait()
        write.start()
    for write in writes:
        write.wait()


def fused(queries, keys, values, out_grad, gain):
    shape = queries.shape
    rows, width = shape[1], shape[2]
    heads = width // HEAD
    half = heads // 2
    count = lax.axis_size("seq")
    spread = lax.axis_size("dp")
    hops = []
    for axis, size in (("seq", count), ("dp", spread)):
        bit = 1
        while bit < size:
            hops.append((axis, bit))
            bit *= 2
    stages = len(hops)
    scale = math.sqrt(shape[0] * rows * count * spread)
    flat = [a.reshape(rows, width) for a in (queries, keys, values, out_grad)]
    state = pltpu.VMEM((half, HEAD, HEAD), F32)
    held = pltpu.VMEM((heads, HEAD, HEAD), BF16)
    wide = pltpu.VMEM((heads, HEAD, HEAD), F32)
    block = pltpu.VMEM((rows, width), BF16)
    anywhere = pl.BlockSpec(memory_space=pl.ANY)
    result = pl.pallas_call(
        functools.partial(kernel, count // 2, tuple(hops), scale),
        out_shape=[jax.ShapeDtypeStruct((rows, width), BF16)] * 4
        + [jax.ShapeDtypeStruct((heads, HEAD), F32)],
        in_specs=[anywhere] * 5,
        out_specs=[anywhere] * 5,
        scratch_shapes=[state] * 14
        + [held] * 4
        + [wide] * 3
        + [
            pltpu.VMEM((stages + 1, heads, HEAD), F32),
            pltpu.VMEM((stages, heads, HEAD), F32),
            block, block, block, block,
            pltpu.VMEM((heads, HEAD), F32),
            block, block, block, block,
            pltpu.VMEM((heads, HEAD), F32),
            pltpu.SemaphoreType.DMA((6, half)),
            pltpu.SemaphoreType.DMA((6, half)),
            pltpu.SemaphoreType.DMA((stages,)),
            pltpu.SemaphoreType.DMA((stages,)),
            pltpu.SemaphoreType.DMA((5,)),
            pltpu.SemaphoreType.DMA((5,)),
        ],
        compiler_params=pltpu.CompilerParams(
            collective_id=0, has_side_effects=True, vmem_limit_bytes=VMEM_LIMIT
        ),
    )(*flat, gain.reshape(heads, HEAD))
    result = pl.pallas_call(
        flush,
        out_shape=[jax.ShapeDtypeStruct(a.shape, a.dtype) for a in result],
        in_specs=[anywhere] * 5,
        out_specs=[anywhere] * 5,
        scratch_shapes=[pltpu.VMEM(a.shape, a.dtype) for a in result]
        + [pltpu.SemaphoreType.DMA((2, 5))],
        compiler_params=pltpu.CompilerParams(vmem_limit_bytes=VMEM_LIMIT),
    )(*result)
    return tuple(a.reshape(shape) for a in result[:4]) + (result[4].reshape(width),)


def fits(queries):
    def power_of_two(size):
        return size & (size - 1) == 0

    heads = queries.shape[2] // HEAD
    return (
        queries.shape[:2] == (1, GROUP)
        and heads % 2 == 0
        and lax.axis_size("seq") >= 2
        and power_of_two(lax.axis_size("seq"))
        and power_of_two(lax.axis_size("dp"))
    )


def on_device(queries, keys, values, out_grad, gain):
    run = fused if fits(queries) else per_device
    return run(queries, keys, values, out_grad, gain)


def solution(mesh):
    in_specs = (
        P("dp", "seq", None),
        P("dp", "seq", None),
        P("dp", "seq", None),
        P("dp", "seq", None),
        P(),
    )
    out_specs = (
        P("dp", "seq", None),
        P("dp", "seq", None),
        P("dp", "seq", None),
        P("dp", "seq", None),
        P(),
    )
    return jax.shard_map(
        on_device, mesh=mesh, in_specs=in_specs, out_specs=out_specs, check_vma=False
    )
```

```python
import functools
import math

import jax
import jax.numpy as jnp
from jax import lax
from jax.experimental import pallas as pl
from jax.experimental.pallas import tpu as pltpu
from jax.sharding import PartitionSpec as P

HEAD = 128
GROUP = 128
LAG_FIRST = 2
LAG_HOP = 2
AHEAD = 2
VMEM_LIMIT = 56 * 1024 * 1024
MESH = pl.DeviceIdType.MESH
F32 = jnp.float32
BF16 = jnp.bfloat16


def prefix(part, axis, combine, identity, reverse):
    count = lax.axis_size(axis)
    place = lax.axis_index(axis)
    ahead = count - 1 - place if reverse else place
    gathered = lax.all_gather(part, axis)
    state = jnp.zeros_like(part) + jnp.asarray(identity, part.dtype)

    def one(lap, state):
        source = count - 1 - lap if reverse else lap
        return combine(state, lax.dynamic_index_in_dim(gathered, source, 0, False))

    return lax.fori_loop(0, ahead, one, state)


def add_states(first_part, second_part):
    return first_part + second_part


def split_state(state):
    state_high = state.astype(jnp.bfloat16)
    state_low = (state - state_high.astype(jnp.float32)).astype(jnp.bfloat16)
    return (state_high, state_low)


def per_device(queries, keys, values, out_grad, gain):
    feature_width = queries.shape[2]
    head_size = HEAD
    head_count = feature_width // head_size
    block_size = GROUP

    def to_blocks(array):
        return array.reshape(-1, block_size, head_count, head_size)

    query_rows = to_blocks(queries)
    key_rows = to_blocks(keys)
    value_rows = to_blocks(values)
    grad_rows = to_blocks(out_grad)
    row_index = lax.broadcasted_iota(jnp.int32, (block_size, block_size), 0)
    col_index = lax.broadcasted_iota(jnp.int32, (block_size, block_size), 1)
    causal = (row_index >= col_index).astype(jnp.float32)
    gain_rows = gain.reshape(head_count, head_size)
    key_value = jnp.einsum(
        "nshe,nshf->nhef", key_rows, value_rows, preferred_element_type=jnp.float32
    )
    device_sum = jnp.sum(key_value, axis=0)
    empty_state = jnp.zeros_like(device_sum)
    incoming = prefix(device_sum, "seq", add_states, empty_state, False)
    states = incoming[None] + (jnp.cumsum(key_value, axis=0) - key_value)
    states_high, states_low = split_state(states)
    scores = (
        jnp.einsum("nthe,nshe->nhts", query_rows, key_rows, preferred_element_type=jnp.float32)
        * causal
    )
    weights = scores.astype(jnp.bfloat16)
    attended = jnp.einsum(
        "nhts,nshe->nthe", weights, value_rows, preferred_element_type=jnp.float32
    )
    attended = attended + jnp.einsum(
        "nthe,nhef->nthf", query_rows, states_high, preferred_element_type=jnp.float32
    )
    attended = attended + jnp.einsum(
        "nthe,nhef->nthf", query_rows, states_low, preferred_element_type=jnp.float32
    )
    mean_square = jnp.mean(attended * attended, axis=-1, keepdims=True)
    inv_rms = lax.rsqrt(mean_square + 1e-05)
    normed = attended * inv_rms
    normed_out = (normed * gain_rows).astype(jnp.bfloat16)
    grad_wide = grad_rows.astype(jnp.float32)
    grad_normed = grad_wide * gain_rows
    grad_out = inv_rms * (
        grad_normed - normed * jnp.mean(grad_normed * normed, axis=-1, keepdims=True)
    )
    grad_half = grad_out.astype(jnp.bfloat16)
    gain_part = jnp.sum(normed * grad_wide, axis=(0, 1)).reshape(feature_width)
    total_tokens = queries.shape[0] * queries.shape[1] * lax.axis_size("seq") * lax.axis_size("dp")
    gain_grad = lax.psum(gain_part, ("seq", "dp")) / math.sqrt(total_tokens)
    mixed = (
        jnp.einsum("nthe,nshe->nhts", grad_half, value_rows, preferred_element_type=jnp.float32)
        * causal
    )
    mixed_half = mixed.astype(jnp.bfloat16)
    grad_query = jnp.einsum(
        "nhts,nshe->nthe", mixed_half, key_rows, preferred_element_type=jnp.float32
    )
    grad_query = grad_query + jnp.einsum(
        "nthf,nhef->nthe", grad_half, states_high, preferred_element_type=jnp.float32
    )
    grad_query = grad_query + jnp.einsum(
        "nthf,nhef->nthe", grad_half, states_low, preferred_element_type=jnp.float32
    )
    outer = jnp.einsum("nthe,nthf->nhef", query_rows, grad_half, preferred_element_type=jnp.float32)
    outer_sum = jnp.sum(outer, axis=0)
    arriving = prefix(outer_sum, "seq", add_states, empty_state, True)
    later_sum = arriving[None] + (outer_sum[None] - jnp.cumsum(outer, axis=0))
    later_high, later_low = split_state(later_sum)
    grad_key = jnp.einsum(
        "nhts,nthe->nshe", mixed_half, query_rows, preferred_element_type=jnp.float32
    )
    grad_key = grad_key + jnp.einsum(
        "nshf,nhef->nshe", value_rows, later_high, preferred_element_type=jnp.float32
    )
    grad_key = grad_key + jnp.einsum(
        "nshf,nhef->nshe", value_rows, later_low, preferred_element_type=jnp.float32
    )
    grad_value = jnp.einsum(
        "nhts,nthf->nshf", weights, grad_half, preferred_element_type=jnp.float32
    )
    grad_value = grad_value + jnp.einsum(
        "nshe,nhef->nshf", key_rows, later_high, preferred_element_type=jnp.float32
    )
    grad_value = grad_value + jnp.einsum(
        "nshe,nhef->nshf", key_rows, later_low, preferred_element_type=jnp.float32
    )
    shape_out = queries.shape
    return (
        normed_out.reshape(shape_out),
        grad_query.astype(jnp.bfloat16).reshape(shape_out),
        grad_key.astype(jnp.bfloat16).reshape(shape_out),
        grad_value.astype(jnp.bfloat16).reshape(shape_out),
        gain_grad,
    )


def dot(a, b, a_dim=1, b_dim=0):
    return lax.dot_general(a, b, (((a_dim,), (b_dim,)), ((), ())), preferred_element_type=F32)


def flip(index, bit):
    return index + bit * (1 - 2 * lax.rem(lax.div(index, bit), 2))


def kernel(
    pairs, hops, scale,
    q_hbm, k_hbm, v_hbm, g_hbm, gain_hbm,
    out_hbm, dq_hbm, dk_hbm, dv_hbm, gg_hbm,
    f_own, f_src, f_in, fz_in, fz_out, f_give, f_take,
    b_own, b_src, b_in, bz_in, bz_out, b_give, b_take,
    w_all, hi_all, lo_all, go_all, inner_all, dk_all, dv_all, gain_sum, gain_in,
    q_ref, k_ref, v_ref, g_ref, gain_ref,
    out_ref, dq_ref, dk_ref, dv_ref, gg_ref,
    send, recv, gain_send, gain_recv, load_sem, store_sem,
):
    half = f_own.shape[0]
    stages = len(hops)
    place = lax.axis_index("seq")
    side = lax.rem(place, 2)
    pair = lax.div(place, 2)
    has_before = pair > 0
    has_after = pair < pairs - 1
    partner = {"seq": flip(place, 1)}
    before = {"seq": place - 2}
    after = {"seq": place + 2}
    def needed(sender, at_end):
        return jnp.logical_not((side == sender) & jnp.logical_not(at_end))

    fx_send, fx_wait = needed(1, has_after), needed(0, has_after)
    fg_send, fg_wait = needed(1, has_before), needed(0, has_before)
    bx_send, bx_wait = needed(0, has_before), needed(1, has_before)
    bg_send, bg_wait = needed(0, has_after), needed(1, has_after)
    own_first = side * half
    other_first = (1 - side) * half

    loads = [
        pltpu.make_async_copy(src, dst, load_sem.at[i])
        for i, (src, dst) in enumerate((
            (k_hbm, k_ref), (v_hbm, v_ref), (q_hbm, q_ref), (g_hbm, g_ref), (gain_hbm, gain_ref),
        ))
    ]
    for load in loads:
        load.start()

    stores = [
        pltpu.make_async_copy(src, dst, store_sem.at[i])
        for i, (src, dst) in enumerate((
            (out_ref, out_hbm), (dq_ref, dq_hbm), (dk_ref, dk_hbm), (dv_ref, dv_hbm),
            (gg_ref, gg_hbm),
        ))
    ]

    def greet(device):
        pl.semaphore_signal(barrier, inc=1, device_id=device, device_id_type=MESH)

    def hop_device(axis, bit):
        return {axis: flip(lax.axis_index(axis), bit)}

    barrier = pltpu.get_barrier_semaphore()
    peers = [hop for hop in hops if hop != ("seq", 2)]
    for axis, bit in peers:
        greet(hop_device(axis, bit))

    @pl.when(has_before)
    def _():
        greet(before)

    @pl.when(has_after)
    def _():
        greet(after)

    def move(kind, src, dst, c, device):
        return pltpu.make_async_remote_copy(
            src_ref=src.at[c], dst_ref=dst.at[c],
            send_sem=send.at[kind, c], recv_sem=recv.at[kind, c],
            device_id=device, device_id_type=MESH,
        )

    def fx(c):
        return move(0, f_src, f_in, c, partner)

    def fz(c, device):
        return move(1, fz_out, fz_in, c, device)

    def fg(c):
        return move(2, f_give, f_take, c, partner)

    def bx(c):
        return move(3, b_src, b_in, c, partner)

    def bz(c, device):
        return move(4, bz_out, bz_in, c, device)

    def bg(c):
        return move(5, b_give, b_take, c, partner)

    def gain_move(s):
        axis, bit = hops[s]
        return pltpu.make_async_remote_copy(
            src_ref=gain_sum.at[s], dst_ref=gain_in.at[s],
            send_sem=gain_send.at[s], recv_sem=gain_recv.at[s],
            device_id=hop_device(axis, bit), device_id_type=MESH,
        )

    def cols(h):
        return pl.ds(pl.multiple_of(h * HEAD, HEAD), HEAD)

    row = lax.broadcasted_iota(jnp.int32, (GROUP, GROUP), 0)
    col = lax.broadcasted_iota(jnp.int32, (GROUP, GROUP), 1)
    causal = row >= col

    def key_value(h):
        return dot(k_ref[:, cols(h)], v_ref[:, cols(h)], 0, 0)

    def local_forward(h):
        w = jnp.where(causal, dot(q_ref[:, cols(h)], k_ref[:, cols(h)], 1, 1), 0.0).astype(BF16)
        return w, dot(w, v_ref[:, cols(h)])

    def forward(h, state):
        q = q_ref[:, cols(h)]
        hi, lo = split_state(state)
        attended = inner_all[h] + dot(
            jnp.concatenate([q, q], axis=1), jnp.concatenate([hi, lo], axis=0)
        )
        inv = lax.rsqrt(jnp.mean(attended * attended, axis=1, keepdims=True) + 1e-05)
        normed = attended * inv
        gain = gain_ref[pl.ds(h, 1), :]
        wide = g_ref[:, cols(h)].astype(F32)
        grad_normed = wide * gain
        go = inv * (
            grad_normed - normed * jnp.mean(grad_normed * normed, axis=1, keepdims=True)
        )
        go = go.astype(BF16)
        normed_out = (normed * gain).astype(BF16)
        gain_part = jnp.sum(normed * wide, axis=0, keepdims=True)
        return dot(q, go, 0, 0), hi, lo, go, normed_out, gain_part

    def keep_forward(h, results):
        outer, hi, lo, go, normed_out, gain_part = results
        hi_all[h] = hi
        lo_all[h] = lo
        go_all[h] = go
        out_ref[:, cols(h)] = normed_out
        gain_sum[0, pl.ds(h, 1), :] = gain_part

    def local_backward(h):
        go = go_all[h]
        mixed = jnp.where(causal, dot(go, v_ref[:, cols(h)], 1, 1), 0.0).astype(BF16)
        dq = dot(mixed, k_ref[:, cols(h)]) + dot(
            jnp.concatenate([go, go], axis=1),
            jnp.concatenate([hi_all[h], lo_all[h]], axis=1), 1, 1,
        )
        return dq.astype(BF16), dot(mixed, q_ref[:, cols(h)], 0, 0), dot(w_all[h], go, 0, 0)

    def keep_local_backward(h, results):
        dq_ref[:, cols(h)], dk_all[h], dv_all[h] = results

    def backward(h, later):
        hi, lo = split_state(later)
        v = v_ref[:, cols(h)]
        k = k_ref[:, cols(h)]
        dk = dk_all[h] + dot(
            jnp.concatenate([v, v], axis=1), jnp.concatenate([hi, lo], axis=1), 1, 1
        )
        dv = dv_all[h] + dot(
            jnp.concatenate([k, k], axis=1), jnp.concatenate([hi, lo], axis=0)
        )
        return dk.astype(BF16), dv.astype(BF16)

    def keep_backward(h, results):
        dk_ref[:, cols(h)], dv_ref[:, cols(h)] = results

    def clear(ref, condition):
        @pl.when(condition)
        def _():
            ref[...] = jnp.zeros_like(ref)

    clear(fz_in, jnp.logical_not(has_before))
    clear(bz_in, jnp.logical_not(has_after))
    clear(f_take, jnp.logical_not(fg_wait))
    clear(b_take, jnp.logical_not(bg_wait))

    loads[0].wait()
    loads[1].wait()
    f_src[0] = key_value(other_first)
    ends = has_before.astype(jnp.int32) + has_after.astype(jnp.int32)
    pl.semaphore_wait(barrier, len(peers) + ends)

    def start_if(condition, copy):
        @pl.when(condition)
        def _():
            copy.start()

    def recv_if(condition, copy):
        @pl.when(condition)
        def _():
            copy.wait_recv()

    def sent_if(condition, copy):
        @pl.when(condition)
        def _():
            copy.wait_send()

    start_if(fx_send, fx(0))
    for c in range(1, half):
        f_src[c] = key_value(other_first + c)
        if c < AHEAD:
            start_if(fx_send, fx(c))
    for c in range(half):
        f_own[c] = key_value(own_first + c)
    for load in loads[2:]:
        load.wait()

    lag = LAG_FIRST + LAG_HOP * (pairs - 1 - pair)
    late = 2 * pair >= pairs
    local_lag = jnp.where(late, half + 1, 2)
    final_lag = jnp.maximum(lag + 1, half + 2)
    most = max(LAG_FIRST + LAG_HOP * (pairs - 1) + 1, half + 2)
    steps = half + max(most, stages + 1)

    def local_step(c):
        mine = local_forward(own_first + c)
        theirs = local_forward(other_first + c)
        w_all[own_first + c], inner_all[own_first + c] = mine
        w_all[other_first + c], inner_all[other_first + c] = theirs

    @pl.when(late)
    def _():
        lax.fori_loop(0, half, lambda c, carry: (local_step(c), carry)[1], 0)

    def step(t, carry):
        @pl.when(t < half)
        def _():
            recv_if(fx_wait, fx(t))
            recv_if(has_before, fz(t, partner))

            past, mine, theirs = fz_in[t], f_own[t], f_in[t]
            fz_out[t] = past + (mine + theirs)
            start_if(has_after, fz(t, after))
            f_give[t] = past + jnp.where(side == 0, mine, 0.0)
            start_if(fg_send, fg(t))
            start_if(fx_send & (t < half - AHEAD), fx(jnp.minimum(t + AHEAD, half - 1)))
            f_own[t] = past + jnp.where(side == 1, theirs, 0.0)

        @pl.when((t >= 1) & (t < half + 1))
        def _():
            c = t - 1
            recv_if(fg_wait, fg(c))
            theirs = forward(other_first + c, f_take[c])
            mine = forward(own_first + c, f_own[c])
            b_src[c] = theirs[0]
            start_if(bx_send, bx(c))
            b_own[c] = mine[0]
            keep_forward(other_first + c, theirs)
            keep_forward(own_first + c, mine)

        j = t - lag

        @pl.when((j >= 0) & (j < half))
        def _():
            recv_if(bx_wait, bx(j))
            recv_if(has_after, bz(j, partner))

            past, mine, theirs = bz_in[j], b_own[j], b_in[j]
            bz_out[j] = past + (mine + theirs)
            start_if(has_before, bz(j, before))
            b_give[j] = past + jnp.where(side == 1, mine, 0.0)
            start_if(bg_send, bg(j))
            b_own[j] = past + jnp.where(side == 0, theirs, 0.0)

        @pl.when((t < half) & jnp.logical_not(late))
        def _():
            local_step(t)

        b = t - local_lag

        @pl.when((b >= 0) & (b < half))
        def _():
            mine = local_backward(own_first + b)
            theirs = local_backward(other_first + b)
            keep_local_backward(own_first + b, mine)
            keep_local_backward(other_first + b, theirs)

        e = t - final_lag

        @pl.when((e >= 0) & (e < half))
        def _():
            recv_if(bg_wait, bg(e))
            mine = backward(own_first + e, b_own[e])
            theirs = backward(other_first + e, b_take[e])
            keep_backward(own_first + e, mine)
            keep_backward(other_first + e, theirs)

        for s in range(stages + 1):

            @pl.when(t == half + s)
            def _(s=s):
                if s > 0:
                    gain_move(s - 1).wait_recv()
                    gain_sum[s] = gain_sum[s - 1] + gain_in[s - 1]
                if s < stages:
                    gain_move(s).start()
                else:
                    gg_ref[...] = gain_sum[s] / scale
                    stores[4].start()
                if s == 0:
                    stores[0].start()

        return carry

    lax.fori_loop(0, steps, step, 0)
    for store in stores[1:4]:
        store.start()

    def finish(c, carry):
        sent_if(fx_send, fx(c))
        sent_if(fg_send, fg(c))
        sent_if(bx_send, bx(c))
        sent_if(bg_send, bg(c))
        sent_if(has_after, fz(c, after))
        sent_if(has_before, bz(c, before))
        return carry

    lax.fori_loop(0, half, finish, 0)
    for s in range(stages):
        gain_move(s).wait_send()
    for store in stores:
        store.wait()


def flush(*refs):
    source, target, held = refs[:5], refs[5:10], refs[10:15]
    sems = refs[15]
    reads = [pltpu.make_async_copy(source[i], held[i], sems.at[0, i]) for i in range(5)]
    writes = [pltpu.make_async_copy(held[i], target[i], sems.at[1, i]) for i in range(5)]
    for read in reads:
        read.start()
    for read, write in zip(reads, writes):
        read.wait()
        write.start()
    for write in writes:
        write.wait()


def fused(queries, keys, values, out_grad, gain):
    shape = queries.shape
    rows, width = shape[1], shape[2]
    heads = width // HEAD
    half = heads // 2
    count = lax.axis_size("seq")
    spread = lax.axis_size("dp")
    hops = []
    for axis, size in (("seq", count), ("dp", spread)):
        bit = 1
        while bit < size:
            hops.append((axis, bit))
            bit *= 2
    stages = len(hops)
    scale = math.sqrt(shape[0] * rows * count * spread)
    flat = [a.reshape(rows, width) for a in (queries, keys, values, out_grad)]
    state = pltpu.VMEM((half, HEAD, HEAD), F32)
    held = pltpu.VMEM((heads, HEAD, HEAD), BF16)
    wide = pltpu.VMEM((heads, HEAD, HEAD), F32)
    block = pltpu.VMEM((rows, width), BF16)
    anywhere = pl.BlockSpec(memory_space=pl.ANY)
    result = pl.pallas_call(
        functools.partial(kernel, count // 2, tuple(hops), scale),
        out_shape=[jax.ShapeDtypeStruct((rows, width), BF16)] * 4
        + [jax.ShapeDtypeStruct((heads, HEAD), F32)],
        in_specs=[anywhere] * 5,
        out_specs=[anywhere] * 5,
        scratch_shapes=[state] * 14
        + [held] * 4
        + [wide] * 3
        + [
            pltpu.VMEM((stages + 1, heads, HEAD), F32),
            pltpu.VMEM((stages, heads, HEAD), F32),
            block, block, block, block,
            pltpu.VMEM((heads, HEAD), F32),
            block, block, block, block,
            pltpu.VMEM((heads, HEAD), F32),
            pltpu.SemaphoreType.DMA((6, half)),
            pltpu.SemaphoreType.DMA((6, half)),
            pltpu.SemaphoreType.DMA((stages,)),
            pltpu.SemaphoreType.DMA((stages,)),
            pltpu.SemaphoreType.DMA((5,)),
            pltpu.SemaphoreType.DMA((5,)),
        ],
        compiler_params=pltpu.CompilerParams(
            collective_id=0, has_side_effects=True, vmem_limit_bytes=VMEM_LIMIT
        ),
    )(*flat, gain.reshape(heads, HEAD))
    result = pl.pallas_call(
        flush,
        out_shape=[jax.ShapeDtypeStruct(a.shape, a.dtype) for a in result],
        in_specs=[anywhere] * 5,
        out_specs=[anywhere] * 5,
        scratch_shapes=[pltpu.VMEM(a.shape, a.dtype) for a in result]
        + [pltpu.SemaphoreType.DMA((2, 5))],
        compiler_params=pltpu.CompilerParams(vmem_limit_bytes=VMEM_LIMIT),
    )(*result)
    return tuple(a.reshape(shape) for a in result[:4]) + (result[4].reshape(width),)


def fits(queries):
    def power_of_two(size):
        return size & (size - 1) == 0

    heads = queries.shape[2] // HEAD
    return (
        queries.shape[:2] == (1, GROUP)
        and heads % 2 == 0
        and lax.axis_size("seq") >= 2
        and power_of_two(lax.axis_size("seq"))
        and power_of_two(lax.axis_size("dp"))
    )


def on_device(queries, keys, values, out_grad, gain):
    run = fused if fits(queries) else per_device
    return run(queries, keys, values, out_grad, gain)


def solution(mesh):
    in_specs = (
        P("dp", "seq", None),
        P("dp", "seq", None),
        P("dp", "seq", None),
        P("dp", "seq", None),
        P(),
    )
    out_specs = (
        P("dp", "seq", None),
        P("dp", "seq", None),
        P("dp", "seq", None),
        P("dp", "seq", None),
        P(),
    )
    return jax.shard_map(
        on_device, mesh=mesh, in_specs=in_specs, out_specs=out_specs, check_vma=False
    )
```

```python
import functools
import math

import jax
import jax.numpy as jnp
from jax import lax
from jax.experimental import pallas as pl
from jax.experimental.pallas import tpu as pltpu
from jax.sharding import PartitionSpec as P

HEAD = 128
GROUP = 128
FORWARD_LAG = 3
LAG_FIRST = 5
LAG_HOP = 2
FINAL_LAG = 3
AHEAD = 4
VMEM_LIMIT = 56 * 1024 * 1024
MESH = pl.DeviceIdType.MESH
F32 = jnp.float32
BF16 = jnp.bfloat16


def prefix(part, axis, combine, identity, reverse):
    count = lax.axis_size(axis)
    place = lax.axis_index(axis)
    ahead = count - 1 - place if reverse else place
    gathered = lax.all_gather(part, axis)
    state = jnp.zeros_like(part) + jnp.asarray(identity, part.dtype)

    def one(lap, state):
        source = count - 1 - lap if reverse else lap
        return combine(state, lax.dynamic_index_in_dim(gathered, source, 0, False))

    return lax.fori_loop(0, ahead, one, state)


def add_states(first_part, second_part):
    return first_part + second_part


def split_state(state):
    state_high = state.astype(jnp.bfloat16)
    state_low = (state - state_high.astype(jnp.float32)).astype(jnp.bfloat16)
    return (state_high, state_low)


def per_device(queries, keys, values, out_grad, gain):
    feature_width = queries.shape[2]
    head_size = HEAD
    head_count = feature_width // head_size
    block_size = GROUP

    def to_blocks(array):
        return array.reshape(-1, block_size, head_count, head_size)

    query_rows = to_blocks(queries)
    key_rows = to_blocks(keys)
    value_rows = to_blocks(values)
    grad_rows = to_blocks(out_grad)
    row_index = lax.broadcasted_iota(jnp.int32, (block_size, block_size), 0)
    col_index = lax.broadcasted_iota(jnp.int32, (block_size, block_size), 1)
    causal = (row_index >= col_index).astype(jnp.float32)
    gain_rows = gain.reshape(head_count, head_size)
    key_value = jnp.einsum(
        "nshe,nshf->nhef", key_rows, value_rows, preferred_element_type=jnp.float32
    )
    device_sum = jnp.sum(key_value, axis=0)
    empty_state = jnp.zeros_like(device_sum)
    incoming = prefix(device_sum, "seq", add_states, empty_state, False)
    states = incoming[None] + (jnp.cumsum(key_value, axis=0) - key_value)
    states_high, states_low = split_state(states)
    scores = (
        jnp.einsum("nthe,nshe->nhts", query_rows, key_rows, preferred_element_type=jnp.float32)
        * causal
    )
    weights = scores.astype(jnp.bfloat16)
    attended = jnp.einsum(
        "nhts,nshe->nthe", weights, value_rows, preferred_element_type=jnp.float32
    )
    attended = attended + jnp.einsum(
        "nthe,nhef->nthf", query_rows, states_high, preferred_element_type=jnp.float32
    )
    attended = attended + jnp.einsum(
        "nthe,nhef->nthf", query_rows, states_low, preferred_element_type=jnp.float32
    )
    mean_square = jnp.mean(attended * attended, axis=-1, keepdims=True)
    inv_rms = lax.rsqrt(mean_square + 1e-05)
    normed = attended * inv_rms
    normed_out = (normed * gain_rows).astype(jnp.bfloat16)
    grad_wide = grad_rows.astype(jnp.float32)
    grad_normed = grad_wide * gain_rows
    grad_out = inv_rms * (
        grad_normed - normed * jnp.mean(grad_normed * normed, axis=-1, keepdims=True)
    )
    grad_half = grad_out.astype(jnp.bfloat16)
    gain_part = jnp.sum(normed * grad_wide, axis=(0, 1)).reshape(feature_width)
    total_tokens = queries.shape[0] * queries.shape[1] * lax.axis_size("seq") * lax.axis_size("dp")
    gain_grad = lax.psum(gain_part, ("seq", "dp")) / math.sqrt(total_tokens)
    mixed = (
        jnp.einsum("nthe,nshe->nhts", grad_half, value_rows, preferred_element_type=jnp.float32)
        * causal
    )
    mixed_half = mixed.astype(jnp.bfloat16)
    grad_query = jnp.einsum(
        "nhts,nshe->nthe", mixed_half, key_rows, preferred_element_type=jnp.float32
    )
    grad_query = grad_query + jnp.einsum(
        "nthf,nhef->nthe", grad_half, states_high, preferred_element_type=jnp.float32
    )
    grad_query = grad_query + jnp.einsum(
        "nthf,nhef->nthe", grad_half, states_low, preferred_element_type=jnp.float32
    )
    outer = jnp.einsum("nthe,nthf->nhef", query_rows, grad_half, preferred_element_type=jnp.float32)
    outer_sum = jnp.sum(outer, axis=0)
    arriving = prefix(outer_sum, "seq", add_states, empty_state, True)
    later_sum = arriving[None] + (outer_sum[None] - jnp.cumsum(outer, axis=0))
    later_high, later_low = split_state(later_sum)
    grad_key = jnp.einsum(
        "nhts,nthe->nshe", mixed_half, query_rows, preferred_element_type=jnp.float32
    )
    grad_key = grad_key + jnp.einsum(
        "nshf,nhef->nshe", value_rows, later_high, preferred_element_type=jnp.float32
    )
    grad_key = grad_key + jnp.einsum(
        "nshf,nhef->nshe", value_rows, later_low, preferred_element_type=jnp.float32
    )
    grad_value = jnp.einsum(
        "nhts,nthf->nshf", weights, grad_half, preferred_element_type=jnp.float32
    )
    grad_value = grad_value + jnp.einsum(
        "nshe,nhef->nshf", key_rows, later_high, preferred_element_type=jnp.float32
    )
    grad_value = grad_value + jnp.einsum(
        "nshe,nhef->nshf", key_rows, later_low, preferred_element_type=jnp.float32
    )
    shape_out = queries.shape
    return (
        normed_out.reshape(shape_out),
        grad_query.astype(jnp.bfloat16).reshape(shape_out),
        grad_key.astype(jnp.bfloat16).reshape(shape_out),
        grad_value.astype(jnp.bfloat16).reshape(shape_out),
        gain_grad,
    )


def dot(a, b, a_dim=1, b_dim=0):
    return lax.dot_general(a, b, (((a_dim,), (b_dim,)), ((), ())), preferred_element_type=F32)


def flip(index, bit):
    return index + bit * (1 - 2 * lax.rem(lax.div(index, bit), 2))


def kernel(
    pairs, hops, scale,
    q_hbm, k_hbm, v_hbm, g_hbm, gain_hbm,
    out_hbm, dq_hbm, dk_hbm, dv_hbm, gg_hbm,
    f_own, f_src, f_in, fz_in, fz_out, f_give, f_take,
    b_own, b_src, b_in, bz_in, bz_out, b_give, b_take,
    w_all, hi_all, lo_all, go_all, inner_all, dk_all, dv_all, gain_sum, gain_in,
    q_ref, k_ref, v_ref, g_ref, gain_ref,
    out_ref, dq_ref, dk_ref, dv_ref, gg_ref,
    send, recv, gain_send, gain_recv, load_sem, store_sem,
):
    half = f_own.shape[0]
    stages = len(hops)
    place = lax.axis_index("seq")
    side = lax.rem(place, 2)
    pair = lax.div(place, 2)
    has_before = pair > 0
    has_after = pair < pairs - 1
    partner = {"seq": flip(place, 1)}
    before = {"seq": place - 2}
    after = {"seq": place + 2}
    def needed(sender, at_end):
        return jnp.logical_not((side == sender) & jnp.logical_not(at_end))

    fx_send, fx_wait = needed(1, has_after), needed(0, has_after)
    fg_send, fg_wait = needed(1, has_before), needed(0, has_before)
    bx_send, bx_wait = needed(0, has_before), needed(1, has_before)
    bg_send, bg_wait = needed(0, has_after), needed(1, has_after)
    own_first = side * half
    other_first = (1 - side) * half

    loads = [
        pltpu.make_async_copy(src, dst, load_sem.at[i])
        for i, (src, dst) in enumerate((
            (k_hbm, k_ref), (v_hbm, v_ref), (q_hbm, q_ref), (g_hbm, g_ref), (gain_hbm, gain_ref),
        ))
    ]
    for load in loads:
        load.start()

    stores = [
        pltpu.make_async_copy(src, dst, store_sem.at[i])
        for i, (src, dst) in enumerate((
            (out_ref, out_hbm), (dq_ref, dq_hbm), (dk_ref, dk_hbm), (dv_ref, dv_hbm),
            (gg_ref, gg_hbm),
        ))
    ]

    def greet(device):
        pl.semaphore_signal(barrier, inc=1, device_id=device, device_id_type=MESH)

    def hop_device(axis, bit):
        return {axis: flip(lax.axis_index(axis), bit)}

    barrier = pltpu.get_barrier_semaphore()
    peers = [hop for hop in hops if hop != ("seq", 2)]
    for axis, bit in peers:
        greet(hop_device(axis, bit))

    @pl.when(has_before)
    def _():
        greet(before)

    @pl.when(has_after)
    def _():
        greet(after)

    def move(kind, src, dst, c, device):
        return pltpu.make_async_remote_copy(
            src_ref=src.at[c], dst_ref=dst.at[c],
            send_sem=send.at[kind, c], recv_sem=recv.at[kind, c],
            device_id=device, device_id_type=MESH,
        )

    def fx(c):
        return move(0, f_src, f_in, c, partner)

    def fz(c, device):
        return move(1, fz_out, fz_in, c, device)

    def fg(c):
        return move(2, f_give, f_take, c, partner)

    def bx(c):
        return move(3, b_src, b_in, c, partner)

    def bz(c, device):
        return move(4, bz_out, bz_in, c, device)

    def bg(c):
        return move(5, b_give, b_take, c, partner)

    def gain_move(s):
        axis, bit = hops[s]
        return pltpu.make_async_remote_copy(
            src_ref=gain_sum.at[s], dst_ref=gain_in.at[s],
            send_sem=gain_send.at[s], recv_sem=gain_recv.at[s],
            device_id=hop_device(axis, bit), device_id_type=MESH,
        )

    def cols(h):
        return pl.ds(pl.multiple_of(h * HEAD, HEAD), HEAD)

    row = lax.broadcasted_iota(jnp.int32, (GROUP, GROUP), 0)
    col = lax.broadcasted_iota(jnp.int32, (GROUP, GROUP), 1)
    causal = row >= col

    def key_value(h):
        return dot(k_ref[:, cols(h)], v_ref[:, cols(h)], 0, 0)

    def local_forward(h):
        w = jnp.where(causal, dot(q_ref[:, cols(h)], k_ref[:, cols(h)], 1, 1), 0.0).astype(BF16)
        return w, dot(w, v_ref[:, cols(h)])

    def forward(h, state):
        q = q_ref[:, cols(h)]
        hi, lo = split_state(state)
        attended = inner_all[h] + dot(
            jnp.concatenate([q, q], axis=1), jnp.concatenate([hi, lo], axis=0)
        )
        inv = lax.rsqrt(jnp.mean(attended * attended, axis=1, keepdims=True) + 1e-05)
        normed = attended * inv
        gain = gain_ref[pl.ds(h, 1), :]
        wide = g_ref[:, cols(h)].astype(F32)
        grad_normed = wide * gain
        go = inv * (
            grad_normed - normed * jnp.mean(grad_normed * normed, axis=1, keepdims=True)
        )
        go = go.astype(BF16)
        normed_out = (normed * gain).astype(BF16)
        gain_part = jnp.sum(normed * wide, axis=0, keepdims=True)
        return dot(q, go, 0, 0), hi, lo, go, normed_out, gain_part

    def keep_forward(h, results):
        outer, hi, lo, go, normed_out, gain_part = results
        hi_all[h] = hi
        lo_all[h] = lo
        go_all[h] = go
        out_ref[:, cols(h)] = normed_out
        gain_sum[0, pl.ds(h, 1), :] = gain_part

    def local_backward(h):
        go = go_all[h]
        mixed = jnp.where(causal, dot(go, v_ref[:, cols(h)], 1, 1), 0.0).astype(BF16)
        dq = dot(mixed, k_ref[:, cols(h)]) + dot(
            jnp.concatenate([go, go], axis=1),
            jnp.concatenate([hi_all[h], lo_all[h]], axis=1), 1, 1,
        )
        return dq.astype(BF16), dot(mixed, q_ref[:, cols(h)], 0, 0), dot(w_all[h], go, 0, 0)

    def keep_local_backward(h, results):
        dq_ref[:, cols(h)], dk_all[h], dv_all[h] = results

    def backward(h, later):
        hi, lo = split_state(later)
        v = v_ref[:, cols(h)]
        k = k_ref[:, cols(h)]
        dk = dk_all[h] + dot(
            jnp.concatenate([v, v], axis=1), jnp.concatenate([hi, lo], axis=1), 1, 1
        )
        dv = dv_all[h] + dot(
            jnp.concatenate([k, k], axis=1), jnp.concatenate([hi, lo], axis=0)
        )
        return dk.astype(BF16), dv.astype(BF16)

    def keep_backward(h, results):
        dk_ref[:, cols(h)], dv_ref[:, cols(h)] = results

    def clear(ref, condition):
        @pl.when(condition)
        def _():
            ref[...] = jnp.zeros_like(ref)

    clear(fz_in, jnp.logical_not(has_before))
    clear(bz_in, jnp.logical_not(has_after))
    clear(f_take, jnp.logical_not(fg_wait))
    clear(b_take, jnp.logical_not(bg_wait))

    loads[0].wait()
    loads[1].wait()
    f_src[0] = key_value(other_first)
    ends = has_before.astype(jnp.int32) + has_after.astype(jnp.int32)
    pl.semaphore_wait(barrier, len(peers) + ends)

    def start_if(condition, copy):
        @pl.when(condition)
        def _():
            copy.start()

    def recv_if(condition, copy):
        @pl.when(condition)
        def _():
            copy.wait_recv()

    def sent_if(condition, copy):
        @pl.when(condition)
        def _():
            copy.wait_send()

    start_if(fx_send, fx(0))
    for c in range(1, half):
        f_src[c] = key_value(other_first + c)
        if c < AHEAD:
            start_if(fx_send, fx(c))
    for c in range(half):
        f_own[c] = key_value(own_first + c)
    for load in loads[2:]:
        load.wait()

    lag = LAG_FIRST + LAG_HOP * (pairs - 1 - pair)
    late = 2 * pair >= pairs
    forward_end = half + FORWARD_LAG
    local_lag = jnp.where(late, forward_end, FORWARD_LAG + 1)
    final_lag = jnp.maximum(lag + FINAL_LAG, forward_end + 1)
    most = max(LAG_FIRST + LAG_HOP * (pairs - 1) + FINAL_LAG, forward_end + 1)
    steps = max(half + most, forward_end + stages)

    def local_step(c):
        mine = local_forward(own_first + c)
        theirs = local_forward(other_first + c)
        w_all[own_first + c], inner_all[own_first + c] = mine
        w_all[other_first + c], inner_all[other_first + c] = theirs

    @pl.when(late)
    def _():
        lax.fori_loop(0, half, lambda c, carry: (local_step(c), carry)[1], 0)

    def step(t, carry):
        @pl.when(t < half)
        def _():
            recv_if(fx_wait, fx(t))
            recv_if(has_before, fz(t, partner))

            past, mine, theirs = fz_in[t], f_own[t], f_in[t]
            fz_out[t] = past + (mine + theirs)
            start_if(has_after, fz(t, after))
            f_give[t] = past + jnp.where(side == 0, mine, 0.0)
            start_if(fg_send, fg(t))
            start_if(fx_send & (t < half - AHEAD), fx(jnp.minimum(t + AHEAD, half - 1)))
            f_own[t] = past + jnp.where(side == 1, theirs, 0.0)

        @pl.when((t >= FORWARD_LAG) & (t < half + FORWARD_LAG))
        def _():
            c = t - FORWARD_LAG
            recv_if(fg_wait, fg(c))
            theirs = forward(other_first + c, f_take[c])
            mine = forward(own_first + c, f_own[c])
            b_src[c] = theirs[0]
            start_if(bx_send, bx(c))
            b_own[c] = mine[0]
            keep_forward(other_first + c, theirs)
            keep_forward(own_first + c, mine)

        j = t - lag

        @pl.when((j >= 0) & (j < half))
        def _():
            recv_if(bx_wait, bx(j))
            recv_if(has_after, bz(j, partner))

            past, mine, theirs = bz_in[j], b_own[j], b_in[j]
            bz_out[j] = past + (mine + theirs)
            start_if(has_before, bz(j, before))
            b_give[j] = past + jnp.where(side == 1, mine, 0.0)
            start_if(bg_send, bg(j))
            b_own[j] = past + jnp.where(side == 0, theirs, 0.0)

        @pl.when((t < half) & jnp.logical_not(late))
        def _():
            local_step(t)

        b = t - local_lag

        @pl.when((b >= 0) & (b < half))
        def _():
            mine = local_backward(own_first + b)
            theirs = local_backward(other_first + b)
            keep_local_backward(own_first + b, mine)
            keep_local_backward(other_first + b, theirs)

        e = t - final_lag

        @pl.when((e >= 0) & (e < half))
        def _():
            recv_if(bg_wait, bg(e))
            mine = backward(own_first + e, b_own[e])
            theirs = backward(other_first + e, b_take[e])
            keep_backward(own_first + e, mine)
            keep_backward(other_first + e, theirs)

        for s in range(stages + 1):

            @pl.when(t == forward_end - 1 + s)
            def _(s=s):
                if s > 0:
                    gain_move(s - 1).wait_recv()
                    gain_sum[s] = gain_sum[s - 1] + gain_in[s - 1]
                if s < stages:
                    gain_move(s).start()
                else:
                    gg_ref[...] = gain_sum[s] / scale
                    stores[4].start()
                if s == 0:
                    stores[0].start()

        return carry

    lax.fori_loop(0, steps, step, 0)
    for store in stores[1:4]:
        store.start()

    def finish(c, carry):
        sent_if(fx_send, fx(c))
        sent_if(fg_send, fg(c))
        sent_if(bx_send, bx(c))
        sent_if(bg_send, bg(c))
        sent_if(has_after, fz(c, after))
        sent_if(has_before, bz(c, before))
        return carry

    lax.fori_loop(0, half, finish, 0)
    for s in range(stages):
        gain_move(s).wait_send()
    for store in stores:
        store.wait()


def flush(*refs):
    source, target, held = refs[:5], refs[5:10], refs[10:15]
    sems = refs[15]
    reads = [pltpu.make_async_copy(source[i], held[i], sems.at[0, i]) for i in range(5)]
    writes = [pltpu.make_async_copy(held[i], target[i], sems.at[1, i]) for i in range(5)]
    for read in reads:
        read.start()
    for read, write in zip(reads, writes):
        read.wait()
        write.start()
    for write in writes:
        write.wait()


def fused(queries, keys, values, out_grad, gain):
    shape = queries.shape
    rows, width = shape[1], shape[2]
    heads = width // HEAD
    half = heads // 2
    count = lax.axis_size("seq")
    spread = lax.axis_size("dp")
    hops = []
    for axis, size in (("seq", count), ("dp", spread)):
        bit = 1
        while bit < size:
            hops.append((axis, bit))
            bit *= 2
    stages = len(hops)
    scale = math.sqrt(shape[0] * rows * count * spread)
    flat = [a.reshape(rows, width) for a in (queries, keys, values, out_grad)]
    state = pltpu.VMEM((half, HEAD, HEAD), F32)
    held = pltpu.VMEM((heads, HEAD, HEAD), BF16)
    wide = pltpu.VMEM((heads, HEAD, HEAD), F32)
    block = pltpu.VMEM((rows, width), BF16)
    anywhere = pl.BlockSpec(memory_space=pl.ANY)
    result = pl.pallas_call(
        functools.partial(kernel, count // 2, tuple(hops), scale),
        out_shape=[jax.ShapeDtypeStruct((rows, width), BF16)] * 4
        + [jax.ShapeDtypeStruct((heads, HEAD), F32)],
        in_specs=[anywhere] * 5,
        out_specs=[anywhere] * 5,
        scratch_shapes=[state] * 14
        + [held] * 4
        + [wide] * 3
        + [
            pltpu.VMEM((stages + 1, heads, HEAD), F32),
            pltpu.VMEM((stages, heads, HEAD), F32),
            block, block, block, block,
            pltpu.VMEM((heads, HEAD), F32),
            block, block, block, block,
            pltpu.VMEM((heads, HEAD), F32),
            pltpu.SemaphoreType.DMA((6, half)),
            pltpu.SemaphoreType.DMA((6, half)),
            pltpu.SemaphoreType.DMA((stages,)),
            pltpu.SemaphoreType.DMA((stages,)),
            pltpu.SemaphoreType.DMA((5,)),
            pltpu.SemaphoreType.DMA((5,)),
        ],
        compiler_params=pltpu.CompilerParams(
            collective_id=0, has_side_effects=True, vmem_limit_bytes=VMEM_LIMIT
        ),
    )(*flat, gain.reshape(heads, HEAD))
    result = pl.pallas_call(
        flush,
        out_shape=[jax.ShapeDtypeStruct(a.shape, a.dtype) for a in result],
        in_specs=[anywhere] * 5,
        out_specs=[anywhere] * 5,
        scratch_shapes=[pltpu.VMEM(a.shape, a.dtype) for a in result]
        + [pltpu.SemaphoreType.DMA((2, 5))],
        compiler_params=pltpu.CompilerParams(vmem_limit_bytes=VMEM_LIMIT),
    )(*result)
    return tuple(a.reshape(shape) for a in result[:4]) + (result[4].reshape(width),)


def fits(queries):
    def power_of_two(size):
        return size & (size - 1) == 0

    heads = queries.shape[2] // HEAD
    return (
        queries.shape[:2] == (1, GROUP)
        and heads % 2 == 0
        and lax.axis_size("seq") >= 2
        and power_of_two(lax.axis_size("seq"))
        and power_of_two(lax.axis_size("dp"))
    )


def on_device(queries, keys, values, out_grad, gain):
    run = fused if fits(queries) else per_device
    return run(queries, keys, values, out_grad, gain)


def solution(mesh):
    in_specs = (
        P("dp", "seq", None),
        P("dp", "seq", None),
        P("dp", "seq", None),
        P("dp", "seq", None),
        P(),
    )
    out_specs = (
        P("dp", "seq", None),
        P("dp", "seq", None),
        P("dp", "seq", None),
        P("dp", "seq", None),
        P(),
    )
    return jax.shard_map(
        on_device, mesh=mesh, in_specs=in_specs, out_specs=out_specs, check_vma=False
    )
```

```python
import functools
import math

import jax
import jax.numpy as jnp
from jax import lax
from jax.experimental import pallas as pl
from jax.experimental.pallas import tpu as pltpu
from jax.sharding import PartitionSpec as P

HEAD = 128
GROUP = 128
FORWARD_LAG = 3
LAG_FIRST = 5
LAG_HOP = 2
FINAL_LAG = 3
AHEAD_FIRST = 2
AHEAD_HOP = 2
VMEM_LIMIT = 56 * 1024 * 1024
MESH = pl.DeviceIdType.MESH
F32 = jnp.float32
BF16 = jnp.bfloat16


def prefix(part, axis, combine, identity, reverse):
    count = lax.axis_size(axis)
    place = lax.axis_index(axis)
    ahead = count - 1 - place if reverse else place
    gathered = lax.all_gather(part, axis)
    state = jnp.zeros_like(part) + jnp.asarray(identity, part.dtype)

    def one(lap, state):
        source = count - 1 - lap if reverse else lap
        return combine(state, lax.dynamic_index_in_dim(gathered, source, 0, False))

    return lax.fori_loop(0, ahead, one, state)


def add_states(first_part, second_part):
    return first_part + second_part


def split_state(state):
    state_high = state.astype(jnp.bfloat16)
    state_low = (state - state_high.astype(jnp.float32)).astype(jnp.bfloat16)
    return (state_high, state_low)


def per_device(queries, keys, values, out_grad, gain):
    feature_width = queries.shape[2]
    head_size = HEAD
    head_count = feature_width // head_size
    block_size = GROUP

    def to_blocks(array):
        return array.reshape(-1, block_size, head_count, head_size)

    query_rows = to_blocks(queries)
    key_rows = to_blocks(keys)
    value_rows = to_blocks(values)
    grad_rows = to_blocks(out_grad)
    row_index = lax.broadcasted_iota(jnp.int32, (block_size, block_size), 0)
    col_index = lax.broadcasted_iota(jnp.int32, (block_size, block_size), 1)
    causal = (row_index >= col_index).astype(jnp.float32)
    gain_rows = gain.reshape(head_count, head_size)
    key_value = jnp.einsum(
        "nshe,nshf->nhef", key_rows, value_rows, preferred_element_type=jnp.float32
    )
    device_sum = jnp.sum(key_value, axis=0)
    empty_state = jnp.zeros_like(device_sum)
    incoming = prefix(device_sum, "seq", add_states, empty_state, False)
    states = incoming[None] + (jnp.cumsum(key_value, axis=0) - key_value)
    states_high, states_low = split_state(states)
    scores = (
        jnp.einsum("nthe,nshe->nhts", query_rows, key_rows, preferred_element_type=jnp.float32)
        * causal
    )
    weights = scores.astype(jnp.bfloat16)
    attended = jnp.einsum(
        "nhts,nshe->nthe", weights, value_rows, preferred_element_type=jnp.float32
    )
    attended = attended + jnp.einsum(
        "nthe,nhef->nthf", query_rows, states_high, preferred_element_type=jnp.float32
    )
    attended = attended + jnp.einsum(
        "nthe,nhef->nthf", query_rows, states_low, preferred_element_type=jnp.float32
    )
    mean_square = jnp.mean(attended * attended, axis=-1, keepdims=True)
    inv_rms = lax.rsqrt(mean_square + 1e-05)
    normed = attended * inv_rms
    normed_out = (normed * gain_rows).astype(jnp.bfloat16)
    grad_wide = grad_rows.astype(jnp.float32)
    grad_normed = grad_wide * gain_rows
    grad_out = inv_rms * (
        grad_normed - normed * jnp.mean(grad_normed * normed, axis=-1, keepdims=True)
    )
    grad_half = grad_out.astype(jnp.bfloat16)
    gain_part = jnp.sum(normed * grad_wide, axis=(0, 1)).reshape(feature_width)
    total_tokens = queries.shape[0] * queries.shape[1] * lax.axis_size("seq") * lax.axis_size("dp")
    gain_grad = lax.psum(gain_part, ("seq", "dp")) / math.sqrt(total_tokens)
    mixed = (
        jnp.einsum("nthe,nshe->nhts", grad_half, value_rows, preferred_element_type=jnp.float32)
        * causal
    )
    mixed_half = mixed.astype(jnp.bfloat16)
    grad_query = jnp.einsum(
        "nhts,nshe->nthe", mixed_half, key_rows, preferred_element_type=jnp.float32
    )
    grad_query = grad_query + jnp.einsum(
        "nthf,nhef->nthe", grad_half, states_high, preferred_element_type=jnp.float32
    )
    grad_query = grad_query + jnp.einsum(
        "nthf,nhef->nthe", grad_half, states_low, preferred_element_type=jnp.float32
    )
    outer = jnp.einsum("nthe,nthf->nhef", query_rows, grad_half, preferred_element_type=jnp.float32)
    outer_sum = jnp.sum(outer, axis=0)
    arriving = prefix(outer_sum, "seq", add_states, empty_state, True)
    later_sum = arriving[None] + (outer_sum[None] - jnp.cumsum(outer, axis=0))
    later_high, later_low = split_state(later_sum)
    grad_key = jnp.einsum(
        "nhts,nthe->nshe", mixed_half, query_rows, preferred_element_type=jnp.float32
    )
    grad_key = grad_key + jnp.einsum(
        "nshf,nhef->nshe", value_rows, later_high, preferred_element_type=jnp.float32
    )
    grad_key = grad_key + jnp.einsum(
        "nshf,nhef->nshe", value_rows, later_low, preferred_element_type=jnp.float32
    )
    grad_value = jnp.einsum(
        "nhts,nthf->nshf", weights, grad_half, preferred_element_type=jnp.float32
    )
    grad_value = grad_value + jnp.einsum(
        "nshe,nhef->nshf", key_rows, later_high, preferred_element_type=jnp.float32
    )
    grad_value = grad_value + jnp.einsum(
        "nshe,nhef->nshf", key_rows, later_low, preferred_element_type=jnp.float32
    )
    shape_out = queries.shape
    return (
        normed_out.reshape(shape_out),
        grad_query.astype(jnp.bfloat16).reshape(shape_out),
        grad_key.astype(jnp.bfloat16).reshape(shape_out),
        grad_value.astype(jnp.bfloat16).reshape(shape_out),
        gain_grad,
    )


def dot(a, b, a_dim=1, b_dim=0):
    return lax.dot_general(a, b, (((a_dim,), (b_dim,)), ((), ())), preferred_element_type=F32)


def flip(index, bit):
    return index + bit * (1 - 2 * lax.rem(lax.div(index, bit), 2))


def kernel(
    pairs, hops, scale,
    q_hbm, k_hbm, v_hbm, g_hbm, gain_hbm,
    out_hbm, dq_hbm, dk_hbm, dv_hbm, gg_hbm,
    f_own, f_src, f_in, fz_in, fz_out, f_give, f_take,
    b_own, b_src, b_in, bz_in, bz_out, b_give, b_take,
    w_all, hi_all, lo_all, go_all, inner_all, dk_all, dv_all, gain_sum, gain_in,
    q_ref, k_ref, v_ref, g_ref, gain_ref,
    out_ref, dq_ref, dk_ref, dv_ref, gg_ref,
    send, recv, gain_send, gain_recv, load_sem, store_sem,
):
    half = f_own.shape[0]
    stages = len(hops)
    place = lax.axis_index("seq")
    side = lax.rem(place, 2)
    pair = lax.div(place, 2)
    has_before = pair > 0
    has_after = pair < pairs - 1
    partner = {"seq": flip(place, 1)}
    before = {"seq": place - 2}
    after = {"seq": place + 2}
    def needed(sender, at_end):
        return jnp.logical_not((side == sender) & jnp.logical_not(at_end))

    fx_send, fx_wait = needed(1, has_after), needed(0, has_after)
    fg_send, fg_wait = needed(1, has_before), needed(0, has_before)
    bx_send, bx_wait = needed(0, has_before), needed(1, has_before)
    bg_send, bg_wait = needed(0, has_after), needed(1, has_after)
    own_first = side * half
    other_first = (1 - side) * half

    loads = [
        pltpu.make_async_copy(src, dst, load_sem.at[i])
        for i, (src, dst) in enumerate((
            (k_hbm, k_ref), (v_hbm, v_ref), (q_hbm, q_ref), (g_hbm, g_ref), (gain_hbm, gain_ref),
        ))
    ]
    for load in loads:
        load.start()

    stores = [
        pltpu.make_async_copy(src, dst, store_sem.at[i])
        for i, (src, dst) in enumerate((
            (out_ref, out_hbm), (dq_ref, dq_hbm), (dk_ref, dk_hbm), (dv_ref, dv_hbm),
            (gg_ref, gg_hbm),
        ))
    ]

    def greet(device):
        pl.semaphore_signal(barrier, inc=1, device_id=device, device_id_type=MESH)

    def hop_device(axis, bit):
        return {axis: flip(lax.axis_index(axis), bit)}

    barrier = pltpu.get_barrier_semaphore()
    peers = [hop for hop in hops if hop != ("seq", 2)]
    for axis, bit in peers:
        greet(hop_device(axis, bit))

    @pl.when(has_before)
    def _():
        greet(before)

    @pl.when(has_after)
    def _():
        greet(after)

    def move(kind, src, dst, c, device):
        return pltpu.make_async_remote_copy(
            src_ref=src.at[c], dst_ref=dst.at[c],
            send_sem=send.at[kind, c], recv_sem=recv.at[kind, c],
            device_id=device, device_id_type=MESH,
        )

    def fx(c):
        return move(0, f_src, f_in, c, partner)

    def fz(c, device):
        return move(1, fz_out, fz_in, c, device)

    def fg(c):
        return move(2, f_give, f_take, c, partner)

    def bx(c):
        return move(3, b_src, b_in, c, partner)

    def bz(c, device):
        return move(4, bz_out, bz_in, c, device)

    def bg(c):
        return move(5, b_give, b_take, c, partner)

    def gain_move(s):
        axis, bit = hops[s]
        return pltpu.make_async_remote_copy(
            src_ref=gain_sum.at[s], dst_ref=gain_in.at[s],
            send_sem=gain_send.at[s], recv_sem=gain_recv.at[s],
            device_id=hop_device(axis, bit), device_id_type=MESH,
        )

    def cols(h):
        return pl.ds(pl.multiple_of(h * HEAD, HEAD), HEAD)

    row = lax.broadcasted_iota(jnp.int32, (GROUP, GROUP), 0)
    col = lax.broadcasted_iota(jnp.int32, (GROUP, GROUP), 1)
    causal = row >= col

    def key_value(h):
        return dot(k_ref[:, cols(h)], v_ref[:, cols(h)], 0, 0)

    def local_forward(h):
        w = jnp.where(causal, dot(q_ref[:, cols(h)], k_ref[:, cols(h)], 1, 1), 0.0).astype(BF16)
        return w, dot(w, v_ref[:, cols(h)])

    def forward(h, state):
        q = q_ref[:, cols(h)]
        hi, lo = split_state(state)
        attended = inner_all[h] + dot(
            jnp.concatenate([q, q], axis=1), jnp.concatenate([hi, lo], axis=0)
        )
        inv = lax.rsqrt(jnp.mean(attended * attended, axis=1, keepdims=True) + 1e-05)
        normed = attended * inv
        gain = gain_ref[pl.ds(h, 1), :]
        wide = g_ref[:, cols(h)].astype(F32)
        grad_normed = wide * gain
        go = inv * (
            grad_normed - normed * jnp.mean(grad_normed * normed, axis=1, keepdims=True)
        )
        go = go.astype(BF16)
        normed_out = (normed * gain).astype(BF16)
        gain_part = jnp.sum(normed * wide, axis=0, keepdims=True)
        return dot(q, go, 0, 0), hi, lo, go, normed_out, gain_part

    def keep_forward(h, results):
        outer, hi, lo, go, normed_out, gain_part = results
        hi_all[h] = hi
        lo_all[h] = lo
        go_all[h] = go
        out_ref[:, cols(h)] = normed_out
        gain_sum[0, pl.ds(h, 1), :] = gain_part

    def local_backward(h):
        go = go_all[h]
        mixed = jnp.where(causal, dot(go, v_ref[:, cols(h)], 1, 1), 0.0).astype(BF16)
        dq = dot(mixed, k_ref[:, cols(h)]) + dot(
            jnp.concatenate([go, go], axis=1),
            jnp.concatenate([hi_all[h], lo_all[h]], axis=1), 1, 1,
        )
        return dq.astype(BF16), dot(mixed, q_ref[:, cols(h)], 0, 0), dot(w_all[h], go, 0, 0)

    def keep_local_backward(h, results):
        dq_ref[:, cols(h)], dk_all[h], dv_all[h] = results

    def backward(h, later):
        hi, lo = split_state(later)
        v = v_ref[:, cols(h)]
        k = k_ref[:, cols(h)]
        dk = dk_all[h] + dot(
            jnp.concatenate([v, v], axis=1), jnp.concatenate([hi, lo], axis=1), 1, 1
        )
        dv = dv_all[h] + dot(
            jnp.concatenate([k, k], axis=1), jnp.concatenate([hi, lo], axis=0)
        )
        return dk.astype(BF16), dv.astype(BF16)

    def keep_backward(h, results):
        dk_ref[:, cols(h)], dv_ref[:, cols(h)] = results

    def clear(ref, condition):
        @pl.when(condition)
        def _():
            ref[...] = jnp.zeros_like(ref)

    clear(fz_in, jnp.logical_not(has_before))
    clear(bz_in, jnp.logical_not(has_after))
    clear(f_take, jnp.logical_not(fg_wait))
    clear(b_take, jnp.logical_not(bg_wait))

    loads[0].wait()
    loads[1].wait()
    f_src[0] = key_value(other_first)
    ends = has_before.astype(jnp.int32) + has_after.astype(jnp.int32)
    pl.semaphore_wait(barrier, len(peers) + ends)

    def start_if(condition, copy):
        @pl.when(condition)
        def _():
            copy.start()

    def recv_if(condition, copy):
        @pl.when(condition)
        def _():
            copy.wait_recv()

    def sent_if(condition, copy):
        @pl.when(condition)
        def _():
            copy.wait_send()

    ahead = jnp.minimum(half, AHEAD_FIRST + AHEAD_HOP * pair)
    start_if(fx_send, fx(0))
    for c in range(1, half):
        f_src[c] = key_value(other_first + c)
        start_if(fx_send & (c < ahead), fx(c))
    for c in range(half):
        f_own[c] = key_value(own_first + c)
    for load in loads[2:]:
        load.wait()

    lag = LAG_FIRST + LAG_HOP * (pairs - 1 - pair)
    late = 2 * pair >= pairs
    forward_end = half + FORWARD_LAG
    local_lag = jnp.where(late, forward_end, FORWARD_LAG + 1)
    give_lag = jnp.maximum(lag, forward_end)
    final_lag = give_lag + FINAL_LAG
    most = max(LAG_FIRST + LAG_HOP * (pairs - 1), forward_end) + FINAL_LAG
    steps = max(half + most, forward_end + stages)

    def local_step(c):
        mine = local_forward(own_first + c)
        theirs = local_forward(other_first + c)
        w_all[own_first + c], inner_all[own_first + c] = mine
        w_all[other_first + c], inner_all[other_first + c] = theirs

    @pl.when(late)
    def _():
        lax.fori_loop(0, half, lambda c, carry: (local_step(c), carry)[1], 0)

    def step(t, carry):
        @pl.when(t < half)
        def _():
            recv_if(fx_wait, fx(t))
            recv_if(has_before, fz(t, partner))

            past, mine, theirs = fz_in[t], f_own[t], f_in[t]
            fz_out[t] = past + (mine + theirs)
            start_if(has_after, fz(t, after))
            f_give[t] = past + jnp.where(side == 0, mine, 0.0)
            start_if(fg_send, fg(t))
            start_if(fx_send & (t < half - ahead), fx(jnp.minimum(t + ahead, half - 1)))
            f_own[t] = past + jnp.where(side == 1, theirs, 0.0)

        @pl.when((t >= FORWARD_LAG) & (t < half + FORWARD_LAG))
        def _():
            c = t - FORWARD_LAG
            recv_if(fg_wait, fg(c))
            theirs = forward(other_first + c, f_take[c])
            mine = forward(own_first + c, f_own[c])
            b_src[c] = theirs[0]
            start_if(bx_send, bx(c))
            b_own[c] = mine[0]
            keep_forward(other_first + c, theirs)
            keep_forward(own_first + c, mine)

        j = t - lag

        @pl.when((j >= 0) & (j < half))
        def _():
            recv_if(bx_wait, bx(j))
            recv_if(has_after, bz(j, partner))

            past, mine, theirs = bz_in[j], b_own[j], b_in[j]
            bz_out[j] = past + (mine + theirs)
            start_if(has_before, bz(j, before))
            b_give[j] = past + jnp.where(side == 1, mine, 0.0)
            b_own[j] = past + jnp.where(side == 0, theirs, 0.0)

        u = t - give_lag

        @pl.when((u >= 0) & (u < half))
        def _():
            start_if(bg_send, bg(u))

        @pl.when((t < half) & jnp.logical_not(late))
        def _():
            local_step(t)

        b = t - local_lag

        @pl.when((b >= 0) & (b < half))
        def _():
            mine = local_backward(own_first + b)
            theirs = local_backward(other_first + b)
            keep_local_backward(own_first + b, mine)
            keep_local_backward(other_first + b, theirs)

        e = t - final_lag

        @pl.when((e >= 0) & (e < half))
        def _():
            recv_if(bg_wait, bg(e))
            mine = backward(own_first + e, b_own[e])
            theirs = backward(other_first + e, b_take[e])
            keep_backward(own_first + e, mine)
            keep_backward(other_first + e, theirs)

        for s in range(stages + 1):

            @pl.when(t == forward_end - 1 + s)
            def _(s=s):
                if s > 0:
                    gain_move(s - 1).wait_recv()
                    gain_sum[s] = gain_sum[s - 1] + gain_in[s - 1]
                if s < stages:
                    gain_move(s).start()
                else:
                    gg_ref[...] = gain_sum[s] / scale
                    stores[4].start()
                if s == 0:
                    stores[0].start()

        return carry

    lax.fori_loop(0, steps, step, 0)
    for store in stores[1:4]:
        store.start()

    def finish(c, carry):
        sent_if(fx_send, fx(c))
        sent_if(fg_send, fg(c))
        sent_if(bx_send, bx(c))
        sent_if(bg_send, bg(c))
        sent_if(has_after, fz(c, after))
        sent_if(has_before, bz(c, before))
        return carry

    lax.fori_loop(0, half, finish, 0)
    for s in range(stages):
        gain_move(s).wait_send()
    for store in stores:
        store.wait()


def flush(*refs):
    source, target, held = refs[:5], refs[5:10], refs[10:15]
    sems = refs[15]
    reads = [pltpu.make_async_copy(source[i], held[i], sems.at[0, i]) for i in range(5)]
    writes = [pltpu.make_async_copy(held[i], target[i], sems.at[1, i]) for i in range(5)]
    for read in reads:
        read.start()
    for read, write in zip(reads, writes):
        read.wait()
        write.start()
    for write in writes:
        write.wait()


def fused(queries, keys, values, out_grad, gain):
    shape = queries.shape
    rows, width = shape[1], shape[2]
    heads = width // HEAD
    half = heads // 2
    count = lax.axis_size("seq")
    spread = lax.axis_size("dp")
    hops = []
    for axis, size in (("seq", count), ("dp", spread)):
        bit = 1
        while bit < size:
            hops.append((axis, bit))
            bit *= 2
    stages = len(hops)
    scale = math.sqrt(shape[0] * rows * count * spread)
    flat = [a.reshape(rows, width) for a in (queries, keys, values, out_grad)]
    state = pltpu.VMEM((half, HEAD, HEAD), F32)
    held = pltpu.VMEM((heads, HEAD, HEAD), BF16)
    wide = pltpu.VMEM((heads, HEAD, HEAD), F32)
    block = pltpu.VMEM((rows, width), BF16)
    anywhere = pl.BlockSpec(memory_space=pl.ANY)
    result = pl.pallas_call(
        functools.partial(kernel, count // 2, tuple(hops), scale),
        out_shape=[jax.ShapeDtypeStruct((rows, width), BF16)] * 4
        + [jax.ShapeDtypeStruct((heads, HEAD), F32)],
        in_specs=[anywhere] * 5,
        out_specs=[anywhere] * 5,
        scratch_shapes=[state] * 14
        + [held] * 4
        + [wide] * 3
        + [
            pltpu.VMEM((stages + 1, heads, HEAD), F32),
            pltpu.VMEM((stages, heads, HEAD), F32),
            block, block, block, block,
            pltpu.VMEM((heads, HEAD), F32),
            block, block, block, block,
            pltpu.VMEM((heads, HEAD), F32),
            pltpu.SemaphoreType.DMA((6, half)),
            pltpu.SemaphoreType.DMA((6, half)),
            pltpu.SemaphoreType.DMA((stages,)),
            pltpu.SemaphoreType.DMA((stages,)),
            pltpu.SemaphoreType.DMA((5,)),
            pltpu.SemaphoreType.DMA((5,)),
        ],
        compiler_params=pltpu.CompilerParams(
            collective_id=0, has_side_effects=True, vmem_limit_bytes=VMEM_LIMIT
        ),
    )(*flat, gain.reshape(heads, HEAD))
    result = pl.pallas_call(
        flush,
        out_shape=[jax.ShapeDtypeStruct(a.shape, a.dtype) for a in result],
        in_specs=[anywhere] * 5,
        out_specs=[anywhere] * 5,
        scratch_shapes=[pltpu.VMEM(a.shape, a.dtype) for a in result]
        + [pltpu.SemaphoreType.DMA((2, 5))],
        compiler_params=pltpu.CompilerParams(vmem_limit_bytes=VMEM_LIMIT),
    )(*result)
    return tuple(a.reshape(shape) for a in result[:4]) + (result[4].reshape(width),)


def fits(queries):
    def power_of_two(size):
        return size & (size - 1) == 0

    heads = queries.shape[2] // HEAD
    return (
        queries.shape[:2] == (1, GROUP)
        and heads % 2 == 0
        and lax.axis_size("seq") >= 2
        and power_of_two(lax.axis_size("seq"))
        and power_of_two(lax.axis_size("dp"))
    )


def on_device(queries, keys, values, out_grad, gain):
    run = fused if fits(queries) else per_device
    return run(queries, keys, values, out_grad, gain)


def solution(mesh):
    in_specs = (
        P("dp", "seq", None),
        P("dp", "seq", None),
        P("dp", "seq", None),
        P("dp", "seq", None),
        P(),
    )
    out_specs = (
        P("dp", "seq", None),
        P("dp", "seq", None),
        P("dp", "seq", None),
        P("dp", "seq", None),
        P(),
    )
    return jax.shard_map(
        on_device, mesh=mesh, in_specs=in_specs, out_specs=out_specs, check_vma=False
    )
```

```python
import functools
import math

import jax
import jax.numpy as jnp
from jax import lax
from jax.experimental import pallas as pl
from jax.experimental.pallas import tpu as pltpu
from jax.sharding import PartitionSpec as P

HEAD = 128
GROUP = 128
PARTS = 2
FORWARD_LAG = 3
LAG_FIRST = 5
LAG_HOP = 2
FINAL_LAG = 3
AHEAD_FIRST = 2
AHEAD_HOP = 2
VMEM_LIMIT = 56 * 1024 * 1024
MESH = pl.DeviceIdType.MESH
F32 = jnp.float32
BF16 = jnp.bfloat16


def prefix(part, axis, combine, identity, reverse):
    count = lax.axis_size(axis)
    place = lax.axis_index(axis)
    ahead = count - 1 - place if reverse else place
    gathered = lax.all_gather(part, axis)
    state = jnp.zeros_like(part) + jnp.asarray(identity, part.dtype)

    def one(lap, state):
        source = count - 1 - lap if reverse else lap
        return combine(state, lax.dynamic_index_in_dim(gathered, source, 0, False))

    return lax.fori_loop(0, ahead, one, state)


def add_states(first_part, second_part):
    return first_part + second_part


def split_state(state):
    state_high = state.astype(jnp.bfloat16)
    state_low = (state - state_high.astype(jnp.float32)).astype(jnp.bfloat16)
    return (state_high, state_low)


def per_device(queries, keys, values, out_grad, gain):
    feature_width = queries.shape[2]
    head_size = HEAD
    head_count = feature_width // head_size
    block_size = GROUP

    def to_blocks(array):
        return array.reshape(-1, block_size, head_count, head_size)

    query_rows = to_blocks(queries)
    key_rows = to_blocks(keys)
    value_rows = to_blocks(values)
    grad_rows = to_blocks(out_grad)
    row_index = lax.broadcasted_iota(jnp.int32, (block_size, block_size), 0)
    col_index = lax.broadcasted_iota(jnp.int32, (block_size, block_size), 1)
    causal = (row_index >= col_index).astype(jnp.float32)
    gain_rows = gain.reshape(head_count, head_size)
    key_value = jnp.einsum(
        "nshe,nshf->nhef", key_rows, value_rows, preferred_element_type=jnp.float32
    )
    device_sum = jnp.sum(key_value, axis=0)
    empty_state = jnp.zeros_like(device_sum)
    incoming = prefix(device_sum, "seq", add_states, empty_state, False)
    states = incoming[None] + (jnp.cumsum(key_value, axis=0) - key_value)
    states_high, states_low = split_state(states)
    scores = (
        jnp.einsum("nthe,nshe->nhts", query_rows, key_rows, preferred_element_type=jnp.float32)
        * causal
    )
    weights = scores.astype(jnp.bfloat16)
    attended = jnp.einsum(
        "nhts,nshe->nthe", weights, value_rows, preferred_element_type=jnp.float32
    )
    attended = attended + jnp.einsum(
        "nthe,nhef->nthf", query_rows, states_high, preferred_element_type=jnp.float32
    )
    attended = attended + jnp.einsum(
        "nthe,nhef->nthf", query_rows, states_low, preferred_element_type=jnp.float32
    )
    mean_square = jnp.mean(attended * attended, axis=-1, keepdims=True)
    inv_rms = lax.rsqrt(mean_square + 1e-05)
    normed = attended * inv_rms
    normed_out = (normed * gain_rows).astype(jnp.bfloat16)
    grad_wide = grad_rows.astype(jnp.float32)
    grad_normed = grad_wide * gain_rows
    grad_out = inv_rms * (
        grad_normed - normed * jnp.mean(grad_normed * normed, axis=-1, keepdims=True)
    )
    grad_half = grad_out.astype(jnp.bfloat16)
    gain_part = jnp.sum(normed * grad_wide, axis=(0, 1)).reshape(feature_width)
    total_tokens = queries.shape[0] * queries.shape[1] * lax.axis_size("seq") * lax.axis_size("dp")
    gain_grad = lax.psum(gain_part, ("seq", "dp")) / math.sqrt(total_tokens)
    mixed = (
        jnp.einsum("nthe,nshe->nhts", grad_half, value_rows, preferred_element_type=jnp.float32)
        * causal
    )
    mixed_half = mixed.astype(jnp.bfloat16)
    grad_query = jnp.einsum(
        "nhts,nshe->nthe", mixed_half, key_rows, preferred_element_type=jnp.float32
    )
    grad_query = grad_query + jnp.einsum(
        "nthf,nhef->nthe", grad_half, states_high, preferred_element_type=jnp.float32
    )
    grad_query = grad_query + jnp.einsum(
        "nthf,nhef->nthe", grad_half, states_low, preferred_element_type=jnp.float32
    )
    outer = jnp.einsum("nthe,nthf->nhef", query_rows, grad_half, preferred_element_type=jnp.float32)
    outer_sum = jnp.sum(outer, axis=0)
    arriving = prefix(outer_sum, "seq", add_states, empty_state, True)
    later_sum = arriving[None] + (outer_sum[None] - jnp.cumsum(outer, axis=0))
    later_high, later_low = split_state(later_sum)
    grad_key = jnp.einsum(
        "nhts,nthe->nshe", mixed_half, query_rows, preferred_element_type=jnp.float32
    )
    grad_key = grad_key + jnp.einsum(
        "nshf,nhef->nshe", value_rows, later_high, preferred_element_type=jnp.float32
    )
    grad_key = grad_key + jnp.einsum(
        "nshf,nhef->nshe", value_rows, later_low, preferred_element_type=jnp.float32
    )
    grad_value = jnp.einsum(
        "nhts,nthf->nshf", weights, grad_half, preferred_element_type=jnp.float32
    )
    grad_value = grad_value + jnp.einsum(
        "nshe,nhef->nshf", key_rows, later_high, preferred_element_type=jnp.float32
    )
    grad_value = grad_value + jnp.einsum(
        "nshe,nhef->nshf", key_rows, later_low, preferred_element_type=jnp.float32
    )
    shape_out = queries.shape
    return (
        normed_out.reshape(shape_out),
        grad_query.astype(jnp.bfloat16).reshape(shape_out),
        grad_key.astype(jnp.bfloat16).reshape(shape_out),
        grad_value.astype(jnp.bfloat16).reshape(shape_out),
        gain_grad,
    )


def dot(a, b, a_dim=1, b_dim=0):
    return lax.dot_general(a, b, (((a_dim,), (b_dim,)), ((), ())), preferred_element_type=F32)


def flip(index, bit):
    return index + bit * (1 - 2 * lax.rem(lax.div(index, bit), 2))


def kernel(
    pairs, hops, scale,
    q_hbm, k_hbm, v_hbm, g_hbm, gain_hbm,
    out_hbm, dq_hbm, dk_hbm, dv_hbm, gg_hbm,
    f_own, f_src, f_in, fz_in, fz_out, f_give, f_take,
    b_own, b_src, b_in, bz_in, bz_out, b_give, b_take,
    w_all, hi_all, lo_all, go_all, inner_all, dk_all, dv_all, gain_sum, gain_in,
    q_ref, k_ref, v_ref, g_ref, gain_ref,
    out_ref, dq_ref, dk_ref, dv_ref, gg_ref,
    send, recv, chain_send, chain_recv, gain_send, gain_recv, load_sem, store_sem,
):
    half = f_own.shape[0]
    stages = len(hops)
    place = lax.axis_index("seq")
    side = lax.rem(place, 2)
    pair = lax.div(place, 2)
    has_before = pair > 0
    has_after = pair < pairs - 1
    partner = {"seq": flip(place, 1)}
    before = {"seq": place - 2}
    after = {"seq": place + 2}
    def needed(sender, at_end):
        return jnp.logical_not((side == sender) & jnp.logical_not(at_end))

    fx_send, fx_wait = needed(1, has_after), needed(0, has_after)
    fg_send, fg_wait = needed(1, has_before), needed(0, has_before)
    bx_send, bx_wait = needed(0, has_before), needed(1, has_before)
    bg_send, bg_wait = needed(0, has_after), needed(1, has_after)
    own_first = side * half
    other_first = (1 - side) * half

    loads = [
        pltpu.make_async_copy(src, dst, load_sem.at[i])
        for i, (src, dst) in enumerate((
            (k_hbm, k_ref), (v_hbm, v_ref), (q_hbm, q_ref), (g_hbm, g_ref), (gain_hbm, gain_ref),
        ))
    ]
    for load in loads:
        load.start()

    stores = [
        pltpu.make_async_copy(src, dst, store_sem.at[i])
        for i, (src, dst) in enumerate((
            (out_ref, out_hbm), (dq_ref, dq_hbm), (dk_ref, dk_hbm), (dv_ref, dv_hbm),
            (gg_ref, gg_hbm),
        ))
    ]

    def greet(device):
        pl.semaphore_signal(barrier, inc=1, device_id=device, device_id_type=MESH)

    def hop_device(axis, bit):
        return {axis: flip(lax.axis_index(axis), bit)}

    barrier = pltpu.get_barrier_semaphore()
    peers = [hop for hop in hops if hop != ("seq", 2)]
    for axis, bit in peers:
        greet(hop_device(axis, bit))

    @pl.when(has_before)
    def _():
        greet(before)

    @pl.when(has_after)
    def _():
        greet(after)

    def move(kind, src, dst, c, device):
        return pltpu.make_async_remote_copy(
            src_ref=src.at[c], dst_ref=dst.at[c],
            send_sem=send.at[kind, c], recv_sem=recv.at[kind, c],
            device_id=device, device_id_type=MESH,
        )

    def fx(c):
        return move(0, f_src, f_in, c, partner)

    def chain_rows(p):
        return pl.ds(p * (HEAD // PARTS), HEAD // PARTS)

    def chain_move(kind, src, dst, c, p, device):
        return pltpu.make_async_remote_copy(
            src_ref=src.at[c, chain_rows(p)], dst_ref=dst.at[c, chain_rows(p)],
            send_sem=chain_send.at[kind, c, p], recv_sem=chain_recv.at[kind, c, p],
            device_id=device, device_id_type=MESH,
        )

    def fz(c, p, device):
        return chain_move(0, fz_out, fz_in, c, p, device)

    def fg(c):
        return move(1, f_give, f_take, c, partner)

    def bx(c):
        return move(2, b_src, b_in, c, partner)

    def bz(c, p, device):
        return chain_move(1, bz_out, bz_in, c, p, device)

    def bg(c):
        return move(3, b_give, b_take, c, partner)

    def gain_move(s):
        axis, bit = hops[s]
        return pltpu.make_async_remote_copy(
            src_ref=gain_sum.at[s], dst_ref=gain_in.at[s],
            send_sem=gain_send.at[s], recv_sem=gain_recv.at[s],
            device_id=hop_device(axis, bit), device_id_type=MESH,
        )

    def cols(h):
        return pl.ds(pl.multiple_of(h * HEAD, HEAD), HEAD)

    row = lax.broadcasted_iota(jnp.int32, (GROUP, GROUP), 0)
    col = lax.broadcasted_iota(jnp.int32, (GROUP, GROUP), 1)
    causal = row >= col

    def key_value(h):
        return dot(k_ref[:, cols(h)], v_ref[:, cols(h)], 0, 0)

    def local_forward(h):
        w = jnp.where(causal, dot(q_ref[:, cols(h)], k_ref[:, cols(h)], 1, 1), 0.0).astype(BF16)
        return w, dot(w, v_ref[:, cols(h)])

    def forward(h, state):
        q = q_ref[:, cols(h)]
        hi, lo = split_state(state)
        attended = inner_all[h] + dot(
            jnp.concatenate([q, q], axis=1), jnp.concatenate([hi, lo], axis=0)
        )
        inv = lax.rsqrt(jnp.mean(attended * attended, axis=1, keepdims=True) + 1e-05)
        normed = attended * inv
        gain = gain_ref[pl.ds(h, 1), :]
        wide = g_ref[:, cols(h)].astype(F32)
        grad_normed = wide * gain
        go = inv * (
            grad_normed - normed * jnp.mean(grad_normed * normed, axis=1, keepdims=True)
        )
        go = go.astype(BF16)
        normed_out = (normed * gain).astype(BF16)
        gain_part = jnp.sum(normed * wide, axis=0, keepdims=True)
        return dot(q, go, 0, 0), hi, lo, go, normed_out, gain_part

    def keep_forward(h, results):
        outer, hi, lo, go, normed_out, gain_part = results
        hi_all[h] = hi
        lo_all[h] = lo
        go_all[h] = go
        out_ref[:, cols(h)] = normed_out
        gain_sum[0, pl.ds(h, 1), :] = gain_part

    def local_backward(h):
        go = go_all[h]
        mixed = jnp.where(causal, dot(go, v_ref[:, cols(h)], 1, 1), 0.0).astype(BF16)
        dq = dot(mixed, k_ref[:, cols(h)]) + dot(
            jnp.concatenate([go, go], axis=1),
            jnp.concatenate([hi_all[h], lo_all[h]], axis=1), 1, 1,
        )
        return dq.astype(BF16), dot(mixed, q_ref[:, cols(h)], 0, 0), dot(w_all[h], go, 0, 0)

    def keep_local_backward(h, results):
        dq_ref[:, cols(h)], dk_all[h], dv_all[h] = results

    def backward(h, later):
        hi, lo = split_state(later)
        v = v_ref[:, cols(h)]
        k = k_ref[:, cols(h)]
        dk = dk_all[h] + dot(
            jnp.concatenate([v, v], axis=1), jnp.concatenate([hi, lo], axis=1), 1, 1
        )
        dv = dv_all[h] + dot(
            jnp.concatenate([k, k], axis=1), jnp.concatenate([hi, lo], axis=0)
        )
        return dk.astype(BF16), dv.astype(BF16)

    def keep_backward(h, results):
        dk_ref[:, cols(h)], dv_ref[:, cols(h)] = results

    def clear(ref, condition):
        @pl.when(condition)
        def _():
            ref[...] = jnp.zeros_like(ref)

    clear(fz_in, jnp.logical_not(has_before))
    clear(bz_in, jnp.logical_not(has_after))
    clear(f_take, jnp.logical_not(fg_wait))
    clear(b_take, jnp.logical_not(bg_wait))

    loads[0].wait()
    loads[1].wait()
    f_src[0] = key_value(other_first)
    ends = has_before.astype(jnp.int32) + has_after.astype(jnp.int32)
    pl.semaphore_wait(barrier, len(peers) + ends)

    def start_if(condition, copy):
        @pl.when(condition)
        def _():
            copy.start()

    def recv_if(condition, copy):
        @pl.when(condition)
        def _():
            copy.wait_recv()

    def sent_if(condition, copy):
        @pl.when(condition)
        def _():
            copy.wait_send()

    ahead = jnp.minimum(half, AHEAD_FIRST + AHEAD_HOP * pair)
    start_if(fx_send, fx(0))
    for c in range(1, half):
        f_src[c] = key_value(other_first + c)
        start_if(fx_send & (c < ahead), fx(c))
    for c in range(half):
        f_own[c] = key_value(own_first + c)
    for load in loads[2:]:
        load.wait()

    lag = LAG_FIRST + LAG_HOP * (pairs - 1 - pair)
    late = 2 * pair >= pairs
    forward_end = half + FORWARD_LAG
    local_lag = jnp.where(late, forward_end, FORWARD_LAG + 1)
    give_lag = jnp.maximum(lag, forward_end)
    final_lag = give_lag + FINAL_LAG
    most = max(LAG_FIRST + LAG_HOP * (pairs - 1), forward_end) + FINAL_LAG
    steps = max(half + most, forward_end + stages)

    def local_step(c):
        mine = local_forward(own_first + c)
        theirs = local_forward(other_first + c)
        w_all[own_first + c], inner_all[own_first + c] = mine
        w_all[other_first + c], inner_all[other_first + c] = theirs

    @pl.when(late)
    def _():
        lax.fori_loop(0, half, lambda c, carry: (local_step(c), carry)[1], 0)

    def step(t, carry):
        @pl.when(t < half)
        def _():
            recv_if(fx_wait, fx(t))
            for p in range(PARTS):
                rows = chain_rows(p)
                recv_if(has_before, fz(t, p, partner))
                fz_out[t, rows] = fz_in[t, rows] + (f_own[t, rows] + f_in[t, rows])
                start_if(has_after, fz(t, p, after))
            past, mine, theirs = fz_in[t], f_own[t], f_in[t]
            f_give[t] = past + jnp.where(side == 0, mine, 0.0)
            start_if(fg_send, fg(t))
            start_if(fx_send & (t < half - ahead), fx(jnp.minimum(t + ahead, half - 1)))
            f_own[t] = past + jnp.where(side == 1, theirs, 0.0)

        @pl.when((t >= FORWARD_LAG) & (t < half + FORWARD_LAG))
        def _():
            c = t - FORWARD_LAG
            recv_if(fg_wait, fg(c))
            theirs = forward(other_first + c, f_take[c])
            mine = forward(own_first + c, f_own[c])
            b_src[c] = theirs[0]
            start_if(bx_send, bx(c))
            b_own[c] = mine[0]
            keep_forward(other_first + c, theirs)
            keep_forward(own_first + c, mine)

        j = t - lag

        @pl.when((j >= 0) & (j < half))
        def _():
            recv_if(bx_wait, bx(j))
            for p in range(PARTS):
                rows = chain_rows(p)
                recv_if(has_after, bz(j, p, partner))
                bz_out[j, rows] = bz_in[j, rows] + (b_own[j, rows] + b_in[j, rows])
                start_if(has_before, bz(j, p, before))
            past, mine, theirs = bz_in[j], b_own[j], b_in[j]
            b_give[j] = past + jnp.where(side == 1, mine, 0.0)
            b_own[j] = past + jnp.where(side == 0, theirs, 0.0)

        u = t - give_lag

        @pl.when((u >= 0) & (u < half))
        def _():
            start_if(bg_send, bg(u))

        @pl.when((t < half) & jnp.logical_not(late))
        def _():
            local_step(t)

        b = t - local_lag

        @pl.when((b >= 0) & (b < half))
        def _():
            mine = local_backward(own_first + b)
            theirs = local_backward(other_first + b)
            keep_local_backward(own_first + b, mine)
            keep_local_backward(other_first + b, theirs)

            @pl.when(b == half - 1)
            def _():
                stores[1].start()

        e = t - final_lag

        @pl.when((e >= 0) & (e < half))
        def _():
            recv_if(bg_wait, bg(e))
            mine = backward(own_first + e, b_own[e])
            theirs = backward(other_first + e, b_take[e])
            keep_backward(own_first + e, mine)
            keep_backward(other_first + e, theirs)

        for s in range(stages + 1):

            @pl.when(t == forward_end - 1 + s)
            def _(s=s):
                if s > 0:
                    gain_move(s - 1).wait_recv()
                    gain_sum[s] = gain_sum[s - 1] + gain_in[s - 1]
                if s < stages:
                    gain_move(s).start()
                else:
                    gg_ref[...] = gain_sum[s] / scale
                    stores[4].start()
                if s == 0:
                    stores[0].start()

        return carry

    lax.fori_loop(0, steps, step, 0)
    for store in stores[2:4]:
        store.start()

    def finish(c, carry):
        sent_if(fx_send, fx(c))
        sent_if(fg_send, fg(c))
        sent_if(bx_send, bx(c))
        sent_if(bg_send, bg(c))
        for p in range(PARTS):
            sent_if(has_after, fz(c, p, after))
            sent_if(has_before, bz(c, p, before))
        return carry

    lax.fori_loop(0, half, finish, 0)
    for s in range(stages):
        gain_move(s).wait_send()
    for store in stores:
        store.wait()


def flush(*refs):
    source, target, held = refs[:5], refs[5:10], refs[10:15]
    sems = refs[15]
    reads = [pltpu.make_async_copy(source[i], held[i], sems.at[0, i]) for i in range(5)]
    writes = [pltpu.make_async_copy(held[i], target[i], sems.at[1, i]) for i in range(5)]
    for read in reads:
        read.start()
    for read, write in zip(reads, writes):
        read.wait()
        write.start()
    for write in writes:
        write.wait()


def fused(queries, keys, values, out_grad, gain):
    shape = queries.shape
    rows, width = shape[1], shape[2]
    heads = width // HEAD
    half = heads // 2
    count = lax.axis_size("seq")
    spread = lax.axis_size("dp")
    hops = []
    for axis, size in (("seq", count), ("dp", spread)):
        bit = 1
        while bit < size:
            hops.append((axis, bit))
            bit *= 2
    stages = len(hops)
    scale = math.sqrt(shape[0] * rows * count * spread)
    flat = [a.reshape(rows, width) for a in (queries, keys, values, out_grad)]
    state = pltpu.VMEM((half, HEAD, HEAD), F32)
    held = pltpu.VMEM((heads, HEAD, HEAD), BF16)
    wide = pltpu.VMEM((heads, HEAD, HEAD), F32)
    block = pltpu.VMEM((rows, width), BF16)
    anywhere = pl.BlockSpec(memory_space=pl.ANY)
    result = pl.pallas_call(
        functools.partial(kernel, count // 2, tuple(hops), scale),
        out_shape=[jax.ShapeDtypeStruct((rows, width), BF16)] * 4
        + [jax.ShapeDtypeStruct((heads, HEAD), F32)],
        in_specs=[anywhere] * 5,
        out_specs=[anywhere] * 5,
        scratch_shapes=[state] * 14
        + [held] * 4
        + [wide] * 3
        + [
            pltpu.VMEM((stages + 1, heads, HEAD), F32),
            pltpu.VMEM((stages, heads, HEAD), F32),
            block, block, block, block,
            pltpu.VMEM((heads, HEAD), F32),
            block, block, block, block,
            pltpu.VMEM((heads, HEAD), F32),
            pltpu.SemaphoreType.DMA((4, half)),
            pltpu.SemaphoreType.DMA((4, half)),
            pltpu.SemaphoreType.DMA((2, half, PARTS)),
            pltpu.SemaphoreType.DMA((2, half, PARTS)),
            pltpu.SemaphoreType.DMA((stages,)),
            pltpu.SemaphoreType.DMA((stages,)),
            pltpu.SemaphoreType.DMA((5,)),
            pltpu.SemaphoreType.DMA((5,)),
        ],
        compiler_params=pltpu.CompilerParams(
            collective_id=0, has_side_effects=True, vmem_limit_bytes=VMEM_LIMIT
        ),
    )(*flat, gain.reshape(heads, HEAD))
    result = pl.pallas_call(
        flush,
        out_shape=[jax.ShapeDtypeStruct(a.shape, a.dtype) for a in result],
        in_specs=[anywhere] * 5,
        out_specs=[anywhere] * 5,
        scratch_shapes=[pltpu.VMEM(a.shape, a.dtype) for a in result]
        + [pltpu.SemaphoreType.DMA((2, 5))],
        compiler_params=pltpu.CompilerParams(vmem_limit_bytes=VMEM_LIMIT),
    )(*result)
    return tuple(a.reshape(shape) for a in result[:4]) + (result[4].reshape(width),)


def fits(queries):
    def power_of_two(size):
        return size & (size - 1) == 0

    heads = queries.shape[2] // HEAD
    return (
        queries.shape[:2] == (1, GROUP)
        and heads % 2 == 0
        and lax.axis_size("seq") >= 2
        and power_of_two(lax.axis_size("seq"))
        and power_of_two(lax.axis_size("dp"))
    )


def on_device(queries, keys, values, out_grad, gain):
    run = fused if fits(queries) else per_device
    return run(queries, keys, values, out_grad, gain)


def solution(mesh):
    in_specs = (
        P("dp", "seq", None),
        P("dp", "seq", None),
        P("dp", "seq", None),
        P("dp", "seq", None),
        P(),
    )
    out_specs = (
        P("dp", "seq", None),
        P("dp", "seq", None),
        P("dp", "seq", None),
        P("dp", "seq", None),
        P(),
    )
    return jax.shard_map(
        on_device, mesh=mesh, in_specs=in_specs, out_specs=out_specs, check_vma=False
    )
```

```python
import functools
import math

import jax
import jax.numpy as jnp
from jax import lax
from jax.experimental import pallas as pl
from jax.experimental.pallas import tpu as pltpu
from jax.sharding import PartitionSpec as P

HEAD = 128
GROUP = 128
PARTS = 2
FORWARD_LAG = 3
LAG_FIRST = 5
LAG_HOP = 2
FINAL_LAG = 3
AHEAD_FIRST = 2
AHEAD_HOP = 2
VMEM_LIMIT = 56 * 1024 * 1024
MESH = pl.DeviceIdType.MESH
F32 = jnp.float32
BF16 = jnp.bfloat16


def prefix(part, axis, combine, identity, reverse):
    count = lax.axis_size(axis)
    place = lax.axis_index(axis)
    ahead = count - 1 - place if reverse else place
    gathered = lax.all_gather(part, axis)
    state = jnp.zeros_like(part) + jnp.asarray(identity, part.dtype)

    def one(lap, state):
        source = count - 1 - lap if reverse else lap
        return combine(state, lax.dynamic_index_in_dim(gathered, source, 0, False))

    return lax.fori_loop(0, ahead, one, state)


def add_states(first_part, second_part):
    return first_part + second_part


def split_state(state):
    state_high = state.astype(jnp.bfloat16)
    state_low = (state - state_high.astype(jnp.float32)).astype(jnp.bfloat16)
    return (state_high, state_low)


def per_device(queries, keys, values, out_grad, gain):
    feature_width = queries.shape[2]
    head_size = HEAD
    head_count = feature_width // head_size
    block_size = GROUP

    def to_blocks(array):
        return array.reshape(-1, block_size, head_count, head_size)

    query_rows = to_blocks(queries)
    key_rows = to_blocks(keys)
    value_rows = to_blocks(values)
    grad_rows = to_blocks(out_grad)
    row_index = lax.broadcasted_iota(jnp.int32, (block_size, block_size), 0)
    col_index = lax.broadcasted_iota(jnp.int32, (block_size, block_size), 1)
    causal = (row_index >= col_index).astype(jnp.float32)
    gain_rows = gain.reshape(head_count, head_size)
    key_value = jnp.einsum(
        "nshe,nshf->nhef", key_rows, value_rows, preferred_element_type=jnp.float32
    )
    device_sum = jnp.sum(key_value, axis=0)
    empty_state = jnp.zeros_like(device_sum)
    incoming = prefix(device_sum, "seq", add_states, empty_state, False)
    states = incoming[None] + (jnp.cumsum(key_value, axis=0) - key_value)
    states_high, states_low = split_state(states)
    scores = (
        jnp.einsum("nthe,nshe->nhts", query_rows, key_rows, preferred_element_type=jnp.float32)
        * causal
    )
    weights = scores.astype(jnp.bfloat16)
    attended = jnp.einsum(
        "nhts,nshe->nthe", weights, value_rows, preferred_element_type=jnp.float32
    )
    attended = attended + jnp.einsum(
        "nthe,nhef->nthf", query_rows, states_high, preferred_element_type=jnp.float32
    )
    attended = attended + jnp.einsum(
        "nthe,nhef->nthf", query_rows, states_low, preferred_element_type=jnp.float32
    )
    mean_square = jnp.mean(attended * attended, axis=-1, keepdims=True)
    inv_rms = lax.rsqrt(mean_square + 1e-05)
    normed = attended * inv_rms
    normed_out = (normed * gain_rows).astype(jnp.bfloat16)
    grad_wide = grad_rows.astype(jnp.float32)
    grad_normed = grad_wide * gain_rows
    grad_out = inv_rms * (
        grad_normed - normed * jnp.mean(grad_normed * normed, axis=-1, keepdims=True)
    )
    grad_half = grad_out.astype(jnp.bfloat16)
    gain_part = jnp.sum(normed * grad_wide, axis=(0, 1)).reshape(feature_width)
    total_tokens = queries.shape[0] * queries.shape[1] * lax.axis_size("seq") * lax.axis_size("dp")
    gain_grad = lax.psum(gain_part, ("seq", "dp")) / math.sqrt(total_tokens)
    mixed = (
        jnp.einsum("nthe,nshe->nhts", grad_half, value_rows, preferred_element_type=jnp.float32)
        * causal
    )
    mixed_half = mixed.astype(jnp.bfloat16)
    grad_query = jnp.einsum(
        "nhts,nshe->nthe", mixed_half, key_rows, preferred_element_type=jnp.float32
    )
    grad_query = grad_query + jnp.einsum(
        "nthf,nhef->nthe", grad_half, states_high, preferred_element_type=jnp.float32
    )
    grad_query = grad_query + jnp.einsum(
        "nthf,nhef->nthe", grad_half, states_low, preferred_element_type=jnp.float32
    )
    outer = jnp.einsum("nthe,nthf->nhef", query_rows, grad_half, preferred_element_type=jnp.float32)
    outer_sum = jnp.sum(outer, axis=0)
    arriving = prefix(outer_sum, "seq", add_states, empty_state, True)
    later_sum = arriving[None] + (outer_sum[None] - jnp.cumsum(outer, axis=0))
    later_high, later_low = split_state(later_sum)
    grad_key = jnp.einsum(
        "nhts,nthe->nshe", mixed_half, query_rows, preferred_element_type=jnp.float32
    )
    grad_key = grad_key + jnp.einsum(
        "nshf,nhef->nshe", value_rows, later_high, preferred_element_type=jnp.float32
    )
    grad_key = grad_key + jnp.einsum(
        "nshf,nhef->nshe", value_rows, later_low, preferred_element_type=jnp.float32
    )
    grad_value = jnp.einsum(
        "nhts,nthf->nshf", weights, grad_half, preferred_element_type=jnp.float32
    )
    grad_value = grad_value + jnp.einsum(
        "nshe,nhef->nshf", key_rows, later_high, preferred_element_type=jnp.float32
    )
    grad_value = grad_value + jnp.einsum(
        "nshe,nhef->nshf", key_rows, later_low, preferred_element_type=jnp.float32
    )
    shape_out = queries.shape
    return (
        normed_out.reshape(shape_out),
        grad_query.astype(jnp.bfloat16).reshape(shape_out),
        grad_key.astype(jnp.bfloat16).reshape(shape_out),
        grad_value.astype(jnp.bfloat16).reshape(shape_out),
        gain_grad,
    )


def dot(a, b, a_dim=1, b_dim=0):
    return lax.dot_general(a, b, (((a_dim,), (b_dim,)), ((), ())), preferred_element_type=F32)


def flip(index, bit):
    return index + bit * (1 - 2 * lax.rem(lax.div(index, bit), 2))


def kernel(
    pairs, hops, scale,
    q_hbm, k_hbm, v_hbm, g_hbm, gain_hbm,
    out_hbm, dq_hbm, dk_hbm, dv_hbm, gg_hbm,
    f_own, f_src, f_in, fz_in, fz_out, f_give, f_take,
    b_own, b_src, b_in, bz_in, bz_out, b_give, b_take,
    w_all, hi_all, lo_all, go_all, inner_all, dk_all, dv_all, gain_sum, gain_in,
    q_ref, k_ref, v_ref, g_ref, gain_ref,
    out_ref, dq_ref, dk_ref, dv_ref, gg_ref,
    send, recv, chain_send, chain_recv, gain_send, gain_recv, load_sem, store_sem,
):
    half = f_own.shape[0]
    stages = len(hops)
    place = lax.axis_index("seq")
    side = lax.rem(place, 2)
    pair = lax.div(place, 2)
    has_before = pair > 0
    has_after = pair < pairs - 1
    partner = {"seq": flip(place, 1)}
    before = {"seq": place - 2}
    after = {"seq": place + 2}
    def needed(sender, at_end):
        return jnp.logical_not((side == sender) & jnp.logical_not(at_end))

    fx_send, fx_wait = needed(1, has_after), needed(0, has_after)
    fg_send, fg_wait = needed(1, has_before), needed(0, has_before)
    bx_send, bx_wait = needed(0, has_before), needed(1, has_before)
    bg_send, bg_wait = needed(0, has_after), needed(1, has_after)
    own_first = side * half
    other_first = (1 - side) * half

    loads = [
        pltpu.make_async_copy(src, dst, load_sem.at[i])
        for i, (src, dst) in enumerate((
            (k_hbm, k_ref), (v_hbm, v_ref), (q_hbm, q_ref), (g_hbm, g_ref), (gain_hbm, gain_ref),
        ))
    ]
    for load in loads[:2]:
        load.start()

    stores = [
        pltpu.make_async_copy(src, dst, store_sem.at[i])
        for i, (src, dst) in enumerate((
            (out_ref, out_hbm), (dq_ref, dq_hbm), (dk_ref, dk_hbm), (dv_ref, dv_hbm),
            (gg_ref, gg_hbm),
        ))
    ]

    def greet(device):
        pl.semaphore_signal(barrier, inc=1, device_id=device, device_id_type=MESH)

    def hop_device(axis, bit):
        return {axis: flip(lax.axis_index(axis), bit)}

    barrier = pltpu.get_barrier_semaphore()
    peers = [hop for hop in hops if hop != ("seq", 2)]
    for axis, bit in peers:
        greet(hop_device(axis, bit))

    @pl.when(has_before)
    def _():
        greet(before)

    @pl.when(has_after)
    def _():
        greet(after)

    def move(kind, src, dst, c, device):
        return pltpu.make_async_remote_copy(
            src_ref=src.at[c], dst_ref=dst.at[c],
            send_sem=send.at[kind, c], recv_sem=recv.at[kind, c],
            device_id=device, device_id_type=MESH,
        )

    def fx(c):
        return move(0, f_src, f_in, c, partner)

    def chain_rows(p):
        return pl.ds(p * (HEAD // PARTS), HEAD // PARTS)

    def chain_move(kind, src, dst, c, p, device):
        return pltpu.make_async_remote_copy(
            src_ref=src.at[c, chain_rows(p)], dst_ref=dst.at[c, chain_rows(p)],
            send_sem=chain_send.at[kind, c, p], recv_sem=chain_recv.at[kind, c, p],
            device_id=device, device_id_type=MESH,
        )

    def fz(c, p, device):
        return chain_move(0, fz_out, fz_in, c, p, device)

    def fg(c):
        return move(1, f_give, f_take, c, partner)

    def bx(c):
        return move(2, b_src, b_in, c, partner)

    def bz(c, p, device):
        return chain_move(1, bz_out, bz_in, c, p, device)

    def bg(c):
        return move(3, b_give, b_take, c, partner)

    def gain_move(s):
        axis, bit = hops[s]
        return pltpu.make_async_remote_copy(
            src_ref=gain_sum.at[s], dst_ref=gain_in.at[s],
            send_sem=gain_send.at[s], recv_sem=gain_recv.at[s],
            device_id=hop_device(axis, bit), device_id_type=MESH,
        )

    def cols(h):
        return pl.ds(pl.multiple_of(h * HEAD, HEAD), HEAD)

    row = lax.broadcasted_iota(jnp.int32, (GROUP, GROUP), 0)
    col = lax.broadcasted_iota(jnp.int32, (GROUP, GROUP), 1)
    causal = row >= col

    def key_value(h):
        return dot(k_ref[:, cols(h)], v_ref[:, cols(h)], 0, 0)

    def local_forward(h):
        w = jnp.where(causal, dot(q_ref[:, cols(h)], k_ref[:, cols(h)], 1, 1), 0.0).astype(BF16)
        return w, dot(w, v_ref[:, cols(h)])

    def forward(h, state):
        q = q_ref[:, cols(h)]
        hi, lo = split_state(state)
        attended = inner_all[h] + dot(
            jnp.concatenate([q, q], axis=1), jnp.concatenate([hi, lo], axis=0)
        )
        inv = lax.rsqrt(jnp.mean(attended * attended, axis=1, keepdims=True) + 1e-05)
        normed = attended * inv
        gain = gain_ref[pl.ds(h, 1), :]
        wide = g_ref[:, cols(h)].astype(F32)
        grad_normed = wide * gain
        go = inv * (
            grad_normed - normed * jnp.mean(grad_normed * normed, axis=1, keepdims=True)
        )
        go = go.astype(BF16)
        normed_out = (normed * gain).astype(BF16)
        gain_part = jnp.sum(normed * wide, axis=0, keepdims=True)
        return dot(q, go, 0, 0), hi, lo, go, normed_out, gain_part

    def keep_forward(h, results):
        outer, hi, lo, go, normed_out, gain_part = results
        hi_all[h] = hi
        lo_all[h] = lo
        go_all[h] = go
        out_ref[:, cols(h)] = normed_out
        gain_sum[0, pl.ds(h, 1), :] = gain_part

    def local_backward(h):
        go = go_all[h]
        mixed = jnp.where(causal, dot(go, v_ref[:, cols(h)], 1, 1), 0.0).astype(BF16)
        dq = dot(mixed, k_ref[:, cols(h)]) + dot(
            jnp.concatenate([go, go], axis=1),
            jnp.concatenate([hi_all[h], lo_all[h]], axis=1), 1, 1,
        )
        return dq.astype(BF16), dot(mixed, q_ref[:, cols(h)], 0, 0), dot(w_all[h], go, 0, 0)

    def keep_local_backward(h, results):
        dq_ref[:, cols(h)], dk_all[h], dv_all[h] = results

    def backward(h, later):
        hi, lo = split_state(later)
        v = v_ref[:, cols(h)]
        k = k_ref[:, cols(h)]
        dk = dk_all[h] + dot(
            jnp.concatenate([v, v], axis=1), jnp.concatenate([hi, lo], axis=1), 1, 1
        )
        dv = dv_all[h] + dot(
            jnp.concatenate([k, k], axis=1), jnp.concatenate([hi, lo], axis=0)
        )
        return dk.astype(BF16), dv.astype(BF16)

    def keep_backward(h, results):
        dk_ref[:, cols(h)], dv_ref[:, cols(h)] = results

    def clear(ref, condition):
        @pl.when(condition)
        def _():
            ref[...] = jnp.zeros_like(ref)

    clear(fz_in, jnp.logical_not(has_before))
    clear(bz_in, jnp.logical_not(has_after))
    clear(f_take, jnp.logical_not(fg_wait))
    clear(b_take, jnp.logical_not(bg_wait))

    for load in loads[:2]:
        load.wait()
    for load in loads[2:]:
        load.start()
    f_src[0] = key_value(other_first)
    ends = has_before.astype(jnp.int32) + has_after.astype(jnp.int32)
    pl.semaphore_wait(barrier, len(peers) + ends)

    def start_if(condition, copy):
        @pl.when(condition)
        def _():
            copy.start()

    def recv_if(condition, copy):
        @pl.when(condition)
        def _():
            copy.wait_recv()

    def sent_if(condition, copy):
        @pl.when(condition)
        def _():
            copy.wait_send()

    ahead = jnp.minimum(half, AHEAD_FIRST + AHEAD_HOP * pair)
    start_if(fx_send, fx(0))
    for c in range(1, half):
        f_src[c] = key_value(other_first + c)
        start_if(fx_send & (c < ahead), fx(c))
    for c in range(half):
        f_own[c] = key_value(own_first + c)
    for load in loads[2:]:
        load.wait()

    lag = LAG_FIRST + LAG_HOP * (pairs - 1 - pair)
    late = 2 * pair >= pairs
    forward_end = half + FORWARD_LAG
    local_lag = jnp.where(late, forward_end, FORWARD_LAG + 1)
    give_lag = jnp.maximum(lag, forward_end - 1)
    final_lag = give_lag + FINAL_LAG
    most = max(LAG_FIRST + LAG_HOP * (pairs - 1), forward_end) + FINAL_LAG
    steps = max(half + most, forward_end + stages)

    def local_step(c):
        mine = local_forward(own_first + c)
        theirs = local_forward(other_first + c)
        w_all[own_first + c], inner_all[own_first + c] = mine
        w_all[other_first + c], inner_all[other_first + c] = theirs

    @pl.when(late)
    def _():
        lax.fori_loop(0, half, lambda c, carry: (local_step(c), carry)[1], 0)

    def step(t, carry):
        @pl.when(t < half)
        def _():
            recv_if(fx_wait, fx(t))
            for p in range(PARTS):
                rows = chain_rows(p)
                recv_if(has_before, fz(t, p, partner))
                fz_out[t, rows] = fz_in[t, rows] + (f_own[t, rows] + f_in[t, rows])
                start_if(has_after, fz(t, p, after))
            past, mine, theirs = fz_in[t], f_own[t], f_in[t]
            f_give[t] = past + jnp.where(side == 0, mine, 0.0)
            start_if(fg_send, fg(t))
            start_if(fx_send & (t < half - ahead), fx(jnp.minimum(t + ahead, half - 1)))
            f_own[t] = past + jnp.where(side == 1, theirs, 0.0)

        @pl.when((t >= FORWARD_LAG) & (t < half + FORWARD_LAG))
        def _():
            c = t - FORWARD_LAG
            recv_if(fg_wait, fg(c))
            theirs = forward(other_first + c, f_take[c])
            mine = forward(own_first + c, f_own[c])
            b_src[c] = theirs[0]
            start_if(bx_send, bx(c))
            b_own[c] = mine[0]
            keep_forward(other_first + c, theirs)
            keep_forward(own_first + c, mine)

        j = t - lag
        u = t - give_lag

        @pl.when((u >= 0) & (u < half) & (u < j))
        def _():
            start_if(bg_send, bg(u))

        @pl.when((j >= 0) & (j < half))
        def _():
            recv_if(bx_wait, bx(j))
            for p in range(PARTS):
                rows = chain_rows(p)
                recv_if(has_after, bz(j, p, partner))
                bz_out[j, rows] = bz_in[j, rows] + (b_own[j, rows] + b_in[j, rows])
                start_if(has_before, bz(j, p, before))
            past, mine, theirs = bz_in[j], b_own[j], b_in[j]
            b_give[j] = past + jnp.where(side == 1, mine, 0.0)
            b_own[j] = past + jnp.where(side == 0, theirs, 0.0)

        @pl.when((u >= 0) & (u < half) & (u == j))
        def _():
            start_if(bg_send, bg(u))

        @pl.when((t < half) & jnp.logical_not(late))
        def _():
            local_step(t)

        b = t - local_lag

        @pl.when((b >= 0) & (b < half))
        def _():
            mine = local_backward(own_first + b)
            theirs = local_backward(other_first + b)
            keep_local_backward(own_first + b, mine)
            keep_local_backward(other_first + b, theirs)

            @pl.when(b == half - 1)
            def _():
                stores[1].start()

        e = t - final_lag

        @pl.when((e >= 0) & (e < half))
        def _():
            recv_if(bg_wait, bg(e))
            mine = backward(own_first + e, b_own[e])
            theirs = backward(other_first + e, b_take[e])
            keep_backward(own_first + e, mine)
            keep_backward(other_first + e, theirs)

        for s in range(stages + 1):

            @pl.when(t == forward_end - 1 + s)
            def _(s=s):
                if s > 0:
                    gain_move(s - 1).wait_recv()
                    gain_sum[s] = gain_sum[s - 1] + gain_in[s - 1]
                if s < stages:
                    gain_move(s).start()
                else:
                    gg_ref[...] = gain_sum[s] / scale
                    stores[4].start()
                if s == 0:
                    stores[0].start()

        return carry

    lax.fori_loop(0, steps, step, 0)
    for store in stores[2:4]:
        store.start()

    def finish(c, carry):
        sent_if(fx_send, fx(c))
        sent_if(fg_send, fg(c))
        sent_if(bx_send, bx(c))
        sent_if(bg_send, bg(c))
        for p in range(PARTS):
            sent_if(has_after, fz(c, p, after))
            sent_if(has_before, bz(c, p, before))
        return carry

    lax.fori_loop(0, half, finish, 0)
    for s in range(stages):
        gain_move(s).wait_send()
    for store in stores:
        store.wait()


def flush(*refs):
    source, target, held = refs[:5], refs[5:10], refs[10:15]
    sems = refs[15]
    reads = [pltpu.make_async_copy(source[i], held[i], sems.at[0, i]) for i in range(5)]
    writes = [pltpu.make_async_copy(held[i], target[i], sems.at[1, i]) for i in range(5)]
    for read in reads:
        read.start()
    for read, write in zip(reads, writes):
        read.wait()
        write.start()
    for write in writes:
        write.wait()


def fused(queries, keys, values, out_grad, gain):
    shape = queries.shape
    rows, width = shape[1], shape[2]
    heads = width // HEAD
    half = heads // 2
    count = lax.axis_size("seq")
    spread = lax.axis_size("dp")
    hops = []
    for axis, size in (("seq", count), ("dp", spread)):
        bit = 1
        while bit < size:
            hops.append((axis, bit))
            bit *= 2
    stages = len(hops)
    scale = math.sqrt(shape[0] * rows * count * spread)
    flat = [a.reshape(rows, width) for a in (queries, keys, values, out_grad)]
    state = pltpu.VMEM((half, HEAD, HEAD), F32)
    held = pltpu.VMEM((heads, HEAD, HEAD), BF16)
    wide = pltpu.VMEM((heads, HEAD, HEAD), F32)
    block = pltpu.VMEM((rows, width), BF16)
    anywhere = pl.BlockSpec(memory_space=pl.ANY)
    result = pl.pallas_call(
        functools.partial(kernel, count // 2, tuple(hops), scale),
        out_shape=[jax.ShapeDtypeStruct((rows, width), BF16)] * 4
        + [jax.ShapeDtypeStruct((heads, HEAD), F32)],
        in_specs=[anywhere] * 5,
        out_specs=[anywhere] * 5,
        scratch_shapes=[state] * 14
        + [held] * 4
        + [wide] * 3
        + [
            pltpu.VMEM((stages + 1, heads, HEAD), F32),
            pltpu.VMEM((stages, heads, HEAD), F32),
            block, block, block, block,
            pltpu.VMEM((heads, HEAD), F32),
            block, block, block, block,
            pltpu.VMEM((heads, HEAD), F32),
            pltpu.SemaphoreType.DMA((4, half)),
            pltpu.SemaphoreType.DMA((4, half)),
            pltpu.SemaphoreType.DMA((2, half, PARTS)),
            pltpu.SemaphoreType.DMA((2, half, PARTS)),
            pltpu.SemaphoreType.DMA((stages,)),
            pltpu.SemaphoreType.DMA((stages,)),
            pltpu.SemaphoreType.DMA((5,)),
            pltpu.SemaphoreType.DMA((5,)),
        ],
        compiler_params=pltpu.CompilerParams(
            collective_id=0, has_side_effects=True, vmem_limit_bytes=VMEM_LIMIT
        ),
    )(*flat, gain.reshape(heads, HEAD))
    result = pl.pallas_call(
        flush,
        out_shape=[jax.ShapeDtypeStruct(a.shape, a.dtype) for a in result],
        in_specs=[anywhere] * 5,
        out_specs=[anywhere] * 5,
        scratch_shapes=[pltpu.VMEM(a.shape, a.dtype) for a in result]
        + [pltpu.SemaphoreType.DMA((2, 5))],
        compiler_params=pltpu.CompilerParams(vmem_limit_bytes=VMEM_LIMIT),
    )(*result)
    return tuple(a.reshape(shape) for a in result[:4]) + (result[4].reshape(width),)


def fits(queries):
    def power_of_two(size):
        return size & (size - 1) == 0

    heads = queries.shape[2] // HEAD
    return (
        queries.shape[:2] == (1, GROUP)
        and heads % 2 == 0
        and lax.axis_size("seq") >= 2
        and power_of_two(lax.axis_size("seq"))
        and power_of_two(lax.axis_size("dp"))
    )


def on_device(queries, keys, values, out_grad, gain):
    run = fused if fits(queries) else per_device
    return run(queries, keys, values, out_grad, gain)


def solution(mesh):
    in_specs = (
        P("dp", "seq", None),
        P("dp", "seq", None),
        P("dp", "seq", None),
        P("dp", "seq", None),
        P(),
    )
    out_specs = (
        P("dp", "seq", None),
        P("dp", "seq", None),
        P("dp", "seq", None),
        P("dp", "seq", None),
        P(),
    )
    return jax.shard_map(
        on_device, mesh=mesh, in_specs=in_specs, out_specs=out_specs, check_vma=False
    )
```

```python
import functools
import math

import jax
import jax.numpy as jnp
from jax import lax
from jax.experimental import pallas as pl
from jax.experimental.pallas import tpu as pltpu
from jax.sharding import PartitionSpec as P

HEAD = 128
GROUP = 128
PARTS = 4
FORWARD_LAG = 3
LAG_FIRST = 5
LAG_HOP = 2
FINAL_LAG = 3
AHEAD_FIRST = 2
AHEAD_HOP = 2
VMEM_LIMIT = 56 * 1024 * 1024
MESH = pl.DeviceIdType.MESH
F32 = jnp.float32
BF16 = jnp.bfloat16


def prefix(part, axis, combine, identity, reverse):
    count = lax.axis_size(axis)
    place = lax.axis_index(axis)
    ahead = count - 1 - place if reverse else place
    gathered = lax.all_gather(part, axis)
    state = jnp.zeros_like(part) + jnp.asarray(identity, part.dtype)

    def one(lap, state):
        source = count - 1 - lap if reverse else lap
        return combine(state, lax.dynamic_index_in_dim(gathered, source, 0, False))

    return lax.fori_loop(0, ahead, one, state)


def add_states(first_part, second_part):
    return first_part + second_part


def split_state(state):
    state_high = state.astype(jnp.bfloat16)
    state_low = (state - state_high.astype(jnp.float32)).astype(jnp.bfloat16)
    return (state_high, state_low)


def per_device(queries, keys, values, out_grad, gain):
    feature_width = queries.shape[2]
    head_size = HEAD
    head_count = feature_width // head_size
    block_size = GROUP

    def to_blocks(array):
        return array.reshape(-1, block_size, head_count, head_size)

    query_rows = to_blocks(queries)
    key_rows = to_blocks(keys)
    value_rows = to_blocks(values)
    grad_rows = to_blocks(out_grad)
    row_index = lax.broadcasted_iota(jnp.int32, (block_size, block_size), 0)
    col_index = lax.broadcasted_iota(jnp.int32, (block_size, block_size), 1)
    causal = (row_index >= col_index).astype(jnp.float32)
    gain_rows = gain.reshape(head_count, head_size)
    key_value = jnp.einsum(
        "nshe,nshf->nhef", key_rows, value_rows, preferred_element_type=jnp.float32
    )
    device_sum = jnp.sum(key_value, axis=0)
    empty_state = jnp.zeros_like(device_sum)
    incoming = prefix(device_sum, "seq", add_states, empty_state, False)
    states = incoming[None] + (jnp.cumsum(key_value, axis=0) - key_value)
    states_high, states_low = split_state(states)
    scores = (
        jnp.einsum("nthe,nshe->nhts", query_rows, key_rows, preferred_element_type=jnp.float32)
        * causal
    )
    weights = scores.astype(jnp.bfloat16)
    attended = jnp.einsum(
        "nhts,nshe->nthe", weights, value_rows, preferred_element_type=jnp.float32
    )
    attended = attended + jnp.einsum(
        "nthe,nhef->nthf", query_rows, states_high, preferred_element_type=jnp.float32
    )
    attended = attended + jnp.einsum(
        "nthe,nhef->nthf", query_rows, states_low, preferred_element_type=jnp.float32
    )
    mean_square = jnp.mean(attended * attended, axis=-1, keepdims=True)
    inv_rms = lax.rsqrt(mean_square + 1e-05)
    normed = attended * inv_rms
    normed_out = (normed * gain_rows).astype(jnp.bfloat16)
    grad_wide = grad_rows.astype(jnp.float32)
    grad_normed = grad_wide * gain_rows
    grad_out = inv_rms * (
        grad_normed - normed * jnp.mean(grad_normed * normed, axis=-1, keepdims=True)
    )
    grad_half = grad_out.astype(jnp.bfloat16)
    gain_part = jnp.sum(normed * grad_wide, axis=(0, 1)).reshape(feature_width)
    total_tokens = queries.shape[0] * queries.shape[1] * lax.axis_size("seq") * lax.axis_size("dp")
    gain_grad = lax.psum(gain_part, ("seq", "dp")) / math.sqrt(total_tokens)
    mixed = (
        jnp.einsum("nthe,nshe->nhts", grad_half, value_rows, preferred_element_type=jnp.float32)
        * causal
    )
    mixed_half = mixed.astype(jnp.bfloat16)
    grad_query = jnp.einsum(
        "nhts,nshe->nthe", mixed_half, key_rows, preferred_element_type=jnp.float32
    )
    grad_query = grad_query + jnp.einsum(
        "nthf,nhef->nthe", grad_half, states_high, preferred_element_type=jnp.float32
    )
    grad_query = grad_query + jnp.einsum(
        "nthf,nhef->nthe", grad_half, states_low, preferred_element_type=jnp.float32
    )
    outer = jnp.einsum("nthe,nthf->nhef", query_rows, grad_half, preferred_element_type=jnp.float32)
    outer_sum = jnp.sum(outer, axis=0)
    arriving = prefix(outer_sum, "seq", add_states, empty_state, True)
    later_sum = arriving[None] + (outer_sum[None] - jnp.cumsum(outer, axis=0))
    later_high, later_low = split_state(later_sum)
    grad_key = jnp.einsum(
        "nhts,nthe->nshe", mixed_half, query_rows, preferred_element_type=jnp.float32
    )
    grad_key = grad_key + jnp.einsum(
        "nshf,nhef->nshe", value_rows, later_high, preferred_element_type=jnp.float32
    )
    grad_key = grad_key + jnp.einsum(
        "nshf,nhef->nshe", value_rows, later_low, preferred_element_type=jnp.float32
    )
    grad_value = jnp.einsum(
        "nhts,nthf->nshf", weights, grad_half, preferred_element_type=jnp.float32
    )
    grad_value = grad_value + jnp.einsum(
        "nshe,nhef->nshf", key_rows, later_high, preferred_element_type=jnp.float32
    )
    grad_value = grad_value + jnp.einsum(
        "nshe,nhef->nshf", key_rows, later_low, preferred_element_type=jnp.float32
    )
    shape_out = queries.shape
    return (
        normed_out.reshape(shape_out),
        grad_query.astype(jnp.bfloat16).reshape(shape_out),
        grad_key.astype(jnp.bfloat16).reshape(shape_out),
        grad_value.astype(jnp.bfloat16).reshape(shape_out),
        gain_grad,
    )


def dot(a, b, a_dim=1, b_dim=0):
    return lax.dot_general(a, b, (((a_dim,), (b_dim,)), ((), ())), preferred_element_type=F32)


def flip(index, bit):
    return index + bit * (1 - 2 * lax.rem(lax.div(index, bit), 2))


def kernel(
    pairs, hops, scale,
    q_hbm, k_hbm, v_hbm, g_hbm, gain_hbm,
    out_hbm, dq_hbm, dk_hbm, dv_hbm, gg_hbm,
    f_own, f_src, f_in, fz_in, fz_out, f_give, f_take,
    b_own, b_src, b_in, bz_in, bz_out, b_give, b_take,
    w_all, hi_all, lo_all, go_all, inner_all, dk_all, dv_all, gain_sum, gain_in,
    q_ref, k_ref, v_ref, g_ref, gain_ref,
    out_ref, dq_ref, dk_ref, dv_ref, gg_ref,
    send, recv, chain_send, chain_recv, gain_send, gain_recv, load_sem, store_sem,
):
    half = f_own.shape[0]
    stages = len(hops)
    place = lax.axis_index("seq")
    side = lax.rem(place, 2)
    pair = lax.div(place, 2)
    has_before = pair > 0
    has_after = pair < pairs - 1
    partner = {"seq": flip(place, 1)}
    before = {"seq": place - 2}
    after = {"seq": place + 2}
    def needed(sender, at_end):
        return jnp.logical_not((side == sender) & jnp.logical_not(at_end))

    fx_send, fx_wait = needed(1, has_after), needed(0, has_after)
    fg_send, fg_wait = needed(1, has_before), needed(0, has_before)
    bx_send, bx_wait = needed(0, has_before), needed(1, has_before)
    bg_send, bg_wait = needed(0, has_after), needed(1, has_after)
    own_first = side * half
    other_first = (1 - side) * half

    loads = [
        pltpu.make_async_copy(src, dst, load_sem.at[i])
        for i, (src, dst) in enumerate((
            (k_hbm, k_ref), (v_hbm, v_ref), (q_hbm, q_ref), (g_hbm, g_ref), (gain_hbm, gain_ref),
        ))
    ]
    for load in loads:
        load.start()

    stores = [
        pltpu.make_async_copy(src, dst, store_sem.at[i])
        for i, (src, dst) in enumerate((
            (out_ref, out_hbm), (dq_ref, dq_hbm), (dk_ref, dk_hbm), (dv_ref, dv_hbm),
            (gg_ref, gg_hbm),
        ))
    ]

    def greet(device):
        pl.semaphore_signal(barrier, inc=1, device_id=device, device_id_type=MESH)

    def hop_device(axis, bit):
        return {axis: flip(lax.axis_index(axis), bit)}

    barrier = pltpu.get_barrier_semaphore()
    peers = [hop for hop in hops if hop != ("seq", 2)]
    for axis, bit in peers:
        greet(hop_device(axis, bit))

    @pl.when(has_before)
    def _():
        greet(before)

    @pl.when(has_after)
    def _():
        greet(after)

    def move(kind, src, dst, c, device):
        return pltpu.make_async_remote_copy(
            src_ref=src.at[c], dst_ref=dst.at[c],
            send_sem=send.at[kind, c], recv_sem=recv.at[kind, c],
            device_id=device, device_id_type=MESH,
        )

    def fx(c):
        return move(0, f_src, f_in, c, partner)

    def chain_rows(p):
        return pl.ds(p * (HEAD // PARTS), HEAD // PARTS)

    def chain_move(kind, src, dst, c, p, device):
        return pltpu.make_async_remote_copy(
            src_ref=src.at[c, chain_rows(p)], dst_ref=dst.at[c, chain_rows(p)],
            send_sem=chain_send.at[kind, c, p], recv_sem=chain_recv.at[kind, c, p],
            device_id=device, device_id_type=MESH,
        )

    def fz(c, p, device):
        return chain_move(0, fz_out, fz_in, c, p, device)

    def fg(c):
        return move(1, f_give, f_take, c, partner)

    def bx(c):
        return move(2, b_src, b_in, c, partner)

    def bz(c, p, device):
        return chain_move(1, bz_out, bz_in, c, p, device)

    def bg(c):
        return move(3, b_give, b_take, c, partner)

    def gain_move(s):
        axis, bit = hops[s]
        return pltpu.make_async_remote_copy(
            src_ref=gain_sum.at[s], dst_ref=gain_in.at[s],
            send_sem=gain_send.at[s], recv_sem=gain_recv.at[s],
            device_id=hop_device(axis, bit), device_id_type=MESH,
        )

    def cols(h):
        return pl.ds(pl.multiple_of(h * HEAD, HEAD), HEAD)

    row = lax.broadcasted_iota(jnp.int32, (GROUP, GROUP), 0)
    col = lax.broadcasted_iota(jnp.int32, (GROUP, GROUP), 1)
    causal = row >= col

    def key_value(h):
        return dot(k_ref[:, cols(h)], v_ref[:, cols(h)], 0, 0)

    def local_forward(h):
        w = jnp.where(causal, dot(q_ref[:, cols(h)], k_ref[:, cols(h)], 1, 1), 0.0).astype(BF16)
        return w, dot(w, v_ref[:, cols(h)])

    def forward(h, state):
        q = q_ref[:, cols(h)]
        hi, lo = split_state(state)
        attended = inner_all[h] + dot(
            jnp.concatenate([q, q], axis=1), jnp.concatenate([hi, lo], axis=0)
        )
        inv = lax.rsqrt(jnp.mean(attended * attended, axis=1, keepdims=True) + 1e-05)
        normed = attended * inv
        gain = gain_ref[pl.ds(h, 1), :]
        wide = g_ref[:, cols(h)].astype(F32)
        grad_normed = wide * gain
        go = inv * (
            grad_normed - normed * jnp.mean(grad_normed * normed, axis=1, keepdims=True)
        )
        go = go.astype(BF16)
        normed_out = (normed * gain).astype(BF16)
        gain_part = jnp.sum(normed * wide, axis=0, keepdims=True)
        return dot(q, go, 0, 0), hi, lo, go, normed_out, gain_part

    def keep_forward(h, results):
        outer, hi, lo, go, normed_out, gain_part = results
        hi_all[h] = hi
        lo_all[h] = lo
        go_all[h] = go
        out_ref[:, cols(h)] = normed_out
        gain_sum[0, pl.ds(h, 1), :] = gain_part

    def local_backward(h):
        go = go_all[h]
        mixed = jnp.where(causal, dot(go, v_ref[:, cols(h)], 1, 1), 0.0).astype(BF16)
        dq = dot(mixed, k_ref[:, cols(h)]) + dot(
            jnp.concatenate([go, go], axis=1),
            jnp.concatenate([hi_all[h], lo_all[h]], axis=1), 1, 1,
        )
        return dq.astype(BF16), dot(mixed, q_ref[:, cols(h)], 0, 0), dot(w_all[h], go, 0, 0)

    def keep_local_backward(h, results):
        dq_ref[:, cols(h)], dk_all[h], dv_all[h] = results

    def backward(h, later):
        hi, lo = split_state(later)
        v = v_ref[:, cols(h)]
        k = k_ref[:, cols(h)]
        dk = dk_all[h] + dot(
            jnp.concatenate([v, v], axis=1), jnp.concatenate([hi, lo], axis=1), 1, 1
        )
        dv = dv_all[h] + dot(
            jnp.concatenate([k, k], axis=1), jnp.concatenate([hi, lo], axis=0)
        )
        return dk.astype(BF16), dv.astype(BF16)

    def keep_backward(h, results):
        dk_ref[:, cols(h)], dv_ref[:, cols(h)] = results

    def clear(ref, condition):
        @pl.when(condition)
        def _():
            ref[...] = jnp.zeros_like(ref)

    clear(fz_in, jnp.logical_not(has_before))
    clear(bz_in, jnp.logical_not(has_after))
    clear(f_take, jnp.logical_not(fg_wait))
    clear(b_take, jnp.logical_not(bg_wait))

    loads[0].wait()
    loads[1].wait()
    f_src[0] = key_value(other_first)
    ends = has_before.astype(jnp.int32) + has_after.astype(jnp.int32)
    pl.semaphore_wait(barrier, len(peers) + ends)

    def start_if(condition, copy):
        @pl.when(condition)
        def _():
            copy.start()

    def recv_if(condition, copy):
        @pl.when(condition)
        def _():
            copy.wait_recv()

    def sent_if(condition, copy):
        @pl.when(condition)
        def _():
            copy.wait_send()

    ahead = jnp.minimum(half, AHEAD_FIRST + AHEAD_HOP * pair)
    start_if(fx_send, fx(0))
    for c in range(1, half):
        f_src[c] = key_value(other_first + c)
        start_if(fx_send & (c < ahead), fx(c))
    for c in range(half):
        f_own[c] = key_value(own_first + c)
    for load in loads[2:]:
        load.wait()

    lag = LAG_FIRST + LAG_HOP * (pairs - 1 - pair)
    late = 2 * pair >= pairs
    forward_end = half + FORWARD_LAG
    local_lag = jnp.where(late, forward_end, FORWARD_LAG + 1)
    give_lag = jnp.maximum(lag, forward_end)
    final_lag = give_lag + FINAL_LAG
    most = max(LAG_FIRST + LAG_HOP * (pairs - 1), forward_end) + FINAL_LAG
    steps = max(half + most, forward_end + stages)

    def local_step(c):
        mine = local_forward(own_first + c)
        theirs = local_forward(other_first + c)
        w_all[own_first + c], inner_all[own_first + c] = mine
        w_all[other_first + c], inner_all[other_first + c] = theirs

    @pl.when(late)
    def _():
        lax.fori_loop(0, half, lambda c, carry: (local_step(c), carry)[1], 0)

    def step(t, carry):
        @pl.when(t < half)
        def _():
            recv_if(fx_wait, fx(t))
            for p in range(PARTS):
                rows = chain_rows(p)
                recv_if(has_before, fz(t, p, partner))
                fz_out[t, rows] = fz_in[t, rows] + (f_own[t, rows] + f_in[t, rows])
                start_if(has_after, fz(t, p, after))
            past, mine, theirs = fz_in[t], f_own[t], f_in[t]
            f_give[t] = past + jnp.where(side == 0, mine, 0.0)
            start_if(fg_send, fg(t))
            start_if(fx_send & (t < half - ahead), fx(jnp.minimum(t + ahead, half - 1)))
            f_own[t] = past + jnp.where(side == 1, theirs, 0.0)

        @pl.when((t >= FORWARD_LAG) & (t < half + FORWARD_LAG))
        def _():
            c = t - FORWARD_LAG
            recv_if(fg_wait, fg(c))
            theirs = forward(other_first + c, f_take[c])
            mine = forward(own_first + c, f_own[c])
            b_src[c] = theirs[0]
            start_if(bx_send, bx(c))
            b_own[c] = mine[0]
            keep_forward(other_first + c, theirs)
            keep_forward(own_first + c, mine)

        j = t - lag

        @pl.when((j >= 0) & (j < half))
        def _():
            recv_if(bx_wait, bx(j))
            for p in range(PARTS):
                rows = chain_rows(p)
                recv_if(has_after, bz(j, p, partner))
                bz_out[j, rows] = bz_in[j, rows] + (b_own[j, rows] + b_in[j, rows])
                start_if(has_before, bz(j, p, before))
            past, mine, theirs = bz_in[j], b_own[j], b_in[j]
            b_give[j] = past + jnp.where(side == 1, mine, 0.0)
            b_own[j] = past + jnp.where(side == 0, theirs, 0.0)

        u = t - give_lag

        @pl.when((u >= 0) & (u < half))
        def _():
            start_if(bg_send, bg(u))

        @pl.when((t < half) & jnp.logical_not(late))
        def _():
            local_step(t)

        b = t - local_lag

        @pl.when((b >= 0) & (b < half))
        def _():
            mine = local_backward(own_first + b)
            theirs = local_backward(other_first + b)
            keep_local_backward(own_first + b, mine)
            keep_local_backward(other_first + b, theirs)

            @pl.when(b == half - 1)
            def _():
                stores[1].start()

        e = t - final_lag

        @pl.when((e >= 0) & (e < half))
        def _():
            recv_if(bg_wait, bg(e))
            mine = backward(own_first + e, b_own[e])
            theirs = backward(other_first + e, b_take[e])
            keep_backward(own_first + e, mine)
            keep_backward(other_first + e, theirs)

        for s in range(stages + 1):

            @pl.when(t == forward_end - 1 + s)
            def _(s=s):
                if s > 0:
                    gain_move(s - 1).wait_recv()
                    gain_sum[s] = gain_sum[s - 1] + gain_in[s - 1]
                if s < stages:
                    gain_move(s).start()
                else:
                    gg_ref[...] = gain_sum[s] / scale
                    stores[4].start()
                if s == 0:
                    stores[0].start()

        return carry

    lax.fori_loop(0, steps, step, 0)
    for store in stores[2:4]:
        store.start()

    def finish(c, carry):
        sent_if(fx_send, fx(c))
        sent_if(fg_send, fg(c))
        sent_if(bx_send, bx(c))
        sent_if(bg_send, bg(c))
        for p in range(PARTS):
            sent_if(has_after, fz(c, p, after))
            sent_if(has_before, bz(c, p, before))
        return carry

    lax.fori_loop(0, half, finish, 0)
    for s in range(stages):
        gain_move(s).wait_send()
    for store in stores:
        store.wait()


def flush(*refs):
    source, target, held = refs[:5], refs[5:10], refs[10:15]
    sems = refs[15]
    reads = [pltpu.make_async_copy(source[i], held[i], sems.at[0, i]) for i in range(5)]
    writes = [pltpu.make_async_copy(held[i], target[i], sems.at[1, i]) for i in range(5)]
    for read in reads:
        read.start()
    for read, write in zip(reads, writes):
        read.wait()
        write.start()
    for write in writes:
        write.wait()


def fused(queries, keys, values, out_grad, gain):
    shape = queries.shape
    rows, width = shape[1], shape[2]
    heads = width // HEAD
    half = heads // 2
    count = lax.axis_size("seq")
    spread = lax.axis_size("dp")
    hops = []
    for axis, size in (("seq", count), ("dp", spread)):
        bit = 1
        while bit < size:
            hops.append((axis, bit))
            bit *= 2
    stages = len(hops)
    scale = math.sqrt(shape[0] * rows * count * spread)
    flat = [a.reshape(rows, width) for a in (queries, keys, values, out_grad)]
    state = pltpu.VMEM((half, HEAD, HEAD), F32)
    held = pltpu.VMEM((heads, HEAD, HEAD), BF16)
    wide = pltpu.VMEM((heads, HEAD, HEAD), F32)
    block = pltpu.VMEM((rows, width), BF16)
    anywhere = pl.BlockSpec(memory_space=pl.ANY)
    result = pl.pallas_call(
        functools.partial(kernel, count // 2, tuple(hops), scale),
        out_shape=[jax.ShapeDtypeStruct((rows, width), BF16)] * 4
        + [jax.ShapeDtypeStruct((heads, HEAD), F32)],
        in_specs=[anywhere] * 5,
        out_specs=[anywhere] * 5,
        scratch_shapes=[state] * 14
        + [held] * 4
        + [wide] * 3
        + [
            pltpu.VMEM((stages + 1, heads, HEAD), F32),
            pltpu.VMEM((stages, heads, HEAD), F32),
            block, block, block, block,
            pltpu.VMEM((heads, HEAD), F32),
            block, block, block, block,
            pltpu.VMEM((heads, HEAD), F32),
            pltpu.SemaphoreType.DMA((4, half)),
            pltpu.SemaphoreType.DMA((4, half)),
            pltpu.SemaphoreType.DMA((2, half, PARTS)),
            pltpu.SemaphoreType.DMA((2, half, PARTS)),
            pltpu.SemaphoreType.DMA((stages,)),
            pltpu.SemaphoreType.DMA((stages,)),
            pltpu.SemaphoreType.DMA((5,)),
            pltpu.SemaphoreType.DMA((5,)),
        ],
        compiler_params=pltpu.CompilerParams(
            collective_id=0, has_side_effects=True, vmem_limit_bytes=VMEM_LIMIT
        ),
    )(*flat, gain.reshape(heads, HEAD))
    result = pl.pallas_call(
        flush,
        out_shape=[jax.ShapeDtypeStruct(a.shape, a.dtype) for a in result],
        in_specs=[anywhere] * 5,
        out_specs=[anywhere] * 5,
        scratch_shapes=[pltpu.VMEM(a.shape, a.dtype) for a in result]
        + [pltpu.SemaphoreType.DMA((2, 5))],
        compiler_params=pltpu.CompilerParams(vmem_limit_bytes=VMEM_LIMIT),
    )(*result)
    return tuple(a.reshape(shape) for a in result[:4]) + (result[4].reshape(width),)


def fits(queries):
    def power_of_two(size):
        return size & (size - 1) == 0

    heads = queries.shape[2] // HEAD
    return (
        queries.shape[:2] == (1, GROUP)
        and heads % 2 == 0
        and lax.axis_size("seq") >= 2
        and power_of_two(lax.axis_size("seq"))
        and power_of_two(lax.axis_size("dp"))
    )


def on_device(queries, keys, values, out_grad, gain):
    run = fused if fits(queries) else per_device
    return run(queries, keys, values, out_grad, gain)


def solution(mesh):
    in_specs = (
        P("dp", "seq", None),
        P("dp", "seq", None),
        P("dp", "seq", None),
        P("dp", "seq", None),
        P(),
    )
    out_specs = (
        P("dp", "seq", None),
        P("dp", "seq", None),
        P("dp", "seq", None),
        P("dp", "seq", None),
        P(),
    )
    return jax.shard_map(
        on_device, mesh=mesh, in_specs=in_specs, out_specs=out_specs, check_vma=False
    )
```
